32 devices in a mesh: dp: 8 (over y, x, core), mp: 4 (over z).
Axes of the slice: x: 2, y: 2, z: 4, core: 2. Of those that a mesh axis runs over, the one named last changes fastest.
Arguments:
- tokens: bfloat16 [12608, 1024], P(('dp', 'mp')), may hold values from -6 to 6
- slide_tiles: int32 [16], P('dp'), may hold values from 1 to 4, as said below
- norm1_gain: float32 [1024], replicated, may hold values from 0.5 to 1.5
- norm1_bias: float32 [1024], replicated, may hold values from -1.75 to 1.75
- w_query: bfloat16 [1024, 1024], P(None, 'mp'), may hold values from -0.25 to 0.25
- b_query: float32 [1024], P('mp'), may hold values from -1.75 to 1.75
- w_key: bfloat16 [1024, 1024], P(None, 'mp'), may hold values from -0.1875 to 0.1875
- w_value: bfloat16 [1024, 1024], P(None, 'mp'), may hold values from -0.1875 to 0.1875
- b_value: float32 [1024], P('mp'), may hold values from -1.75 to 1.75
- w_out: bfloat16 [1024, 1024], P('mp'), may hold values from -1 to 1
- b_out: float32 [1024], replicated, may hold values from -1.75 to 1.75
- scale_attn: float32 [1024], replicated, may hold values from 0.3 to 1
- norm2_gain: float32 [1024], replicated, may hold values from 0.5 to 1.5
- norm2_bias: float32 [1024], replicated, may hold values from -1.75 to 1.75
- w_up: bfloat16 [1024, 4096], P(None, 'mp'), may hold values from -0.1875 to 0.1875
- b_up: float32 [4096], P('mp'), may hold values from -3 to 3
- w_down: bfloat16 [4096, 1024], P('mp'), may hold values from -0.09375 to 0.09375
- b_down: float32 [1024], replicated, may hold values from -1.75 to 1.75
- scale_mlp: float32 [1024], replicated, may hold values from 0.3 to 1
- cotangent: bfloat16 [12608, 1024], P(('dp', 'mp')), may hold values from -6 to 6
Outputs:
- layer_out: float32 [12608, 1024], P(('dp', 'mp'))
- grad_tokens: float32 [12608, 1024], P(('dp', 'mp'))
- grad_norm1_gain: float32 [1024], replicated
- grad_norm1_bias: float32 [1024], replicated
- grad_w_query: float32 [1024, 1024], P(None, 'mp')
- grad_b_query: float32 [1024], P('mp')
- grad_w_key: float32 [1024, 1024], P(None, 'mp')
- grad_w_value: float32 [1024, 1024], P(None, 'mp')
- grad_b_value: float32 [1024], P('mp')
- grad_w_out: float32 [1024, 1024], P('mp')
- grad_b_out: float32 [1024], replicated
- grad_scale_attn: float32 [1024], replicated
- grad_norm2_gain: float32 [1024], replicated
- grad_norm2_bias: float32 [1024], replicated
- grad_w_up: float32 [1024, 4096], P(None, 'mp')
- grad_b_up: float32 [4096], P('mp')
- grad_w_down: float32 [4096, 1024], P('mp')
- grad_b_down: float32 [1024], replicated
- grad_scale_mlp: float32 [1024], replicated
The draws below stay inside these ranges and needn't reach their ends.
Inputs may be any that keep to these rules, and one draw needn't show every extreme that they name: `slide_tiles`: every draw has a slide with 4 crops.
All inputs are finite; a program needn't handle non-finite values.
Results may differ from the reference program's by a relative error of at most 0.023.
Values may be sent and summed in bfloat16 or wider, within the bound.
No kernel may reach another device: no remote copies, remote signals or barrier semaphores. Data moves between devices by JAX's collectives and lax.ppermute only.
A program may use at most 128 MiB of HBM per device.

```python
import math
import jax
import jax.numpy as jnp
from jax import lax

D = 1024
HEADS = 16
DH = 64
FF = 4096
L = 197
SLIDES_DEV = 2
CROPS_DEV = 8
SLIDES = 16
TOKENS = 12608
N_DP = 8
N_MP = 4


def draw_slide_tiles(key, part):
    key = jax.random.fold_in(key, 11)
    per_slide = CROPS_DEV // SLIDES_DEV
    key_count, key_pick = jax.random.split(key)
    counts = jax.random.randint(key_count, (SLIDES,), 1, per_slide + 1, dtype=jnp.int32)
    chosen = jax.random.randint(key_pick, (), 0, SLIDES, dtype=jnp.int32)
    return jnp.where(jnp.arange(SLIDES, dtype=jnp.int32) == chosen, per_slide, counts).astype(jnp.int32)


def block_scale(key, shape, pieces, smallest, high):
    level = 1.0
    for dim, shards_of in pieces:
        steps = jax.random.uniform(jax.random.fold_in(jax.random.fold_in(key, 6), dim), (shards_of,), jnp.float32, smallest / len(pieces), high / len(pieces))
        level = level * jnp.repeat(jnp.exp(steps), shape[dim] // shards_of).reshape((-1,) + (1,) * (len(shape) - 1 - dim))
    return level


def bell_draw(rng, extent, scale, most, cuts=(), kind=jnp.bfloat16):
    array = jax.random.normal(rng, extent, jnp.float32) * scale
    if len(cuts) > 0:
        array = block_scale(rng, extent, cuts, -0.22, 0.18) * array
    return jnp.clip(array, min=-most, max=most).astype(kind)


def setup_inputs(seed: int = 0) -> dict:
    streams_of = jax.random.split(jax.random.key(seed), 21)
    tokens = bell_draw(streams_of[0], (TOKENS, D), 1.0, 6.0, ((0, 32),))
    slide_tiles = draw_slide_tiles(jax.random.fold_in(streams_of[20], 71), 0)
    norm1_gain = jnp.clip(1.0 + 0.1 * jax.random.normal(streams_of[2], (D,), jnp.float32), 0.5, 1.5)
    norm1_bias = bell_draw(streams_of[3], (D,), 0.3, 1.75, (), jnp.float32)
    w_query = bell_draw(streams_of[4], (D, D), (D // 2) ** -0.5, 0.25, ((1, 4),))
    b_query = bell_draw(streams_of[5], (D,), 0.3, 1.75, ((0, 4),), jnp.float32)
    w_key = bell_draw(streams_of[6], (D, D), D ** -0.5, 0.1875, ((1, 4),))
    w_value = bell_draw(streams_of[7], (D, D), D ** -0.5, 0.1875, ((1, 4),))
    b_value = bell_draw(streams_of[8], (D,), 0.3, 1.75, ((0, 4),), jnp.float32)
    w_out = bell_draw(streams_of[9], (D, D), (D // 32) ** -0.5, 1.0, ((0, 4),))
    b_out = bell_draw(streams_of[10], (D,), 0.3, 1.75, (), jnp.float32)
    scale_attn = jnp.clip(jnp.exp(jax.random.uniform(streams_of[11], (D,), jnp.float32, math.log(0.3), math.log(1.0))), 0.3, 1.0)
    norm2_gain = jnp.clip(1.0 + 0.1 * jax.random.normal(streams_of[12], (D,), jnp.float32), 0.5, 1.5)
    norm2_bias = bell_draw(streams_of[13], (D,), 0.3, 1.75, (), jnp.float32)
    w_up = bell_draw(streams_of[14], (D, FF), D ** -0.5, 0.1875, ((1, 4),))
    b_up = bell_draw(streams_of[15], (FF,), 0.5, 3.0, ((0, 4),), jnp.float32)
    w_down = bell_draw(streams_of[16], (FF, D), FF ** -0.5, 0.09375, ((0, 4),))
    b_down = bell_draw(streams_of[17], (D,), 0.3, 1.75, (), jnp.float32)
    scale_mlp = jnp.clip(jnp.exp(jax.random.uniform(streams_of[18], (D,), jnp.float32, math.log(0.3), math.log(1.0))), 0.3, 1.0)
    cotangent = bell_draw(streams_of[19], (TOKENS, D), 1.0, 6.0, ((0, 32),))
    return dict(tokens=tokens, slide_tiles=slide_tiles, norm1_gain=norm1_gain, norm1_bias=norm1_bias, w_query=w_query, b_query=b_query, w_key=w_key, w_value=w_value, b_value=b_value, w_out=w_out, b_out=b_out, scale_attn=scale_attn, norm2_gain=norm2_gain, norm2_bias=norm2_bias, w_up=w_up, b_up=b_up, w_down=w_down, b_down=b_down, scale_mlp=scale_mlp, cotangent=cotangent)


@jax.custom_vjp
def low(v):
    return lax.optimization_barrier(v.astype(jnp.bfloat16)).astype(jnp.float32)

@jax.custom_vjp
def low_back(v):
    return v

def low_keep(v):
    return (low(v), None)

def low_pass(kept, grad):
    return (grad,)

def back_keep(v):
    return (v, None)

def back_low(kept, grad):
    return (low(grad),)
low.defvjp(low_keep, low_pass)
low_back.defvjp(back_keep, back_low)

def layer_norm(values, gain, shift):
    average = lax.optimization_barrier(jnp.mean(values, axis=-1, keepdims=True))
    centered = values - average
    spread = lax.optimization_barrier(jnp.mean(centered * centered, axis=-1, keepdims=True))
    return centered * lax.rsqrt(spread + 1e-06) * gain + shift

def matmul(left, right):
    return jnp.dot(left, right, precision=lax.Precision.HIGHEST)

def attend_block(queries, keys_in, values_in):
    crops = queries.shape[0] // L
    query_heads = queries.reshape(crops, L, HEADS, DH)
    key_heads = keys_in.reshape(crops, L, HEADS, DH)
    value_heads = values_in.reshape(crops, L, HEADS, DH)
    scores = jnp.einsum('cqhd,ckhd->chqk', query_heads, key_heads, precision=lax.Precision.HIGHEST)
    scores = low_back(scores * (1.0 / math.sqrt(DH)))
    probs = low(jax.nn.softmax(scores, axis=-1))
    mixed_heads = jnp.einsum('chqk,ckhd->cqhd', probs, value_heads, precision=lax.Precision.HIGHEST)
    return mixed_heads.reshape(crops * L, HEADS * DH)

def grouped_sum(left, right, width):
    total = low(matmul(left[:, 0:width], right[0:width]))
    for group in range(1, N_MP):
        total = total + low(matmul(left[:, group * width:(group + 1) * width], right[group * width:(group + 1) * width]))
    return total

def forward(inputs, valid_rows, weights):
    norm1_gain, norm1_bias, w_query, b_query, w_key, w_value, b_value, w_out, b_out, scale_attn, norm2_gain, norm2_bias, w_up, b_up, w_down, b_down, scale_mlp = weights
    width_d = D // N_MP
    width_f = FF // N_MP
    normed_one = low(layer_norm(inputs, norm1_gain, norm1_bias))
    query_parts, key_parts, value_parts = ([], [], [])
    for group in range(N_MP):
        copy_one = low_back(normed_one)
        cols = slice(group * width_d, (group + 1) * width_d)
        query_parts.append(matmul(copy_one, w_query[:, cols]))
        key_parts.append(matmul(copy_one, w_key[:, cols]))
        value_parts.append(matmul(copy_one, w_value[:, cols]))
    queries = low(low_back(jnp.concatenate(query_parts, axis=1) + b_query))
    keys_all = low(low_back(jnp.concatenate(key_parts, axis=1)))
    values_all = low(low_back(jnp.concatenate(value_parts, axis=1) + b_value))
    attended = low(low_back(jax.checkpoint(attend_block)(queries, keys_all, values_all)))
    attn_sum = low_back(grouped_sum(attended, w_out, width_d))
    hidden_state = inputs + scale_attn * (attn_sum + b_out)
    normed_two = low(layer_norm(hidden_state, norm2_gain, norm2_bias))
    up_parts = []
    for group in range(N_MP):
        copy_two = low_back(normed_two)
        up_parts.append(matmul(copy_two, w_up[:, group * width_f:(group + 1) * width_f]))
    up_pre = low_back(jnp.concatenate(up_parts, axis=1) + b_up)
    activated = low(jax.nn.gelu(up_pre, approximate=False))
    down_sum = low_back(grouped_sum(activated, w_down, width_f))
    return valid_rows * (hidden_state + scale_mlp * (down_sum + b_down))

def reference(tokens, slide_tiles, norm1_gain, norm1_bias, w_query, b_query, w_key, w_value, b_value, w_out, b_out, scale_attn, norm2_gain, norm2_bias, w_up, b_up, w_down, b_down, scale_mlp, cotangent):
    params = tuple((weight.astype(jnp.float32) for weight in (norm1_gain, norm1_bias, w_query, b_query, w_key, w_value, b_value, w_out, b_out, scale_attn, norm2_gain, norm2_bias, w_up, b_up, w_down, b_down, scale_mlp)))
    group_rows = CROPS_DEV * L
    per_slide = CROPS_DEV // SLIDES_DEV
    crop_index = jnp.arange(CROPS_DEV, dtype=jnp.int32)
    inputs = tokens.astype(jnp.float32).reshape(N_DP, group_rows, D)
    seed_rows = cotangent.astype(jnp.float32).reshape(N_DP, group_rows, D)
    tile_table = slide_tiles.astype(jnp.int32).reshape(N_DP, SLIDES_DEV)

    def one_group(totals, group_item):
        group_in, group_seed, counts = group_item
        limits = counts[crop_index // per_slide]
        valid_crop = (crop_index % per_slide < limits).astype(jnp.float32)
        valid_rows = jnp.repeat(valid_crop, L)[:, None]

        def apply(values, weights):
            return forward(values, valid_rows, weights)
        result, pullback = jax.vjp(apply, group_in, params)
        grad_group, grad_params = pullback(group_seed)
        totals = tuple((total + grad for total, grad in zip(totals, grad_params)))
        return (totals, (result, grad_group))
    zeros = tuple((jnp.zeros_like(weight) for weight in params))
    grads, (results, grad_rows) = lax.scan(one_group, zeros, (inputs, seed_rows, tile_table))
    layer_out = results.reshape(TOKENS, D)
    grad_tokens = grad_rows.reshape(TOKENS, D)
    return (layer_out, grad_tokens, grads[0], grads[1], grads[2], grads[3], grads[4], grads[5], grads[6], grads[7], grads[8], grads[9], grads[10], grads[11], grads[12], grads[13], grads[14], grads[15], grads[16])
```

```python
import math

import jax
import jax.numpy as jnp
from jax import lax
from jax.experimental import pallas as pl
from jax.experimental.pallas import tpu as pltpu
from jax.sharding import PartitionSpec as P

DH = 64
L = 197
SLIDES_DEV = 2
CROPS_DEV = 8


def layer_norm(values, gain, shift):
    average = jnp.mean(values, axis=-1, keepdims=True)
    centered = values - average
    spread = jnp.mean(centered * centered, axis=-1, keepdims=True)
    return centered * lax.rsqrt(spread + 1e-06) * gain + shift


def gelu_exact(values):
    return jax.nn.gelu(values, approximate=False)


def contract_rows(left, right):
    return lax.dot_general(
        left, right, (((0,), (0,)), ((), ())), preferred_element_type=jnp.float32
    )


def contract_cols(left, right):
    return lax.dot_general(
        left, right, (((1,), (1,)), ((), ())), preferred_element_type=jnp.float32
    )


def to_heads(matrix, heads_here):
    return matrix.reshape(matrix.shape[0] // L, L, heads_here, DH)


def attn_scores(query_heads, key_heads):
    product = jnp.einsum(
        "cqhd,ckhd->chqk", query_heads, key_heads, preferred_element_type=jnp.float32
    )
    return product * (1.0 / math.sqrt(DH))


BLOCK = 128
X_SIDE, Y_SIDE, CORE_SIDE = 2, 4, 1
PLANE = 8
DEPTH = 4


def swap_plane(values, mask):
    return lax.ppermute(values, "dp", [(i, i ^ mask) for i in range(PLANE)])


def swap_depth(values, mask):
    return lax.ppermute(values, "mp", [(i, i ^ mask) for i in range(DEPTH)])


def place_offset(place):
    return (place & 3) * 2 + (place >> 2)


def offset_place(offset):
    return (offset & 1) * 4 + (offset >> 1)


def to_places(values, here):
    return jnp.concatenate(
        [
            lax.dynamic_slice_in_dim(values, (here ^ place_offset(j)) * BLOCK, BLOCK, axis=-1)
            for j in range(PLANE)
        ],
        axis=-1,
    )


def from_places(values, here):
    return jnp.concatenate(
        [
            lax.dynamic_slice_in_dim(values, offset_place(here ^ j) * BLOCK, BLOCK, axis=-1)
            for j in range(PLANE)
        ],
        axis=-1,
    )


def row_blocks(matrix):
    return matrix.reshape(BLOCK, matrix.shape[1] // BLOCK, BLOCK).transpose(1, 0, 2)


def plane_gather(far):
    half = far.shape[0] // 2
    from_x = swap_plane(far, X_SIDE)
    from_y = swap_plane(far, Y_SIDE)
    corner_low = swap_plane(from_y[:half], X_SIDE)
    corner_high = swap_plane(from_x[half:], Y_SIDE)
    corner = jnp.concatenate([corner_low, corner_high], axis=0)
    mine = jnp.stack([far, from_x, from_y, corner])
    return mine, swap_plane(mine, CORE_SIDE)


def crop_ranges(rows):
    ranges = []
    for crop in range(rows // L):
        low = crop * L // 16 * 16
        high = min((crop + 1) * L + 15, rows + 15) // 16 * 16
        ranges.append((low, min(high, rows), crop * L - low))
    return ranges


def assemble_attn(table, own, mine, other):
    width = own.shape[1]
    count = mine.shape[1]

    def body(table_ref, own_ref, mine_ref, other_ref, out_ref):
        out_ref[:, 0:width] = own_ref[...]

        @pl.when(pl.program_id(0) < 4)
        def _():
            for b in range(count):
                out_ref[:, width + b * BLOCK : width + (b + 1) * BLOCK] = mine_ref[0, b]

        @pl.when(pl.program_id(0) >= 4)
        def _():
            for b in range(count):
                out_ref[:, width + b * BLOCK : width + (b + 1) * BLOCK] = other_ref[0, b]

    total = width + count * BLOCK
    return pl.pallas_call(
        body,
        grid_spec=pltpu.PrefetchScalarGridSpec(
            num_scalar_prefetch=1,
            grid=(PLANE,),
            in_specs=[
                pl.BlockSpec((BLOCK, width), lambda j, t: (t[j], 0)),
                pl.BlockSpec((1, count, BLOCK, BLOCK), lambda j, t: (jnp.minimum(j, 3), 0, 0, 0)),
                pl.BlockSpec((1, count, BLOCK, BLOCK), lambda j, t: (jnp.maximum(j - 4, 0), 0, 0, 0)),
            ],
            out_specs=pl.BlockSpec((BLOCK, total), lambda j, t: (j, 0)),
        ),
        out_shape=jax.ShapeDtypeStruct((PLANE * BLOCK, total), jnp.bfloat16),
        cost_estimate=pl.CostEstimate(flops=0, bytes_accessed=4 * PLANE * BLOCK * total, transcendentals=0),
        name="assemble_attn",
    )(table, own, mine, other)


def assemble_rest(table, own_o, own_up, own_down, mine, other):
    heads_w = own_o.shape[0]
    unit_w = own_up.shape[1]
    n_o = heads_w // BLOCK
    n_u = unit_w // BLOCK
    count = mine.shape[1]

    def fill(src, o_ref, up_ref, down_ref):
        def put_o(slot, first):
            for b in range(n_o):
                o_ref[slot * heads_w + b * BLOCK : slot * heads_w + (b + 1) * BLOCK, :] = src[0, first + b]

        put_o(1, 0)
        put_o(2, n_o)
        for b in range(n_u):
            up_ref[:, unit_w + b * BLOCK : unit_w + (b + 1) * BLOCK] = src[0, 2 * n_o + b]
            down_ref[unit_w + b * BLOCK : unit_w + (b + 1) * BLOCK, :] = src[0, 2 * n_o + n_u + b]
        put_o(3, 2 * n_o + 2 * n_u)

    def body(table_ref, own_o_ref, own_up_ref, own_down_ref, mine_ref, other_ref, o_ref, up_ref, down_ref):
        o_ref[0:heads_w, :] = own_o_ref[...]
        up_ref[:, 0:unit_w] = own_up_ref[...]
        down_ref[0:unit_w, :] = own_down_ref[...]

        @pl.when(pl.program_id(0) < 4)
        def _():
            fill(mine_ref, o_ref, up_ref, down_ref)

        @pl.when(pl.program_id(0) >= 4)
        def _():
            fill(other_ref, o_ref, up_ref, down_ref)

    width = PLANE * BLOCK
    return pl.pallas_call(
        body,
        grid_spec=pltpu.PrefetchScalarGridSpec(
            num_scalar_prefetch=1,
            grid=(PLANE,),
            in_specs=[
                pl.BlockSpec((heads_w, BLOCK), lambda j, t: (0, t[j])),
                pl.BlockSpec((BLOCK, unit_w), lambda j, t: (t[j], 0)),
                pl.BlockSpec((unit_w, BLOCK), lambda j, t: (0, t[j])),
                pl.BlockSpec((1, count, BLOCK, BLOCK), lambda j, t: (jnp.minimum(j, 3), 0, 0, 0)),
                pl.BlockSpec((1, count, BLOCK, BLOCK), lambda j, t: (jnp.maximum(j - 4, 0), 0, 0, 0)),
            ],
            out_specs=[
                pl.BlockSpec((4 * heads_w, BLOCK), lambda j, t: (0, j)),
                pl.BlockSpec((BLOCK, 2 * unit_w), lambda j, t: (j, 0)),
                pl.BlockSpec((2 * unit_w, BLOCK), lambda j, t: (0, j)),
            ],
        ),
        out_shape=[
            jax.ShapeDtypeStruct((4 * heads_w, width), jnp.bfloat16),
            jax.ShapeDtypeStruct((width, 2 * unit_w), jnp.bfloat16),
            jax.ShapeDtypeStruct((2 * unit_w, width), jnp.bfloat16),
        ],
        cost_estimate=pl.CostEstimate(flops=0, bytes_accessed=20 * 2**20, transcendentals=0),
        name="assemble_rest",
    )(table, own_o, own_up, own_down, mine, other)


def dot_nt(left, right):
    return lax.dot_general(left, right, (((1,), (1,)), ((), ())), preferred_element_type=jnp.float32)


def dot_tn(left, right):
    return lax.dot_general(left, right, (((0,), (0,)), ((), ())), preferred_element_type=jnp.float32)


def dot_nn(left, right):
    return lax.dot_general(left, right, (((1,), (0,)), ((), ())), preferred_element_type=jnp.float32)


def attention_forward(qkv, group):
    rows = qkv.shape[0]
    heads_w = group // 3
    ranges = crop_ranges(rows)
    span = max(high - low for low, high, _ in ranges)
    pairs = heads_w // BLOCK
    groups = qkv.shape[1] // group
    scale = 1.0 / math.sqrt(DH)

    def body(qkv_ref, out_ref, prob_ref):
        for pair in range(pairs):
            col = pair * BLOCK
            for index, (low, high, skip) in enumerate(ranges):
                size = high - low
                query = qkv_ref[low:high, col : col + BLOCK]
                key = qkv_ref[low:high, heads_w + col : heads_w + col + BLOCK]
                value = qkv_ref[low:high, 2 * heads_w + col : 2 * heads_w + col + BLOCK]
                lane = lax.broadcasted_iota(jnp.int32, (size, BLOCK), 1)
                row = lax.broadcasted_iota(jnp.int32, (size, size), 0)
                column = lax.broadcasted_iota(jnp.int32, (size, size), 1)
                seen = (column >= skip) & (column < skip + L)
                inside = seen & (row >= skip) & (row < skip + L)
                parts = []
                for head in range(2):
                    mine = (lane < DH) if head == 0 else (lane >= DH)
                    scores = dot_nt(jnp.where(mine, query, jnp.zeros_like(query)), key) * scale
                    scores = jnp.where(seen, scores, -1e30)
                    top = jnp.max(scores, axis=1, keepdims=True)
                    raised = jnp.exp(scores - top)
                    total = jnp.sum(raised, axis=1, keepdims=True)
                    probs = jnp.where(inside, raised * (1.0 / total), 0.0).astype(jnp.bfloat16)
                    prob_ref[0, pair, index, head, 0:size, 0:size] = probs
                    parts.append(dot_nn(probs, value))
                mixed = jnp.where(lane < DH, parts[0], parts[1]).astype(jnp.bfloat16)
                if skip:
                    mixed = jnp.where(
                        lax.broadcasted_iota(jnp.int32, (size, BLOCK), 0) >= skip,
                        mixed,
                        out_ref[low:high, col : col + BLOCK],
                    )
                out_ref[low:high, col : col + BLOCK] = mixed

    prob_shape = (groups, pairs, len(ranges), 2, span, span)
    return pl.pallas_call(
        body,
        grid=(groups,),
        in_specs=[pl.BlockSpec((rows, group), lambda g: (0, g))],
        out_specs=[
            pl.BlockSpec((rows, heads_w), lambda g: (0, g)),
            pl.BlockSpec((1,) + prob_shape[1:], lambda g: (g, 0, 0, 0, 0, 0)),
        ],
        out_shape=[
            jax.ShapeDtypeStruct((rows, groups * heads_w), jnp.bfloat16),
            jax.ShapeDtypeStruct(prob_shape, jnp.bfloat16),
        ],
        compiler_params=pltpu.CompilerParams(vmem_limit_bytes=48 * 2**20),
        cost_estimate=pl.CostEstimate(flops=10**9, bytes_accessed=8 * 2**20, transcendentals=2 * 10**6),
        name="attention_forward",
    )(qkv)


def attention_backward(qkv, probs, grad_mixed, group):
    rows = qkv.shape[0]
    heads_w = group // 3
    ranges = crop_ranges(rows)
    pairs = heads_w // BLOCK
    groups = qkv.shape[1] // group
    scale = 1.0 / math.sqrt(DH)

    def body(qkv_ref, prob_ref, grad_ref, out_ref):
        for pair in range(pairs):
            col = pair * BLOCK
            for index, (low, high, skip) in enumerate(ranges):
                size = high - low
                query = qkv_ref[low:high, col : col + BLOCK]
                key = qkv_ref[low:high, heads_w + col : heads_w + col + BLOCK]
                value = qkv_ref[low:high, 2 * heads_w + col : 2 * heads_w + col + BLOCK]
                grad = grad_ref[low:high, col : col + BLOCK]
                lane = lax.broadcasted_iota(jnp.int32, (size, BLOCK), 1)
                row = lax.broadcasted_iota(jnp.int32, (size, BLOCK), 0)
                parts = []
                for head in range(2):
                    mine = (lane < DH) if head == 0 else (lane >= DH)
                    low_probs = prob_ref[0, pair, index, head, 0:size, 0:size]
                    grad_value = dot_tn(low_probs, grad)
                    grad_probs = dot_nt(jnp.where(mine, grad, jnp.zeros_like(grad)), value)
                    wide = low_probs.astype(jnp.float32)
                    weighted = wide * grad_probs
                    inner = jnp.sum(weighted, axis=1, keepdims=True)
                    grad_scores = (weighted - wide * inner).astype(jnp.bfloat16)
                    grad_query = dot_nn(grad_scores, key) * scale
                    grad_key = dot_tn(grad_scores, query) * scale
                    parts.append((grad_query, grad_key, grad_value))
                for which in range(3):
                    first = which * heads_w + col
                    joined = jnp.where(lane < DH, parts[0][which], parts[1][which]).astype(jnp.bfloat16)
                    if skip:
                        joined = jnp.where(row >= skip, joined, out_ref[low:high, first : first + BLOCK])
                    out_ref[low:high, first : first + BLOCK] = joined

    return pl.pallas_call(
        body,
        grid=(groups,),
        in_specs=[
            pl.BlockSpec((rows, group), lambda g: (0, g)),
            pl.BlockSpec((1,) + probs.shape[1:], lambda g: (g, 0, 0, 0, 0, 0)),
            pl.BlockSpec((rows, heads_w), lambda g: (0, g)),
        ],
        out_specs=pl.BlockSpec((rows, group), lambda g: (0, g)),
        out_shape=jax.ShapeDtypeStruct(qkv.shape, jnp.bfloat16),
        compiler_params=pltpu.CompilerParams(vmem_limit_bytes=48 * 2**20),
        cost_estimate=pl.CostEstimate(flops=2 * 10**9, bytes_accessed=12 * 2**20, transcendentals=0),
        name="attention_backward",
    )(qkv, probs, grad_mixed)


def reduce_plane(near, across, axis):
    arrived = swap_plane(across, CORE_SIDE)
    long = 1 - axis
    half = near.shape[long] // 2

    def part(side, chip):
        def cut(values):
            values = lax.slice_in_dim(values, side * half, (side + 1) * half, axis=long)
            return lax.slice_in_dim(values, chip * BLOCK, (chip + 1) * BLOCK, axis=axis)

        return cut(near).astype(jnp.float32) + cut(arrived).astype(jnp.float32)

    def piece(values, index):
        return lax.slice_in_dim(values, index * BLOCK, (index + 1) * BLOCK, axis=axis).astype(jnp.float32)

    halves = []
    for side, (first, second, one, two) in enumerate(((X_SIDE, Y_SIDE, 1, 2), (Y_SIDE, X_SIDE, 2, 1))):
        sent = jnp.concatenate([part(side, one), part(side, 3)], axis=axis).astype(jnp.bfloat16)
        halves.append((swap_plane(sent, first), second, two))
    done = []
    for side, (received, second, two) in enumerate(halves):
        onward = (part(side, two) + piece(received, 1)).astype(jnp.bfloat16)
        done.append((part(side, 0) + piece(received, 0), swap_plane(onward, second)))
    return [kept + last.astype(jnp.float32) for kept, last in done]


def local_paired(
    tokens,
    slide_tiles,
    norm1_gain,
    norm1_bias,
    w_query,
    b_query,
    w_key,
    w_value,
    b_value,
    w_out,
    b_out,
    scale_attn,
    norm2_gain,
    norm2_bias,
    w_up,
    b_up,
    w_down,
    b_down,
    scale_mlp,
    cotangent,
):
    row_count = tokens.shape[0]
    heads_w = w_query.shape[1]
    unit_w = w_up.shape[1]
    here = lax.axis_index("dp")
    level = lax.axis_index("mp")
    table = jnp.stack([here ^ place_offset(j) for j in range(PLANE)]).astype(jnp.int32)

    own_attn = jnp.concatenate([w_query, w_key, w_value], axis=1)
    slice_attn = row_blocks(lax.dynamic_slice_in_dim(own_attn, here * BLOCK, BLOCK, axis=0))
    slice_out = lax.dynamic_slice_in_dim(w_out, here * BLOCK, BLOCK, axis=1).reshape(-1, BLOCK, BLOCK)
    slice_up = row_blocks(lax.dynamic_slice_in_dim(w_up, here * BLOCK, BLOCK, axis=0))
    slice_down = lax.dynamic_slice_in_dim(w_down, here * BLOCK, BLOCK, axis=1).reshape(-1, BLOCK, BLOCK)
    far_attn = jnp.concatenate([swap_depth(slice_attn, mask) for mask in (1, 2, 3)], axis=0)
    far_rest = jnp.concatenate(
        [
            swap_depth(slice_out, 1),
            swap_depth(jnp.concatenate([slice_out, slice_up, slice_down], axis=0), 2),
            swap_depth(slice_out, 3),
        ],
        axis=0,
    )
    biases = lax.all_gather(jnp.concatenate([b_query, b_value, b_up]), "mp", axis=0)
    near_first = [lax.dynamic_index_in_dim(biases, level ^ mask, 0, keepdims=False) for mask in range(DEPTH)]
    bias_attn = jnp.concatenate(
        [
            jnp.concatenate([row[0:heads_w], jnp.zeros((heads_w,), jnp.float32), row[heads_w : 2 * heads_w]])
            for row in near_first
        ]
    )
    bias_up = jnp.concatenate([near_first[0][2 * heads_w :], near_first[2][2 * heads_w :]])
    full_qkv = assemble_attn(table, own_attn, *plane_gather(far_attn))
    full_out, full_up, full_down = assemble_rest(table, w_out, w_up, w_down, *plane_gather(far_rest))

    per_slide = CROPS_DEV // SLIDES_DEV
    crop_index = (level * row_count + jnp.arange(row_count, dtype=jnp.int32)) // L
    slide_index = crop_index // per_slide
    owner = slide_index[:, None] == jnp.arange(SLIDES_DEV, dtype=jnp.int32)[None, :]
    limit_rows = jnp.sum(jnp.where(owner, slide_tiles[None, :], 0), axis=1)
    valid_rows = (crop_index % per_slide < limit_rows).astype(jnp.float32)[:, None]
    vectors = to_places(
        jnp.stack(
            [norm1_gain, norm1_bias, norm2_gain, norm2_bias, scale_attn, scale_mlp, b_out, b_down]
        ),
        here,
    )
    gain_one, shift_one, gain_two, shift_two, scale_one, scale_two, bias_out, bias_down = vectors
    inputs = to_places(tokens, here).astype(jnp.float32)
    grad_out = valid_rows * to_places(cotangent, here).astype(jnp.float32)
    grad_branch_two = scale_two * grad_out
    grad_b_down = jnp.sum(grad_branch_two, axis=0)
    grad_down_low = grad_branch_two.astype(jnp.bfloat16)
    down_rows = jnp.concatenate([grad_down_low, swap_depth(grad_down_low, 1)], axis=0)

    normed_one = layer_norm(inputs, gain_one, shift_one).astype(jnp.bfloat16)
    qkv = (dot_nn(normed_one, full_qkv) + bias_attn).astype(jnp.bfloat16)
    attended, probs = attention_forward(qkv, 3 * heads_w)
    branch_one = dot_nn(attended, full_out) + bias_out
    hidden_state = inputs + scale_one * branch_one
    normed_two = layer_norm(hidden_state, gain_two, shift_two).astype(jnp.bfloat16)

    rows_two = jnp.concatenate([normed_two, swap_depth(normed_two, 1)], axis=0)
    up_pre = dot_nn(rows_two, full_up) + bias_up
    spread = 0.5 * (1.0 + lax.erf(up_pre * (1.0 / math.sqrt(2.0))))
    activated = (up_pre * spread).astype(jnp.bfloat16)
    slope = spread + up_pre * jnp.exp(-0.5 * up_pre * up_pre) * (1.0 / math.sqrt(2.0 * math.pi))
    grad_up = (dot_nt(down_rows, full_down) * slope).astype(jnp.bfloat16)
    norm_rows = dot_nt(grad_up, full_up).astype(jnp.bfloat16)
    grad_rows_two = norm_rows[:row_count].astype(jnp.float32) + swap_depth(norm_rows[row_count:], 1).astype(
        jnp.float32
    )
    down_part = dot_nn(activated, full_down).astype(jnp.bfloat16)
    down_sum = down_part[:row_count].astype(jnp.float32) + swap_depth(down_part[row_count:], 1).astype(jnp.float32)
    branch_two = down_sum + bias_down
    layer_out = valid_rows * (hidden_state + scale_two * branch_two)
    grad_scale_mlp = jnp.sum(grad_out * branch_two, axis=0)

    side = PLANE * BLOCK // 2
    down_near = dot_tn(activated, down_rows[:, :side]).astype(jnp.bfloat16)
    down_across = dot_tn(activated, down_rows[:, side:]).astype(jnp.bfloat16)
    down_own, down_other = reduce_plane(down_near, down_across, 1)
    grad_down = down_own + swap_depth(down_other.astype(jnp.bfloat16), 2).astype(jnp.float32)
    full_grad_down = lax.all_gather(grad_down.astype(jnp.bfloat16), "dp", axis=1, tiled=True).astype(jnp.float32)

    up_across = dot_tn(rows_two[:, side:], grad_up).astype(jnp.bfloat16)
    up_near = dot_tn(rows_two[:, :side], grad_up).astype(jnp.bfloat16)
    up_own, up_other = reduce_plane(up_near, up_across, 0)
    grad_w_up = up_own + swap_depth(up_other.astype(jnp.bfloat16), 2).astype(jnp.float32)
    full_grad_up = lax.all_gather(grad_w_up.astype(jnp.bfloat16), "dp", axis=0, tiled=True).astype(jnp.float32)
    grad_b_up = jnp.sum(grad_up.astype(jnp.float32), axis=0)

    norm2_value, norm2_back = jax.vjp(layer_norm, hidden_state, gain_two, shift_two)
    grad_hidden_norm, grad_norm2_gain, grad_norm2_bias = norm2_back(grad_rows_two)
    grad_hidden = grad_out + grad_hidden_norm
    grad_scale_attn = jnp.sum(grad_hidden * branch_one, axis=0)
    grad_branch_one = scale_one * grad_hidden
    grad_b_out = jnp.sum(grad_branch_one, axis=0)
    grad_attn_low = grad_branch_one.astype(jnp.bfloat16)
    grad_mixed = dot_nt(grad_attn_low, full_out).astype(jnp.bfloat16)

    out_near = dot_tn(attended, grad_attn_low[:, :side]).astype(jnp.bfloat16)
    out_across = dot_tn(attended, grad_attn_low[:, side:]).astype(jnp.bfloat16)
    out_low, out_high = reduce_plane(out_near, out_across, 1)
    grad_w_out = out_low[:heads_w]
    for mask, values in ((1, out_low[heads_w:]), (2, out_high[:heads_w]), (3, out_high[heads_w:])):
        grad_w_out = grad_w_out + swap_depth(values.astype(jnp.bfloat16), mask).astype(jnp.float32)
    full_grad_out = lax.all_gather(grad_w_out.astype(jnp.bfloat16), "dp", axis=1, tiled=True).astype(jnp.float32)

    grad_qkv = attention_backward(qkv, probs, grad_mixed, 3 * heads_w)
    qkv_across = dot_tn(normed_one[:, side:], grad_qkv).astype(jnp.bfloat16)
    qkv_near = dot_tn(normed_one[:, :side], grad_qkv).astype(jnp.bfloat16)
    qkv_low, qkv_high = reduce_plane(qkv_near, qkv_across, 0)
    group = 3 * heads_w
    grad_attn = qkv_low[:, :group]
    for mask, values in ((1, qkv_low[:, group:]), (2, qkv_high[:, :group]), (3, qkv_high[:, group:])):
        grad_attn = grad_attn + swap_depth(values.astype(jnp.bfloat16), mask).astype(jnp.float32)
    full_grad_attn = lax.all_gather(grad_attn.astype(jnp.bfloat16), "dp", axis=0, tiled=True).astype(jnp.float32)

    grad_rows_one = dot_nt(grad_qkv, full_qkv)
    norm1_value, norm1_back = jax.vjp(layer_norm, inputs, gain_one, shift_one)
    grad_in_norm, grad_norm1_gain, grad_norm1_bias = norm1_back(grad_rows_one)
    grad_tokens = grad_hidden + grad_in_norm

    column_sums = jnp.sum(grad_qkv.astype(jnp.float32), axis=0).reshape(DEPTH, group)
    column_sums = jnp.concatenate([column_sums[:, :heads_w], column_sums[:, 2 * heads_w :]], axis=1)
    up_sums = jnp.stack(
        [grad_b_up[:unit_w], jnp.zeros((unit_w,), jnp.float32), grad_b_up[unit_w:], jnp.zeros((unit_w,), jnp.float32)]
    )
    shared = jnp.concatenate([column_sums, up_sums], axis=1)
    shared = jnp.concatenate(
        [lax.dynamic_index_in_dim(shared, level ^ index, 0, keepdims=False) for index in range(DEPTH)]
    )
    small = from_places(
        jnp.stack(
            [
                grad_norm1_gain,
                grad_norm1_bias,
                grad_norm2_gain,
                grad_norm2_bias,
                grad_scale_attn,
                grad_scale_mlp,
                grad_b_out,
                grad_b_down,
            ]
        ),
        here,
    )
    totals = lax.psum(jnp.concatenate([small.reshape(-1), shared]), ("dp", "mp"))
    width = PLANE * BLOCK
    small_total = totals[: 8 * width].reshape(8, width)
    shared_total = lax.dynamic_index_in_dim(
        totals[8 * width :].reshape(DEPTH, 2 * heads_w + unit_w), level, 0, keepdims=False
    )
    return (
        from_places(layer_out, here),
        from_places(grad_tokens, here),
        small_total[0],
        small_total[1],
        full_grad_attn[:, :heads_w],
        shared_total[:heads_w],
        full_grad_attn[:, heads_w : 2 * heads_w],
        full_grad_attn[:, 2 * heads_w :],
        shared_total[heads_w : 2 * heads_w],
        full_grad_out,
        small_total[6],
        small_total[4],
        small_total[2],
        small_total[3],
        full_grad_up,
        shared_total[2 * heads_w :],
        full_grad_down,
        small_total[7],
        small_total[5],
    )


def local_general(
    tokens,
    slide_tiles,
    norm1_gain,
    norm1_bias,
    w_query,
    b_query,
    w_key,
    w_value,
    b_value,
    w_out,
    b_out,
    scale_attn,
    norm2_gain,
    norm2_bias,
    w_up,
    b_up,
    w_down,
    b_down,
    scale_mlp,
    cotangent,
):
    row_count = tokens.shape[0]
    per_slide = CROPS_DEV // SLIDES_DEV
    crop_index = (lax.axis_index("mp") * row_count + jnp.arange(row_count, dtype=jnp.int32)) // L
    slide_index = crop_index // per_slide
    owner = slide_index[:, None] == jnp.arange(SLIDES_DEV, dtype=jnp.int32)[None, :]
    limit_rows = jnp.sum(jnp.where(owner, slide_tiles[None, :], 0), axis=1)
    valid_rows = (crop_index % per_slide < limit_rows).astype(jnp.float32)[:, None]
    inputs = tokens.astype(jnp.float32)
    normed_one = layer_norm(inputs, norm1_gain, norm1_bias).astype(jnp.bfloat16)
    rows_one = lax.all_gather(normed_one, "mp", axis=0, tiled=True)
    queries = (jnp.dot(rows_one, w_query, preferred_element_type=jnp.float32) + b_query).astype(
        jnp.bfloat16
    )
    keys_all = jnp.dot(rows_one, w_key, preferred_element_type=jnp.float32).astype(jnp.bfloat16)
    values_all = (jnp.dot(rows_one, w_value, preferred_element_type=jnp.float32) + b_value).astype(
        jnp.bfloat16
    )
    heads_here = w_query.shape[1] // DH
    query_heads = to_heads(queries, heads_here)
    key_heads = to_heads(keys_all, heads_here)
    value_heads = to_heads(values_all, heads_here)
    scores = attn_scores(query_heads, key_heads)
    top_score = jnp.max(scores, axis=-1, keepdims=True)
    log_total = top_score + jnp.log(jnp.sum(jnp.exp(scores - top_score), axis=-1, keepdims=True))
    weights_low = jnp.exp(scores - log_total).astype(jnp.bfloat16)
    mixed_heads = jnp.einsum(
        "chqk,ckhd->cqhd", weights_low, value_heads, preferred_element_type=jnp.float32
    )
    attended = mixed_heads.reshape(queries.shape).astype(jnp.bfloat16)
    attn_sum = lax.psum_scatter(
        jnp.dot(attended, w_out, preferred_element_type=jnp.float32).astype(jnp.bfloat16),
        "mp",
        scatter_dimension=0,
        tiled=True,
    ).astype(jnp.float32)
    branch_one = attn_sum + b_out
    hidden_state = inputs + scale_attn * branch_one
    normed_two = layer_norm(hidden_state, norm2_gain, norm2_bias).astype(jnp.bfloat16)
    rows_two = lax.all_gather(normed_two, "mp", axis=0, tiled=True)
    up_pre = jnp.dot(rows_two, w_up, preferred_element_type=jnp.float32) + b_up
    activated = gelu_exact(up_pre).astype(jnp.bfloat16)
    down_sum = lax.psum_scatter(
        jnp.dot(activated, w_down, preferred_element_type=jnp.float32).astype(jnp.bfloat16),
        "mp",
        scatter_dimension=0,
        tiled=True,
    ).astype(jnp.float32)
    branch_two = down_sum + b_down
    layer_out = valid_rows * (hidden_state + scale_mlp * branch_two)
    grad_out = valid_rows * cotangent.astype(jnp.float32)
    grad_scale_mlp = jnp.sum(grad_out * branch_two, axis=0)
    grad_branch_two = scale_mlp * grad_out
    grad_b_down = jnp.sum(grad_branch_two, axis=0)
    grad_down_low = grad_branch_two.astype(jnp.bfloat16)
    gelu_value, gelu_back = jax.vjp(gelu_exact, up_pre)
    grad_down_rows = lax.all_gather(grad_down_low, "mp", axis=0, tiled=True)
    grad_act = contract_cols(grad_down_rows, w_down)
    grad_up = gelu_back(grad_act)[0].astype(jnp.bfloat16)
    grad_w_up = contract_rows(rows_two, grad_up)
    grad_w_down = contract_rows(activated, grad_down_rows)
    grad_b_up = jnp.sum(grad_up.astype(jnp.float32), axis=0)
    grad_rows_two = lax.psum_scatter(
        contract_cols(grad_up, w_up).astype(jnp.bfloat16), "mp", scatter_dimension=0, tiled=True
    ).astype(jnp.float32)
    norm2_value, norm2_back = jax.vjp(layer_norm, hidden_state, norm2_gain, norm2_bias)
    grad_hidden_norm, grad_norm2_gain, grad_norm2_bias = norm2_back(grad_rows_two)
    grad_hidden = grad_out + grad_hidden_norm
    grad_scale_attn = jnp.sum(grad_hidden * branch_one, axis=0)
    grad_branch_one = scale_attn * grad_hidden
    grad_b_out = jnp.sum(grad_branch_one, axis=0)
    grad_attn_low = grad_branch_one.astype(jnp.bfloat16)
    grad_attn_rows = lax.all_gather(grad_attn_low, "mp", axis=0, tiled=True)
    grad_w_out = contract_rows(attended, grad_attn_rows)
    grad_mixed = contract_cols(grad_attn_rows, w_out).astype(jnp.bfloat16)
    grad_mixed_heads = to_heads(grad_mixed, heads_here)
    scores_again = attn_scores(query_heads, key_heads)
    probs = jnp.exp(scores_again - log_total)
    probs_low = probs.astype(jnp.bfloat16)
    grad_value_heads = jnp.einsum(
        "chqk,cqhd->ckhd", probs_low, grad_mixed_heads, preferred_element_type=jnp.float32
    )
    grad_values = grad_value_heads.reshape(queries.shape).astype(jnp.bfloat16)
    grad_probs = jnp.einsum(
        "cqhd,ckhd->chqk", grad_mixed_heads, value_heads, preferred_element_type=jnp.float32
    )
    row_inner = jnp.sum(probs * grad_probs, axis=-1, keepdims=True)
    grad_scores = (probs * (grad_probs - row_inner)).astype(jnp.bfloat16)
    inverse_root = 1.0 / math.sqrt(DH)
    grad_query_heads = jnp.einsum(
        "chqk,ckhd->cqhd", grad_scores, key_heads, preferred_element_type=jnp.float32
    )
    grad_queries = (inverse_root * grad_query_heads).reshape(queries.shape).astype(jnp.bfloat16)
    grad_key_heads = jnp.einsum(
        "chqk,cqhd->ckhd", grad_scores, query_heads, preferred_element_type=jnp.float32
    )
    grad_keys = (inverse_root * grad_key_heads).reshape(queries.shape).astype(jnp.bfloat16)
    grad_w_query = contract_rows(rows_one, grad_queries)
    grad_b_query = jnp.sum(grad_queries.astype(jnp.float32), axis=0)
    grad_w_key = contract_rows(rows_one, grad_keys)
    grad_w_value = contract_rows(rows_one, grad_values)
    grad_b_value = jnp.sum(grad_values.astype(jnp.float32), axis=0)
    grad_rows_one = lax.psum_scatter(
        (
            contract_cols(grad_queries, w_query)
            + contract_cols(grad_keys, w_key)
            + contract_cols(grad_values, w_value)
        ).astype(jnp.bfloat16),
        "mp",
        scatter_dimension=0,
        tiled=True,
    ).astype(jnp.float32)
    norm1_value, norm1_back = jax.vjp(layer_norm, inputs, norm1_gain, norm1_bias)
    grad_in_norm, grad_norm1_gain, grad_norm1_bias = norm1_back(grad_rows_one)
    grad_tokens = grad_hidden + grad_in_norm
    small_stack = jnp.stack(
        [
            grad_norm1_gain,
            grad_norm1_bias,
            grad_norm2_gain,
            grad_norm2_bias,
            grad_scale_attn,
            grad_scale_mlp,
            grad_b_out,
            grad_b_down,
        ],
        axis=1,
    )
    small_total = lax.psum(small_stack.astype(jnp.bfloat16), "mp")
    (
        share_wq,
        share_bq,
        share_wk,
        share_wv,
        share_bv,
        share_wo,
        share_up,
        share_bup,
        share_down,
        share_small,
    ) = (
        lax.psum_scatter(
            grad_w_query.astype(jnp.bfloat16), "dp", scatter_dimension=0, tiled=True
        ).astype(jnp.float32),
        lax.psum_scatter(
            grad_b_query.astype(jnp.bfloat16), "dp", scatter_dimension=0, tiled=True
        ).astype(jnp.float32),
        lax.psum_scatter(
            grad_w_key.astype(jnp.bfloat16), "dp", scatter_dimension=0, tiled=True
        ).astype(jnp.float32),
        lax.psum_scatter(
            grad_w_value.astype(jnp.bfloat16), "dp", scatter_dimension=0, tiled=True
        ).astype(jnp.float32),
        lax.psum_scatter(
            grad_b_value.astype(jnp.bfloat16), "dp", scatter_dimension=0, tiled=True
        ).astype(jnp.float32),
        lax.psum_scatter(
            grad_w_out.astype(jnp.bfloat16), "dp", scatter_dimension=0, tiled=True
        ).astype(jnp.float32),
        lax.psum_scatter(
            grad_w_up.astype(jnp.bfloat16), "dp", scatter_dimension=0, tiled=True
        ).astype(jnp.float32),
        lax.psum_scatter(
            grad_b_up.astype(jnp.bfloat16), "dp", scatter_dimension=0, tiled=True
        ).astype(jnp.float32),
        lax.psum_scatter(
            grad_w_down.astype(jnp.bfloat16), "dp", scatter_dimension=0, tiled=True
        ).astype(jnp.float32),
        lax.psum_scatter(small_total, "dp", scatter_dimension=0, tiled=True).astype(jnp.float32),
    )
    (
        full_wq,
        full_bq,
        full_wk,
        full_wv,
        full_bv,
        full_wo,
        full_up,
        full_bup,
        full_down,
        full_small,
    ) = (
        lax.all_gather(share_wq.astype(jnp.bfloat16), "dp", axis=0, tiled=True).astype(
            share_wq.dtype
        ),
        lax.all_gather(share_bq.astype(jnp.bfloat16), "dp", axis=0, tiled=True).astype(
            share_bq.dtype
        ),
        lax.all_gather(share_wk.astype(jnp.bfloat16), "dp", axis=0, tiled=True).astype(
            share_wk.dtype
        ),
        lax.all_gather(share_wv.astype(jnp.bfloat16), "dp", axis=0, tiled=True).astype(
            share_wv.dtype
        ),
        lax.all_gather(share_bv.astype(jnp.bfloat16), "dp", axis=0, tiled=True).astype(
            share_bv.dtype
        ),
        lax.all_gather(share_wo.astype(jnp.bfloat16), "dp", axis=0, tiled=True).astype(
            share_wo.dtype
        ),
        lax.all_gather(share_up.astype(jnp.bfloat16), "dp", axis=0, tiled=True).astype(
            share_up.dtype
        ),
        lax.all_gather(share_bup.astype(jnp.bfloat16), "dp", axis=0, tiled=True).astype(
            share_bup.dtype
        ),
        lax.all_gather(share_down.astype(jnp.bfloat16), "dp", axis=0, tiled=True).astype(
            share_down.dtype
        ),
        lax.all_gather(share_small.astype(jnp.bfloat16), "dp", axis=0, tiled=True).astype(
            share_small.dtype
        ),
    )
    return (
        layer_out,
        grad_tokens,
        full_small[:, 0],
        full_small[:, 1],
        full_wq,
        full_bq,
        full_wk,
        full_wv,
        full_bv,
        full_wo,
        full_small[:, 6],
        full_small[:, 4],
        full_small[:, 2],
        full_small[:, 3],
        full_up,
        full_bup,
        full_down,
        full_small[:, 7],
        full_small[:, 5],
    )


def solution(mesh):
    in_specs = (
        P(("dp", "mp"), None),
        P("dp"),
        P(),
        P(),
        P(None, "mp"),
        P("mp"),
        P(None, "mp"),
        P(None, "mp"),
        P("mp"),
        P("mp", None),
        P(),
        P(),
        P(),
        P(),
        P(None, "mp"),
        P("mp"),
        P("mp", None),
        P(),
        P(),
        P(("dp", "mp"), None),
    )
    out_specs = (
        P(("dp", "mp"), None),
        P(("dp", "mp"), None),
        P(),
        P(),
        P(None, "mp"),
        P("mp"),
        P(None, "mp"),
        P(None, "mp"),
        P("mp"),
        P("mp", None),
        P(),
        P(),
        P(),
        P(),
        P(None, "mp"),
        P("mp"),
        P("mp", None),
        P(),
        P(),
    )
    paired = mesh.shape["dp"] == 8 and mesh.shape["mp"] == 4
    local = local_paired if paired else local_general
    return jax.shard_map(local, mesh=mesh, in_specs=in_specs, out_specs=out_specs, check_vma=False)
```

```python
import math

import jax
import jax.numpy as jnp
from jax import lax
from jax.experimental import pallas as pl
from jax.experimental.pallas import tpu as pltpu
from jax.sharding import PartitionSpec as P

DH = 64
L = 197
SLIDES_DEV = 2
CROPS_DEV = 8


def layer_norm(values, gain, shift):
    average = jnp.mean(values, axis=-1, keepdims=True)
    centered = values - average
    spread = jnp.mean(centered * centered, axis=-1, keepdims=True)
    return centered * lax.rsqrt(spread + 1e-06) * gain + shift


def gelu_exact(values):
    return jax.nn.gelu(values, approximate=False)


def contract_rows(left, right):
    return lax.dot_general(
        left, right, (((0,), (0,)), ((), ())), preferred_element_type=jnp.float32
    )


def contract_cols(left, right):
    return lax.dot_general(
        left, right, (((1,), (1,)), ((), ())), preferred_element_type=jnp.float32
    )


def to_heads(matrix, heads_here):
    return matrix.reshape(matrix.shape[0] // L, L, heads_here, DH)


def attn_scores(query_heads, key_heads):
    product = jnp.einsum(
        "cqhd,ckhd->chqk", query_heads, key_heads, preferred_element_type=jnp.float32
    )
    return product * (1.0 / math.sqrt(DH))


BLOCK = 128
QUARTER = 256
X_SIDE, Y_SIDE, CORE_SIDE = 2, 4, 1
PLANE = 8
CHIPS = 4
DEPTH = 4
OWN_CORE = CHIPS
FLAGS = CHIPS + 1
GAIN_ONE, SHIFT_ONE, GAIN_TWO, SHIFT_TWO, SCALE_ATTN, SCALE_MLP, BIAS_OUT, BIAS_DOWN = range(8)
VMEM_BYTES = 24 * 2**20


def swap_plane(values, mask):
    return lax.ppermute(values, "dp", [(i, i ^ mask) for i in range(PLANE)])


def swap_depth(values, mask):
    return lax.ppermute(values, "mp", [(i, i ^ mask) for i in range(DEPTH)])


def plane_swaps(values):
    return [swap_plane(values, side) for side in (X_SIDE, Y_SIDE, X_SIDE | Y_SIDE)]


class Order:
    def __init__(self):
        self.last = None

    def hold(self, values):
        leaves, tree = jax.tree.flatten(values)
        return jax.tree.unflatten(tree, lax.optimization_barrier(tuple(leaves) + (self.last,))[:-1])

    def land(self, *arrays):
        *arrays, self.last = lax.optimization_barrier(arrays + (self.last,))
        return arrays

    def __call__(self, step, *args):
        leaves, tree = jax.tree.flatten(args)
        arrays = [i for i, leaf in enumerate(leaves) if isinstance(leaf, jax.Array)]
        if self.last is not None:
            held = lax.optimization_barrier(tuple(leaves[i] for i in arrays) + (self.last,))
            for i, value in zip(arrays, held):
                leaves[i] = value
        out = step(*jax.tree.unflatten(tree, leaves))
        self.last = jax.tree.leaves(out)[0]
        return out


def dot_nt(left, right):
    return lax.dot_general(left, right, (((1,), (1,)), ((), ())), preferred_element_type=jnp.float32)


def dot_tn(left, right):
    return lax.dot_general(left, right, (((0,), (0,)), ((), ())), preferred_element_type=jnp.float32)


def dot_nn(left, right):
    return lax.dot_general(left, right, (((1,), (0,)), ((), ())), preferred_element_type=jnp.float32)


def add_low(*values):
    return sum(value.astype(jnp.float32) for value in values).astype(jnp.bfloat16)


def crop_ranges(rows):
    ranges = []
    for crop in range(rows // L):
        low = crop * L // 16 * 16
        high = min((crop + 1) * L + 15, rows + 15) // 16 * 16
        ranges.append((low, min(high, rows), crop * L - low))
    return ranges


def whole(array):
    zeros = (0,) * array.ndim
    return pl.BlockSpec(array.shape, lambda *_: zeros)


def kernel_call(body, name, meta, args, in_specs, out_shape, out_specs, grid=(1,), scratch=(), flops=1000):
    return pl.pallas_call(
        body,
        grid_spec=pltpu.PrefetchScalarGridSpec(
            num_scalar_prefetch=1,
            grid=grid,
            in_specs=in_specs,
            out_specs=out_specs,
            scratch_shapes=list(scratch),
        ),
        out_shape=out_shape,
        compiler_params=pltpu.CompilerParams(vmem_limit_bytes=VMEM_BYTES),
        cost_estimate=pl.CostEstimate(flops=flops, bytes_accessed=1000, transcendentals=0),
        name=name,
    )(meta, *args)


def shape_of(*dims, dtype=jnp.bfloat16):
    return jax.ShapeDtypeStruct(dims, dtype)


def normalized(values):
    centered = values - jnp.mean(values, axis=-1, keepdims=True)
    inverse = lax.rsqrt(jnp.mean(centered * centered, axis=-1, keepdims=True) + 1e-06)
    return centered * inverse, inverse


def norm_gradient(unit, inverse, gain, grad):
    wide = grad * gain
    return inverse * (
        wide - jnp.mean(wide, axis=-1, keepdims=True) - unit * jnp.mean(wide * unit, axis=-1, keepdims=True)
    )


def valid_column(meta_ref, rows):
    row = lax.broadcasted_iota(jnp.int32, (rows, 1), 0)
    valid = jnp.zeros((rows, 1), jnp.float32)
    for crop in range(rows // L):
        inside = (row >= crop * L) & (row < (crop + 1) * L)
        valid = jnp.where(inside, meta_ref[FLAGS + crop].astype(jnp.float32), valid)
    return valid


def quarter_of(meta_ref, side):
    return pl.ds(pl.multiple_of(meta_ref[side] * QUARTER, QUARTER), QUARTER)


def slice_weights(meta, w_query, w_key, w_value, w_out, w_up, w_down, biases):
    half_h, half_u = w_query.shape[1] // 2, w_up.shape[1] // 2
    n_h, n_u = half_h // BLOCK, half_u // BLOCK

    def body(meta_ref, q_ref, k_ref, v_ref, o_ref, up_ref, down_ref, bias_ref, attn_ref, rest_ref):
        core = meta_ref[OWN_CORE]
        for which, ref in enumerate((q_ref, k_ref, v_ref)):
            attn_ref[which * QUARTER : (which + 1) * QUARTER, :] = ref[...]
        for b in range(2):
            row = 3 * QUARTER + b * half_h
            attn_ref[row : row + half_h, :] = o_ref[:, b * BLOCK : (b + 1) * BLOCK]
        picked = jnp.concatenate(
            [
                bias_ref[pl.ds(core, n_h), :],
                bias_ref[pl.ds(2 * n_h + core, n_h), :],
                bias_ref[pl.ds(4 * n_h + n_u * core, n_u), :],
            ],
            axis=0,
        )
        high = picked.astype(jnp.bfloat16)
        low = (picked - high.astype(jnp.float32)).astype(jnp.bfloat16)
        spare = jnp.zeros((16 - 2 * picked.shape[0], BLOCK), jnp.bfloat16)
        attn_ref[4 * QUARTER :, :] = jnp.concatenate([high, low, spare], axis=0)
        for b in range(n_u):
            rest_ref[b * QUARTER : (b + 1) * QUARTER, :] = up_ref[:, b * BLOCK : (b + 1) * BLOCK]
        for b in range(2):
            row = n_u * QUARTER + b * half_u
            rest_ref[row : row + half_u, :] = down_ref[:, b * BLOCK : (b + 1) * BLOCK]

    args = (w_query, w_key, w_value, w_out, w_up, w_down, biases)
    out = [shape_of(4 * QUARTER + 16, BLOCK), shape_of(2 * n_u * QUARTER, BLOCK)]
    return kernel_call(
        body,
        "slice_weights",
        meta,
        args,
        [pl.BlockSpec((QUARTER, half_h), lambda i, m: (m[0], m[OWN_CORE]))] * 3
        + [
            pl.BlockSpec((half_h, QUARTER), lambda i, m: (m[OWN_CORE], m[0])),
            pl.BlockSpec((QUARTER, half_u), lambda i, m: (m[0], m[OWN_CORE])),
            pl.BlockSpec((half_u, QUARTER), lambda i, m: (m[OWN_CORE], m[0])),
            whole(biases),
        ],
        out,
        [whole(o) for o in out],
    )


def turn_into(meta_ref, values, turned_ref, index=None):
    for side in range(CHIPS):
        rows = slice(side * QUARTER, (side + 1) * QUARTER)
        if index is None:
            turned_ref[rows, :] = values[:, quarter_of(meta_ref, side)].T
        else:
            turned_ref[rows, :] = values[index, :, quarter_of(meta_ref, side)].T


def turn(meta, *arrays):
    def body(meta_ref, *refs):
        for source, target in zip(refs[: len(arrays)], refs[len(arrays) :]):
            turn_into(meta_ref, source, target)

    out = [shape_of(*a.shape[::-1]) for a in arrays]
    return kernel_call(body, "turn", meta, arrays, [whole(a) for a in arrays], out, [whole(o) for o in out])


def prepare(meta, tokens, tokens_other, cotangent, vectors):
    rows, width = tokens.shape

    def body(meta_ref, tokens_ref, other_ref, cot_ref, vec_ref, one_ref, two_ref, grad_ref, sum_ref, *turned):
        for source, target in ((tokens_ref, one_ref), (other_ref, two_ref)):
            unit, _ = normalized(source[...].astype(jnp.float32))
            target[...] = (unit * vec_ref[GAIN_ONE : GAIN_ONE + 1] + vec_ref[SHIFT_ONE : SHIFT_ONE + 1]).astype(
                jnp.bfloat16
            )
        grad = vec_ref[SCALE_MLP : SCALE_MLP + 1] * (valid_column(meta_ref, rows) * cot_ref[...].astype(jnp.float32))
        sum_ref[...] = jnp.sum(grad, axis=0, keepdims=True)
        grad_ref[...] = grad.astype(jnp.bfloat16)
        for source, target in zip((one_ref, two_ref, grad_ref), turned):
            turn_into(meta_ref, source, target)

    args = (tokens, tokens_other, cotangent, vectors)
    out = [shape_of(rows, width)] * 3 + [shape_of(1, width, dtype=jnp.float32)] + [shape_of(width, rows)] * 3
    return kernel_call(body, "prepare", meta, args, [whole(a) for a in args], out, [whole(o) for o in out])


def fill_heads(meta_ref, chip_refs, weight_ref):
    for side, ref in enumerate(chip_refs):
        at = quarter_of(meta_ref, side)
        for which in range(3):
            weight_ref[at, which * BLOCK : (which + 1) * BLOCK] = ref[which * QUARTER : (which + 1) * QUARTER, :]


def head_specs(width, chips):
    own = [pl.BlockSpec((width, BLOCK), lambda g, m: (0, m[OWN_CORE]))] * 3
    far = [pl.BlockSpec((3 * QUARTER, BLOCK), lambda g, m: (jnp.maximum(g - 1, 0), 0))] * len(chips)
    return own, far


def attention_forward(meta, normed, other, w_query, w_key, w_value, biases, level_attn, chips):
    rows, width = normed.shape
    group = 3 * BLOCK
    ranges = crop_ranges(rows)
    span = max(high - low for low, high, _ in ranges)
    scale = 1.0 / math.sqrt(DH)
    count = (level_attn[0].shape[0] - 4 * QUARTER - 4) // 2

    def body(meta_ref, normed_ref, other_ref, q_ref, k_ref, v_ref, bias_ref, one_ref, two_ref, three_ref, *refs):
        chip_refs, (qkv_ref, out_ref, prob_ref, weight_ref, sum_ref) = refs[:CHIPS], refs[CHIPS:]
        step = pl.program_id(0)
        core = meta_ref[OWN_CORE]

        @pl.when(step == 0)
        def _():
            for which, ref in enumerate((q_ref, k_ref, v_ref)):
                weight_ref[:, which * BLOCK : (which + 1) * BLOCK] = ref[...]
            sum_ref[0:1, :] = bias_ref[pl.ds(core, 1), :]
            sum_ref[1:2, :] = bias_ref[pl.ds(2 + core, 1), :]

        for index, ref in enumerate((one_ref, two_ref, three_ref)):
            @pl.when(step == index + 1)
            def _():
                both = ref[...].astype(jnp.float32)
                sum_ref[0:2, :] = both[0:2] + both[count : count + 2]

        @pl.when(step > 0)
        def _():
            fill_heads(meta_ref, chip_refs, weight_ref)

        bias = jnp.concatenate([sum_ref[0:1, :], jnp.zeros((1, BLOCK), jnp.float32), sum_ref[1:2, :]], axis=1)
        for part, rows_ref in enumerate((normed_ref, other_ref)):
            qkv_ref[part] = (dot_nn(rows_ref[...], weight_ref[...]) + bias).astype(jnp.bfloat16)
        for part in range(2):
            for index, (low, high, skip) in enumerate(ranges):
                size = high - low
                query = qkv_ref[part, low:high, 0:BLOCK]
                key = qkv_ref[part, low:high, BLOCK : 2 * BLOCK]
                value = qkv_ref[part, low:high, 2 * BLOCK : 3 * BLOCK]
                lane = lax.broadcasted_iota(jnp.int32, (size, BLOCK), 1)
                row = lax.broadcasted_iota(jnp.int32, (size, size), 0)
                column = lax.broadcasted_iota(jnp.int32, (size, size), 1)
                seen = (column >= skip) & (column < skip + L)
                inside = seen & (row >= skip) & (row < skip + L)
                parts = []
                for head in range(2):
                    own = (lane < DH) if head == 0 else (lane >= DH)
                    scores = dot_nt(jnp.where(own, query, jnp.zeros_like(query)), key) * scale
                    scores = jnp.where(seen, scores, -1e30)
                    top = jnp.max(scores, axis=1, keepdims=True)
                    raised = jnp.exp(scores - top)
                    total = jnp.sum(raised, axis=1, keepdims=True)
                    probs = jnp.where(inside, raised * (1.0 / total), 0.0).astype(jnp.bfloat16)
                    prob_ref[0, part, index, head, 0:size, 0:size] = probs
                    parts.append(dot_nn(probs, value))
                mixed = jnp.where(lane < DH, parts[0], parts[1]).astype(jnp.bfloat16)
                if skip:
                    edge = lax.broadcasted_iota(jnp.int32, (size, BLOCK), 0) >= skip
                    mixed = jnp.where(edge, mixed, out_ref[part, low:high, :])
                out_ref[part, low:high, :] = mixed

    prob_shape = (DEPTH, 2, len(ranges), 2, span, span)
    own_specs, far_specs = head_specs(width, chips)
    tail = 4 * QUARTER // 16
    args = (normed, other, w_query, w_key, w_value, biases) + tuple(level_attn) + tuple(chips)
    return kernel_call(
        body,
        "attention_forward",
        meta,
        args,
        [whole(normed), whole(other)] + own_specs + [whole(biases)] + [pl.BlockSpec((16, BLOCK), lambda g, m: (tail, 0))] * 3 + far_specs,
        [shape_of(2, rows, DEPTH * group), shape_of(2, rows, DEPTH * BLOCK), shape_of(*prob_shape)],
        [
            pl.BlockSpec((2, rows, group), lambda g, m: (0, 0, g)),
            pl.BlockSpec((2, rows, BLOCK), lambda g, m: (0, 0, g)),
            pl.BlockSpec((1,) + prob_shape[1:], lambda g, m: (g, 0, 0, 0, 0, 0)),
        ],
        grid=(DEPTH,),
        scratch=[pltpu.VMEM((width, group), jnp.bfloat16), pltpu.VMEM((8, BLOCK), jnp.float32)],
    )


def attention_out(meta, attended, w_out, chips):
    rows, width = attended.shape[1], w_out.shape[1]

    def body(meta_ref, attended_ref, own_ref, *refs):
        chip_refs, (near_ref, low_ref, high_ref, weight_ref) = refs[:CHIPS], refs[CHIPS:]
        weight_ref[0:BLOCK, :] = own_ref[...]
        for side, ref in enumerate(chip_refs):
            start = pl.multiple_of(meta_ref[side] * QUARTER, QUARTER)
            for index in range(DEPTH - 1):
                for b in range(2):
                    weight_ref[(index + 1) * BLOCK : (index + 2) * BLOCK, pl.ds(start + b * BLOCK, BLOCK)] = ref[
                        index, b * BLOCK : (b + 1) * BLOCK, :
                    ]
        near_ref[...] = dot_nn(attended_ref[0], weight_ref[...])
        across = dot_nn(attended_ref[1], weight_ref[...]).astype(jnp.bfloat16)
        low_ref[...] = across[:, : width // 2]
        high_ref[...] = across[:, width // 2 :]

    views = tuple(chip.reshape(DEPTH - 1, QUARTER, BLOCK) for chip in chips)
    view_spec = whole(views[0])
    out = [shape_of(rows, width, dtype=jnp.float32)] + [shape_of(rows, width // 2)] * 2
    return kernel_call(
        body, "attention_out", meta, (attended, w_out) + views,
        [whole(attended), pl.BlockSpec((BLOCK, width), lambda i, m: (m[OWN_CORE], 0))] + [view_spec] * CHIPS,
        out, [whole(o) for o in out], scratch=[pltpu.VMEM((DEPTH * BLOCK, width), jnp.bfloat16)],
    )


def attention_norm(meta, near, low, high, tokens, vectors):
    rows, width = tokens.shape

    def body(meta_ref, near_ref, low_ref, high_ref, tokens_ref, vec_ref, hidden_ref, branch_ref, normed_ref):
        got = jnp.concatenate([low_ref[...], high_ref[...]], axis=1).astype(jnp.float32)
        branch = near_ref[...] + got + vec_ref[BIAS_OUT : BIAS_OUT + 1]
        branch_ref[...] = branch
        hidden = tokens_ref[...].astype(jnp.float32) + vec_ref[SCALE_ATTN : SCALE_ATTN + 1] * branch
        hidden_ref[...] = hidden
        unit, _ = normalized(hidden)
        normed_ref[...] = (unit * vec_ref[GAIN_TWO : GAIN_TWO + 1] + vec_ref[SHIFT_TWO : SHIFT_TWO + 1]).astype(
            jnp.bfloat16
        )

    args = (near, low, high, tokens, vectors)
    out = [shape_of(rows, width, dtype=jnp.float32)] * 2 + [shape_of(rows, width)]
    return kernel_call(body, "attention_norm", meta, args, [whole(a) for a in args], out, [whole(o) for o in out])


def fill_units(meta_ref, chip_refs, up_weight, down_weight):
    half_u = down_weight.shape[0]
    n_u = half_u // BLOCK
    for side, ref in enumerate(chip_refs):
        at = quarter_of(meta_ref, side)
        start = pl.multiple_of(meta_ref[side] * QUARTER, QUARTER)
        for b in range(n_u):
            up_weight[at, b * BLOCK : (b + 1) * BLOCK] = ref[b * QUARTER : (b + 1) * QUARTER, :]
        base = n_u * QUARTER
        for b in range(2):
            down_weight[:, pl.ds(start + b * BLOCK, BLOCK)] = ref[base + b * half_u : base + (b + 1) * half_u, :]


def feed_forward(meta, normed, grads, w_up, w_down, bias_up, chips, flops=1000):
    rows, width = normed[0].shape
    half_u = w_up.shape[1] // 2
    count = len(normed)

    def body(meta_ref, *refs):
        normed_refs, grad_refs, refs = refs[:count], refs[count : 2 * count], refs[2 * count :]
        up_ref, down_ref, bias_ref = refs[:3]
        chip_refs, refs = refs[3 : 3 + CHIPS], refs[3 + CHIPS :]
        act_refs, gup_refs, back_refs, refs = refs[:count], refs[count : 2 * count], refs[2 * count : 3 * count], refs[3 * count :]
        sum_ref, up_weight, down_weight, total_ref = refs
        step = pl.program_id(0)

        @pl.when(step == 0)
        def _():
            up_weight[...] = up_ref[...]
            down_weight[...] = down_ref[...]

        @pl.when(step == 1)
        def _():
            fill_units(meta_ref, chip_refs, up_weight, down_weight)

        sums = jnp.zeros(sum_ref.shape, jnp.float32)
        for part in range(count):
            pre = dot_nn(normed_refs[part][...], up_weight[...]) + bias_ref[...]
            spread = 0.5 * (1.0 + lax.erf(pre * (1.0 / math.sqrt(2.0))))
            act_refs[part][...] = (pre * spread).astype(jnp.bfloat16)
            slope = spread + pre * jnp.exp(-0.5 * pre * pre) * (1.0 / math.sqrt(2.0 * math.pi))
            grad_up = (dot_nt(grad_refs[part][...], down_weight[...]) * slope).astype(jnp.bfloat16)
            gup_refs[part][...] = grad_up
            sums = sums + jnp.sum(grad_up.astype(jnp.float32), axis=0, keepdims=True)
            back = dot_nt(grad_up, up_weight[...])

            @pl.when(step == 0)
            def _():
                total_ref[part] = back

            @pl.when(step == 1)
            def _():
                back_refs[part][...] = (total_ref[part] + back).astype(jnp.bfloat16)

        sum_ref[...] = sums

    args = tuple(normed) + tuple(grads)
    chip_spec = whole(chips[0])
    by_unit = pl.BlockSpec((rows, half_u), lambda g, m: (0, g))
    outs = kernel_call(
        body,
        "feed_forward",
        meta,
        args + (w_up, w_down, bias_up) + tuple(chips),
        [whole(a) for a in args]
        + [
            pl.BlockSpec((width, half_u), lambda g, m: (0, m[OWN_CORE])),
            pl.BlockSpec((half_u, width), lambda g, m: (m[OWN_CORE], 0)),
            pl.BlockSpec((1, half_u), lambda g, m: (0, g)),
        ]
        + [chip_spec] * CHIPS,
        [shape_of(rows, 2 * half_u)] * (2 * count)
        + [shape_of(rows, width)] * count
        + [shape_of(1, 2 * half_u, dtype=jnp.float32)],
        [by_unit] * (2 * count)
        + [pl.BlockSpec((rows, width), lambda g, m: (0, 0))] * count
        + [pl.BlockSpec((1, half_u), lambda g, m: (0, g))],
        grid=(2,),
        scratch=[
            pltpu.VMEM((width, half_u), jnp.bfloat16),
            pltpu.VMEM((half_u, width), jnp.bfloat16),
            pltpu.VMEM((count, rows, width), jnp.float32),
        ],
        flops=flops,
    )
    return outs[:count], outs[count : 2 * count], outs[2 * count : 3 * count], outs[3 * count]


def feed_down(meta, acts, w_down, chips):
    rows = acts[0].shape[0]
    half_u, width = w_down.shape[0] // 2, w_down.shape[1]
    count = len(acts)

    def body(meta_ref, *refs):
        act_refs, down_ref, refs = refs[:count], refs[count], refs[count + 1 :]
        chip_refs, out_refs, weight_ref = refs[:CHIPS], refs[CHIPS:-1], refs[-1]
        weight_ref[0:half_u, :] = down_ref[...]
        for side, ref in enumerate(chip_refs):
            start = pl.multiple_of(meta_ref[side] * QUARTER, QUARTER)
            for b in range(2):
                weight_ref[half_u:, pl.ds(start + b * BLOCK, BLOCK)] = ref[b * half_u : (b + 1) * half_u, :]
        for act_ref, out_ref in zip(act_refs, out_refs):
            out_ref[...] = dot_nn(act_ref[...], weight_ref[...]).astype(jnp.bfloat16)

    out = [shape_of(rows, width)] * count
    return kernel_call(
        body, "feed_down", meta, tuple(acts) + (w_down,) + tuple(chips),
        [whole(a) for a in acts]
        + [pl.BlockSpec((half_u, width), lambda i, m: (m[OWN_CORE], 0))]
        + [pl.BlockSpec((2 * half_u, BLOCK), lambda i, m: (1, 0))] * CHIPS,
        out, [whole(o) for o in out], scratch=[pltpu.VMEM((2 * half_u, width), jnp.bfloat16)],
    )


def put_sides(lane, values, keep_ref, send_ref, at):
    keep, send = ((0, 2), (1, 3)) if lane == 0 else ((0, 1), (2, 3))
    for ref, sides in ((keep_ref, keep), (send_ref, send)):
        for index, side in enumerate(sides):
            ref[index * QUARTER : (index + 1) * QUARTER, at] = values[side * QUARTER : (side + 1) * QUARTER].astype(
                jnp.bfloat16
            )


def feed_gradients(meta, normed, turned_grads, gups, acts):
    rows, width = normed[0].shape
    half_u = gups[0].shape[1] // 2

    def body(meta_ref, *refs):
        normed_refs, turned_refs, refs = refs[:4], refs[4:8], refs[8:]
        n = len(gups)
        gup_refs, act_refs, refs = refs[:n], refs[n : 2 * n], refs[2 * n :]
        outs, own_turned = refs[:4], refs[4:]
        step = pl.program_id(0)

        @pl.when(step == 0)
        def _():
            for source, target in zip(normed_refs, own_turned):
                turn_into(meta_ref, source, target)

        def product(lefts, rights):
            return sum(dot_nn(left[...], right[...]) for left, right in zip(lefts, rights))

        for lane in range(2):
            @pl.when(step == 2 * lane)
            def _():
                put_sides(lane, product(own_turned, gup_refs), outs[2 * lane], outs[2 * lane + 1], slice(None))

            @pl.when(step == 2 * lane + 1)
            def _():
                put_sides(lane, product(turned_refs, act_refs), outs[2 * lane], outs[2 * lane + 1], slice(None))

    args = tuple(normed) + tuple(turned_grads)
    out = [shape_of(width // 2, 2 * half_u)] * 4
    by_lane = [pl.BlockSpec((rows, half_u), lambda g, m: (0, g >> 1))] * len(gups)
    out_specs = [pl.BlockSpec((width // 2, half_u), lambda g, m: (0, jnp.minimum(g, 1)))] * 2
    out_specs += [pl.BlockSpec((width // 2, half_u), lambda g, m: (0, jnp.maximum(g - 2, 0)))] * 2
    return kernel_call(
        body, "feed_gradients", meta, args + tuple(gups) + tuple(acts),
        [whole(a) for a in args] + by_lane * 2, out, out_specs, grid=(4,),
        scratch=[pltpu.VMEM((width, rows), jnp.bfloat16)] * 4,
    )


def hidden_gradient(meta, backs, hidden, branch, cotangent, vectors):
    rows, width = hidden.shape

    def body(meta_ref, *refs):
        back_refs, (hidden_ref, branch_ref, cot_ref, vec_ref, dh_ref, e1_ref, sum_ref) = refs[: len(backs)], refs[len(backs) :]
        grad = sum(ref[...].astype(jnp.float32) for ref in back_refs)
        unit, inverse = normalized(hidden_ref[...])
        sum_ref[0:1, :] = jnp.sum(grad * unit, axis=0, keepdims=True)
        sum_ref[1:2, :] = jnp.sum(grad, axis=0, keepdims=True)
        total = valid_column(meta_ref, rows) * cot_ref[...].astype(jnp.float32) + norm_gradient(
            unit, inverse, vec_ref[GAIN_TWO : GAIN_TWO + 1], grad
        )
        dh_ref[...] = total
        sum_ref[2:3, :] = jnp.sum(total * branch_ref[...], axis=0, keepdims=True)
        scaled = vec_ref[SCALE_ATTN : SCALE_ATTN + 1] * total
        sum_ref[3:4, :] = jnp.sum(scaled, axis=0, keepdims=True)
        e1_ref[...] = scaled.astype(jnp.bfloat16)

    args = tuple(backs) + (hidden, branch, cotangent, vectors)
    out = [shape_of(rows, width, dtype=jnp.float32), shape_of(rows, width), shape_of(4, width, dtype=jnp.float32)]
    return kernel_call(body, "hidden_gradient", meta, args, [whole(a) for a in args], out, [whole(o) for o in out])


def attention_backward(meta, qkv, probs, attended, grads, turned_normed, w_out, chips, lane):
    rows, width = grads[0].shape
    group = 3 * BLOCK
    ranges = crop_ranges(rows)
    groups = DEPTH // 2
    scale = 1.0 / math.sqrt(DH)
    base = lane * groups

    def body(meta_ref, qkv_ref, prob_ref, mixed_ref, e1_ref, e1_other_ref, n_ref, n_other_ref, own_ref, *refs):
        chip_refs, (out_ref, keep_ref, send_ref, weight_ref, grad_ref, turned_e, turned_other) = refs[:CHIPS], refs[CHIPS:]
        step = pl.program_id(0)

        @pl.when(step == 0)
        def _():
            turn_into(meta_ref, e1_ref, turned_e)
            turn_into(meta_ref, e1_other_ref, turned_other)

        def far_weights():
            for side, ref in enumerate(chip_refs):
                start = pl.multiple_of(meta_ref[side] * QUARTER, QUARTER)
                for b in range(2):
                    weight_ref[:, pl.ds(start + b * BLOCK, BLOCK)] = ref[0, b * BLOCK : (b + 1) * BLOCK, :]

        if lane == 0:
            @pl.when(step == 0)
            def _():
                weight_ref[...] = own_ref[...]

            pl.when(step > 0)(far_weights)
        else:
            far_weights()
        for part, ref in enumerate((e1_ref, e1_other_ref)):
            grad_ref[part] = dot_nt(ref[...], weight_ref[...]).astype(jnp.bfloat16)
        for part in range(2):
            for index, (low, high, skip) in enumerate(ranges):
                size = high - low
                query = qkv_ref[part, low:high, 0:BLOCK]
                key = qkv_ref[part, low:high, BLOCK : 2 * BLOCK]
                value = qkv_ref[part, low:high, 2 * BLOCK : 3 * BLOCK]
                grad = grad_ref[part, low:high, :]
                lane_of = lax.broadcasted_iota(jnp.int32, (size, BLOCK), 1)
                row = lax.broadcasted_iota(jnp.int32, (size, BLOCK), 0)
                parts = []
                for head in range(2):
                    own = (lane_of < DH) if head == 0 else (lane_of >= DH)
                    low_probs = prob_ref[0, part, index, head, 0:size, 0:size]
                    grad_value = dot_tn(low_probs, grad)
                    grad_probs = dot_nt(jnp.where(own, grad, jnp.zeros_like(grad)), value)
                    wide = low_probs.astype(jnp.float32)
                    weighted = wide * grad_probs
                    inner = jnp.sum(weighted, axis=1, keepdims=True)
                    grad_scores = (weighted - wide * inner).astype(jnp.bfloat16)
                    parts.append(
                        (dot_nn(grad_scores, key) * scale, dot_tn(grad_scores, query) * scale, grad_value)
                    )
                for which in range(3):
                    at = slice(which * BLOCK, (which + 1) * BLOCK)
                    joined = jnp.where(lane_of < DH, parts[0][which], parts[1][which]).astype(jnp.bfloat16)
                    if skip:
                        joined = jnp.where(row >= skip, joined, out_ref[part, low:high, at])
                    out_ref[part, low:high, at] = joined
        both = dot_nn(n_ref[...], out_ref[0]) + dot_nn(n_other_ref[...], out_ref[1])
        put_sides(lane, both, keep_ref, send_ref, slice(0, group))
        both = dot_nn(turned_e[...], mixed_ref[0]) + dot_nn(turned_other[...], mixed_ref[1])
        put_sides(lane, both, keep_ref, send_ref, slice(group, group + BLOCK))

    views = tuple(chip.reshape(DEPTH - 1, QUARTER, BLOCK) for chip in chips)
    args = (qkv, probs, attended) + tuple(grads) + tuple(turned_normed) + (w_out,) + views
    return kernel_call(
        body,
        "attention_backward",
        meta,
        args,
        [
            pl.BlockSpec((2, rows, group), lambda g, m: (0, 0, base + g)),
            pl.BlockSpec((1,) + probs.shape[1:], lambda g, m: (base + g, 0, 0, 0, 0, 0)),
            pl.BlockSpec((2, rows, BLOCK), lambda g, m: (0, 0, base + g)),
            whole(grads[0]),
            whole(grads[1]),
            whole(turned_normed[0]),
            whole(turned_normed[1]),
            pl.BlockSpec((BLOCK, width), lambda g, m: (m[OWN_CORE], 0)),
        ]
        + [pl.BlockSpec((1, QUARTER, BLOCK), lambda g, m: (jnp.maximum(base + g - 1, 0), 0, 0))] * CHIPS,
        [shape_of(2, rows, groups * group)] + [shape_of(width // 2, groups * 4 * BLOCK)] * 2,
        [pl.BlockSpec((2, rows, group), lambda g, m: (0, 0, g))]
        + [pl.BlockSpec((width // 2, 4 * BLOCK), lambda g, m: (0, g))] * 2,
        grid=(groups,),
        scratch=[
            pltpu.VMEM((BLOCK, width), jnp.bfloat16),
            pltpu.VMEM((2, rows, BLOCK), jnp.bfloat16),
            pltpu.VMEM((width, rows), jnp.bfloat16),
            pltpu.VMEM((width, rows), jnp.bfloat16),
        ],
    )


def token_shares(meta, grads, w_query, w_key, w_value, chips):
    rows = grads[0].shape[1]
    width = w_query.shape[0]
    group = 3 * BLOCK

    def body(meta_ref, low_ref, high_ref, q_ref, k_ref, v_ref, *refs):
        chip_refs, (near_ref, across_ref, bias_ref, weight_ref, total_ref) = refs[:CHIPS], refs[CHIPS:]
        step = pl.program_id(0)

        @pl.when(step == 0)
        def _():
            for which, ref in enumerate((q_ref, k_ref, v_ref)):
                weight_ref[:, which * BLOCK : (which + 1) * BLOCK] = ref[...]

        @pl.when(step > 0)
        def _():
            fill_heads(meta_ref, chip_refs, weight_ref)

        def add(ref):
            sums = jnp.sum(ref[0].astype(jnp.float32), axis=0, keepdims=True)
            bias_ref[0] = sums + jnp.sum(ref[1].astype(jnp.float32), axis=0, keepdims=True)
            for part in range(2):
                share = dot_nt(ref[part], weight_ref[...])

                @pl.when(step == 0)
                def _():
                    total_ref[part] = share

                @pl.when(step > 0)
                def _():
                    total_ref[part] += share

        pl.when(step < 2)(lambda: add(low_ref))
        pl.when(step >= 2)(lambda: add(high_ref))

        @pl.when(step == DEPTH - 1)
        def _():
            near_ref[...] = total_ref[0]
            across_ref[...] = total_ref[1].astype(jnp.bfloat16)

    own_specs, far_specs = head_specs(width, chips)
    out = [shape_of(rows, width, dtype=jnp.float32), shape_of(rows, width)]
    return kernel_call(
        body,
        "token_shares",
        meta,
        tuple(grads) + (w_query, w_key, w_value) + tuple(chips),
        [
            pl.BlockSpec((2, rows, group), lambda g, m: (0, 0, jnp.minimum(g, 1))),
            pl.BlockSpec((2, rows, group), lambda g, m: (0, 0, jnp.maximum(g - 2, 0))),
        ]
        + own_specs
        + far_specs,
        out + [shape_of(DEPTH, 1, group, dtype=jnp.float32)],
        [whole(o) for o in out] + [pl.BlockSpec((1, 1, group), lambda g, m: (g, 0, 0))],
        grid=(DEPTH,),
        scratch=[pltpu.VMEM((width, group), jnp.bfloat16), pltpu.VMEM((2, rows, width), jnp.float32)],
    )


def token_gradient(meta, near, got, tokens, dh, vectors):
    rows, width = tokens.shape

    def body(meta_ref, near_ref, got_ref, tokens_ref, dh_ref, vec_ref, out_ref, sum_ref):
        grad = near_ref[...] + got_ref[...].astype(jnp.float32)
        unit, inverse = normalized(tokens_ref[...].astype(jnp.float32))
        sum_ref[0:1, :] = jnp.sum(grad * unit, axis=0, keepdims=True)
        sum_ref[1:2, :] = jnp.sum(grad, axis=0, keepdims=True)
        out_ref[...] = dh_ref[...] + norm_gradient(unit, inverse, vec_ref[GAIN_ONE : GAIN_ONE + 1], grad)

    args = (near, got, tokens, dh, vectors)
    out = [shape_of(rows, width, dtype=jnp.float32), shape_of(2, width, dtype=jnp.float32)]
    return kernel_call(body, "token_gradient", meta, args, [whole(a) for a in args], out, [whole(o) for o in out])


def layer_result(meta, downs, hidden, cotangent, vectors):
    rows, width = hidden.shape

    def body(meta_ref, *refs):
        down_refs, (hidden_ref, cot_ref, vec_ref, out_ref, sum_ref) = refs[: len(downs)], refs[len(downs) :]
        branch = sum(ref[...].astype(jnp.float32) for ref in down_refs) + vec_ref[BIAS_DOWN : BIAS_DOWN + 1]
        valid = valid_column(meta_ref, rows)
        out_ref[...] = valid * (hidden_ref[...] + vec_ref[SCALE_MLP : SCALE_MLP + 1] * branch)
        sum_ref[...] = jnp.sum(valid * cot_ref[...].astype(jnp.float32) * branch, axis=0, keepdims=True)

    args = tuple(downs) + (hidden, cotangent, vectors)
    out = [shape_of(rows, width, dtype=jnp.float32), shape_of(1, width, dtype=jnp.float32)]
    return kernel_call(body, "layer_result", meta, args, [whole(a) for a in args], out, [whole(o) for o in out])


def finish(meta, mine, other, kinds, name):
    width = CHIPS * QUARTER

    def body(meta_ref, mine_ref, other_ref, *outs):
        core = meta_ref[OWN_CORE]
        for ref, half in ((mine_ref, core), (other_ref, 1 - core)):
            at = 0
            for out_ref, (units, turned) in zip(outs, kinds):
                values = ref[0, :, at : at + units].astype(jnp.float32)
                place = pl.ds(pl.multiple_of(half * units, units), units)
                if turned:
                    out_ref[place, :] = values.T
                else:
                    out_ref[:, place] = values
                at += units

    side = pl.BlockSpec((1,) + mine.shape[1:], lambda j, m: (j, 0, 0))
    out, specs = [], []
    for units, turned in kinds:
        shape = (2 * units, width) if turned else (width, 2 * units)
        block = (2 * units, QUARTER) if turned else (QUARTER, 2 * units)
        out.append(shape_of(*shape, dtype=jnp.float32))
        specs.append(pl.BlockSpec(block, (lambda j, m: (0, m[j])) if turned else (lambda j, m: (m[j], 0))))
    return kernel_call(body, name, meta, (mine, other), [side, side], out, specs, grid=(CHIPS,))


def local_paired(
    tokens,
    slide_tiles,
    norm1_gain,
    norm1_bias,
    w_query,
    b_query,
    w_key,
    w_value,
    b_value,
    w_out,
    b_out,
    scale_attn,
    norm2_gain,
    norm2_bias,
    w_up,
    b_up,
    w_down,
    b_down,
    scale_mlp,
    cotangent,
):
    row_count, width = tokens.shape
    half_u = w_up.shape[1] // 2
    here = lax.axis_index("dp")
    level = lax.axis_index("mp")
    crops_here = row_count // L
    per_slide = CROPS_DEV // SLIDES_DEV
    crop = level * crops_here + jnp.arange(crops_here, dtype=jnp.int32)
    owner = (crop // per_slide)[:, None] == jnp.arange(SLIDES_DEV, dtype=jnp.int32)[None, :]
    limit = jnp.sum(jnp.where(owner, slide_tiles[None, :], 0), axis=1)
    valid = (crop % per_slide < limit).astype(jnp.int32)
    core = here & 1
    sides = jnp.stack([(here >> 1) ^ side for side in range(CHIPS)] + [core]).astype(jnp.int32)
    meta = jnp.concatenate([sides, valid])
    biases = jnp.concatenate([b_query, b_value, b_up]).reshape(-1, BLOCK)
    vectors = jnp.stack([norm1_gain, norm1_bias, norm2_gain, norm2_bias, scale_attn, scale_mlp, b_out, b_down])
    first, second = (X_SIDE, Y_SIDE), (Y_SIDE, X_SIDE)

    order = Order()

    tokens_other = swap_plane(tokens, CORE_SIDE)
    slice_attn, slice_rest = order(slice_weights, meta, w_query, w_key, w_value, w_out, w_up, w_down, biases)
    level_attn = [swap_depth(slice_attn, mask) for mask in (1, 2, 3)]
    one, one_other, grad, grad_b_down, one_turned, one_other_turned, grad_turned = order(
        prepare, meta, tokens, tokens_other, cotangent, vectors
    )
    level_attn = order.land(*level_attn)

    def stacked(low, high):
        return lambda *parts: jnp.concatenate([part[low:high] for part in parts], axis=0)

    far_attn = order(stacked(0, 3 * QUARTER), *level_attn)
    plane_attn = plane_swaps(far_attn)
    level_rest = swap_depth(order.hold(slice_rest), 2)
    grad_far = swap_depth(order.hold(grad), 1)
    far_out = order(stacked(3 * QUARTER, 4 * QUARTER), *level_attn)
    level_rest, grad_far, *plane_attn = order.land(level_rest, grad_far, *plane_attn)
    chips_attn = [far_attn] + plane_attn
    far_out, grad, grad_far = order.hold((far_out, grad, grad_far))
    plane_out = plane_swaps(far_out)
    grad_other = swap_plane(grad, CORE_SIDE)
    grad_far_other = swap_plane(grad_far, CORE_SIDE)
    qkv, attended, probs = order(
        attention_forward, meta, one, one_other, w_query, w_key, w_value, biases, level_attn, chips_attn
    )
    grad_other, grad_far_other, *plane_out = order.land(grad_other, grad_far_other, *plane_out)
    chips_out = [far_out] + plane_out
    plane_rest = plane_swaps(order.hold(level_rest))
    out_near, *out_across = order(attention_out, meta, attended, w_out, chips_out)
    out_got = [swap_plane(part, CORE_SIDE) for part in out_across]
    grads_turned = [grad_turned] + list(order(turn, meta, grad_other, grad_far, grad_far_other))
    hidden, branch, normed = order(attention_norm, meta, out_near, *out_got, tokens, vectors)
    normed_far = swap_depth(normed, 1)

    plane_rest = order.land(*plane_rest)
    chips_rest = [level_rest] + plane_rest
    normed_other = swap_plane(order.hold(normed), CORE_SIDE)
    pair_rows = level_attn[1][4 * QUARTER :].astype(jnp.float32)
    n_u = half_u // BLOCK
    pair_bias = (pair_rows[2 : 2 + n_u] + pair_rows[4 + n_u : 4 + 2 * n_u]).reshape(-1)
    bias_up = jnp.concatenate([lax.dynamic_slice_in_dim(b_up, core * half_u, half_u), pair_bias])[None, :]
    near = order(
        feed_forward, meta, (normed, normed_other), (grad, grad_other), w_up, w_down, bias_up, chips_rest, 10**12
    )
    (normed_far,) = order.land(normed_far)
    normed_far_other = swap_plane(order.hold(normed_far), CORE_SIDE)
    far = order(feed_forward, meta, (normed_far,), (grad_far,), w_up, w_down, bias_up, chips_rest)
    far_other = order(
        feed_forward, meta, (normed_far_other,), (grad_far_other,), w_up, w_down, bias_up, chips_rest
    )
    acts, gups, backs = [list(a) + list(b) + list(c) for a, b, c in zip(near[:3], far[:3], far_other[:3])]
    grad_b_up = near[3] + far[3] + far_other[3]
    (back_got,) = order.land(swap_plane(backs[3], CORE_SIDE))
    back_far = order(add_low, backs[2], back_got)
    back_far, back_near = order.hold((back_far, backs[1]))
    back_far = swap_depth(back_far, 1)
    back_near = swap_plane(back_near, CORE_SIDE)
    kept_own, sent_own, kept_pair, sent_pair = order(
        feed_gradients, meta, (normed, normed_other, normed_far, normed_far_other), grads_turned, gups, acts
    )
    downs = order(feed_down, meta, acts, w_down, chips_rest)
    back_far, back_near = order.land(back_far, back_near)
    sent_own, sent_pair, down_near, down_far = order.hold((sent_own, sent_pair, downs[1], downs[3]))
    rest_got = [swap_plane(sent, side) for sent, side in zip((sent_own, sent_pair), first)]
    down_near = swap_plane(down_near, CORE_SIDE)
    down_far = swap_plane(down_far, CORE_SIDE)
    dh, e1, sums_two = order(
        hidden_gradient, meta, (backs[0], back_near, back_far), hidden, branch, cotangent, vectors
    )
    e1_other = swap_plane(e1, CORE_SIDE)
    down_near, down_far = order.land(down_near, down_far)
    down_far = swap_depth(order(add_low, downs[2], down_far), 1)
    low_qkv, low_kept, low_sent = order(
        attention_backward, meta, qkv, probs, attended, (e1, e1_other), (one_turned, one_other_turned), w_out, chips_out, 0
    )
    rest_got = order.land(*rest_got)

    def add_sent(kept, got):
        return add_low(kept[QUARTER:], got[QUARTER:])

    def add_kept(kept, got, last):
        return add_low(kept[:QUARTER], got[:QUARTER], last)

    rest_kept = (kept_own, kept_pair)
    rest_sent = [order(add_sent, kept, got) for kept, got in zip(rest_kept, rest_got)]
    rest_last = [swap_plane(sent, side) for sent, side in zip(order.hold(rest_sent), second)]
    high_qkv, high_kept, high_sent = order(
        attention_backward, meta, qkv, probs, attended, (e1, e1_other), (one_turned, one_other_turned), w_out, chips_out, 1
    )
    *rest_last, down_far = order.land(*rest_last, down_far)
    rest_own, rest_pair = [order(add_kept, *parts) for parts in zip(rest_kept, rest_got, rest_last)]
    low_sent, high_sent, rest_pair = order.hold((low_sent, high_sent, rest_pair))
    attn_got = [swap_plane(sent, side) for sent, side in zip((low_sent, high_sent), first)]
    rest_pair = swap_depth(rest_pair, 2)
    one_near, one_across, sums_qkv = order(
        token_shares, meta, (low_qkv, high_qkv), w_query, w_key, w_value, chips_attn
    )
    one_got = swap_plane(one_across, CORE_SIDE)
    layer_out, grad_scale_mlp = order(
        layer_result, meta, (downs[0], down_near, down_far), hidden, cotangent, vectors
    )
    grad_tokens, sums_one = order(token_gradient, meta, one_near, one_got, tokens, dh, vectors)
    *attn_got, rest_pair = order.land(*attn_got, rest_pair)
    attn_kept = (low_kept, high_kept)
    attn_sent = [order(add_sent, kept, got) for kept, got in zip(attn_kept, attn_got)]
    attn_last = [swap_plane(sent, side) for sent, side in zip(order.hold(attn_sent), second)]
    grad_rest = order(add_low, rest_own, rest_pair)

    def gather_small(sums_qkv, grad_b_up, *small):
        sums_qkv = sums_qkv.reshape(DEPTH, 3, BLOCK)
        nothing = jnp.zeros((1, half_u), jnp.float32)
        sums_up = jnp.concatenate([grad_b_up[:, :half_u], nothing, grad_b_up[:, half_u:], nothing], axis=0)
        shared = jnp.concatenate([sums_qkv[:, 0], sums_qkv[:, 2], sums_up], axis=1)
        shared = jnp.concatenate(
            [lax.dynamic_slice_in_dim(shared, level ^ index, 1, 0) for index in range(DEPTH)]
        ).reshape(1, -1, BLOCK)
        shared = jnp.concatenate([jnp.where(core == half, shared, 0.0) for half in range(2)])
        return jnp.concatenate([value.reshape(-1, BLOCK) for value in small] + [shared.reshape(-1, BLOCK)])

    totals = order(gather_small, sums_qkv, grad_b_up, sums_one, sums_two, grad_scale_mlp, grad_b_down)
    totals_got = swap_plane(totals, X_SIDE)
    *attn_last, totals_got = order.land(*attn_last, totals_got)
    totals = order(jnp.add, totals, totals_got)
    low, high = [order(add_kept, *parts) for parts in zip(attn_kept, attn_got, attn_last)]
    wide = 4 * BLOCK
    level_sent = order(lambda low, high: jnp.stack([low[:, wide:], high[:, wide:]]), low, high)
    totals, grad_rest, level_sent = order.hold((totals, grad_rest, level_sent))
    level_got = swap_depth(level_sent, 1)
    rest_x, rest_y = swap_plane(grad_rest, X_SIDE), swap_plane(grad_rest, Y_SIDE)
    totals_got = swap_plane(totals, Y_SIDE)
    level_got, rest_x, rest_y, totals_got = order.land(level_got, rest_x, rest_y, totals_got)
    totals = order(jnp.add, totals, totals_got)
    level_kept, level_sent = order(
        lambda low, high, got: (add_low(low[:, :wide], got[0]), add_low(high[:, :wide], got[1])), low, high, level_got
    )
    totals, grad_rest, level_sent = order.hold((totals, grad_rest, level_sent))
    level_got = swap_depth(level_sent, 2)
    rest_corner = swap_plane(grad_rest, X_SIDE | Y_SIDE)
    totals_got = swap_depth(totals, 1)
    level_got, rest_corner, totals_got = order.land(level_got, rest_corner, totals_got)
    grad_attn = order(add_low, level_kept, level_got)
    totals = order(jnp.add, totals, totals_got)
    rest_mine = order(lambda *parts: jnp.stack(parts), grad_rest, rest_x, rest_y, rest_corner)
    totals, grad_attn, rest_mine = order.hold((totals, grad_attn, rest_mine))
    plane_attn = plane_swaps(grad_attn)
    rest_other = swap_plane(rest_mine, CORE_SIDE)
    totals_got = swap_depth(totals, 2)
    full_grad_up, full_grad_down = order(
        finish, meta, rest_mine, rest_other, ((half_u, False), (half_u, True)), "finish_rest"
    )
    *plane_attn, totals_got = order.land(*plane_attn, totals_got)
    attn_mine = order(lambda *parts: jnp.stack(parts), grad_attn, *plane_attn)
    totals = order(jnp.add, totals, totals_got)
    totals, attn_mine = order.hold((totals, attn_mine))
    attn_other = swap_plane(attn_mine, CORE_SIDE)
    totals_got = swap_plane(totals, CORE_SIDE)
    full_grad_q, full_grad_k, full_grad_v, full_grad_o = order(
        finish, meta, attn_mine, attn_other, ((BLOCK, False),) * 3 + ((BLOCK, True),), "finish_attn"
    )
    totals = order(jnp.add, totals, totals_got)
    lines = width // BLOCK
    small_total = totals[: 8 * lines].reshape(8, width)
    shared_total = totals[8 * lines :].reshape(2, DEPTH, -1)
    shared_total = lax.dynamic_index_in_dim(shared_total, level, 1, keepdims=False)
    return (
        layer_out,
        grad_tokens,
        small_total[0],
        small_total[1],
        full_grad_q,
        shared_total[:, :BLOCK].reshape(-1),
        full_grad_k,
        full_grad_v,
        shared_total[:, BLOCK : 2 * BLOCK].reshape(-1),
        full_grad_o,
        small_total[5],
        small_total[4],
        small_total[2],
        small_total[3],
        full_grad_up,
        shared_total[:, 2 * BLOCK :].reshape(-1),
        full_grad_down,
        small_total[7],
        small_total[6],
    )


def local_general(
    tokens,
    slide_tiles,
    norm1_gain,
    norm1_bias,
    w_query,
    b_query,
    w_key,
    w_value,
    b_value,
    w_out,
    b_out,
    scale_attn,
    norm2_gain,
    norm2_bias,
    w_up,
    b_up,
    w_down,
    b_down,
    scale_mlp,
    cotangent,
):
    row_count = tokens.shape[0]
    per_slide = CROPS_DEV // SLIDES_DEV
    crop_index = (lax.axis_index("mp") * row_count + jnp.arange(row_count, dtype=jnp.int32)) // L
    slide_index = crop_index // per_slide
    owner = slide_index[:, None] == jnp.arange(SLIDES_DEV, dtype=jnp.int32)[None, :]
    limit_rows = jnp.sum(jnp.where(owner, slide_tiles[None, :], 0), axis=1)
    valid_rows = (crop_index % per_slide < limit_rows).astype(jnp.float32)[:, None]
    inputs = tokens.astype(jnp.float32)
    normed_one = layer_norm(inputs, norm1_gain, norm1_bias).astype(jnp.bfloat16)
    rows_one = lax.all_gather(normed_one, "mp", axis=0, tiled=True)
    queries = (jnp.dot(rows_one, w_query, preferred_element_type=jnp.float32) + b_query).astype(
        jnp.bfloat16
    )
    keys_all = jnp.dot(rows_one, w_key, preferred_element_type=jnp.float32).astype(jnp.bfloat16)
    values_all = (jnp.dot(rows_one, w_value, preferred_element_type=jnp.float32) + b_value).astype(
        jnp.bfloat16
    )
    heads_here = w_query.shape[1] // DH
    query_heads = to_heads(queries, heads_here)
    key_heads = to_heads(keys_all, heads_here)
    value_heads = to_heads(values_all, heads_here)
    scores = attn_scores(query_heads, key_heads)
    top_score = jnp.max(scores, axis=-1, keepdims=True)
    log_total = top_score + jnp.log(jnp.sum(jnp.exp(scores - top_score), axis=-1, keepdims=True))
    weights_low = jnp.exp(scores - log_total).astype(jnp.bfloat16)
    mixed_heads = jnp.einsum(
        "chqk,ckhd->cqhd", weights_low, value_heads, preferred_element_type=jnp.float32
    )
    attended = mixed_heads.reshape(queries.shape).astype(jnp.bfloat16)
    attn_sum = lax.psum_scatter(
        jnp.dot(attended, w_out, preferred_element_type=jnp.float32).astype(jnp.bfloat16),
        "mp",
        scatter_dimension=0,
        tiled=True,
    ).astype(jnp.float32)
    branch_one = attn_sum + b_out
    hidden_state = inputs + scale_attn * branch_one
    normed_two = layer_norm(hidden_state, norm2_gain, norm2_bias).astype(jnp.bfloat16)
    rows_two = lax.all_gather(normed_two, "mp", axis=0, tiled=True)
    up_pre = jnp.dot(rows_two, w_up, preferred_element_type=jnp.float32) + b_up
    activated = gelu_exact(up_pre).astype(jnp.bfloat16)
    down_sum = lax.psum_scatter(
        jnp.dot(activated, w_down, preferred_element_type=jnp.float32).astype(jnp.bfloat16),
        "mp",
        scatter_dimension=0,
        tiled=True,
    ).astype(jnp.float32)
    branch_two = down_sum + b_down
    layer_out = valid_rows * (hidden_state + scale_mlp * branch_two)
    grad_out = valid_rows * cotangent.astype(jnp.float32)
    grad_scale_mlp = jnp.sum(grad_out * branch_two, axis=0)
    grad_branch_two = scale_mlp * grad_out
    grad_b_down = jnp.sum(grad_branch_two, axis=0)
    grad_down_low = grad_branch_two.astype(jnp.bfloat16)
    gelu_value, gelu_back = jax.vjp(gelu_exact, up_pre)
    grad_down_rows = lax.all_gather(grad_down_low, "mp", axis=0, tiled=True)
    grad_act = contract_cols(grad_down_rows, w_down)
    grad_up = gelu_back(grad_act)[0].astype(jnp.bfloat16)
    grad_w_up = contract_rows(rows_two, grad_up)
    grad_w_down = contract_rows(activated, grad_down_rows)
    grad_b_up = jnp.sum(grad_up.astype(jnp.float32), axis=0)
    grad_rows_two = lax.psum_scatter(
        contract_cols(grad_up, w_up).astype(jnp.bfloat16), "mp", scatter_dimension=0, tiled=True
    ).astype(jnp.float32)
    norm2_value, norm2_back = jax.vjp(layer_norm, hidden_state, norm2_gain, norm2_bias)
    grad_hidden_norm, grad_norm2_gain, grad_norm2_bias = norm2_back(grad_rows_two)
    grad_hidden = grad_out + grad_hidden_norm
    grad_scale_attn = jnp.sum(grad_hidden * branch_one, axis=0)
    grad_branch_one = scale_attn * grad_hidden
    grad_b_out = jnp.sum(grad_branch_one, axis=0)
    grad_attn_low = grad_branch_one.astype(jnp.bfloat16)
    grad_attn_rows = lax.all_gather(grad_attn_low, "mp", axis=0, tiled=True)
    grad_w_out = contract_rows(attended, grad_attn_rows)
    grad_mixed = contract_cols(grad_attn_rows, w_out).astype(jnp.bfloat16)
    grad_mixed_heads = to_heads(grad_mixed, heads_here)
    scores_again = attn_scores(query_heads, key_heads)
    probs = jnp.exp(scores_again - log_total)
    probs_low = probs.astype(jnp.bfloat16)
    grad_value_heads = jnp.einsum(
        "chqk,cqhd->ckhd", probs_low, grad_mixed_heads, preferred_element_type=jnp.float32
    )
    grad_values = grad_value_heads.reshape(queries.shape).astype(jnp.bfloat16)
    grad_probs = jnp.einsum(
        "cqhd,ckhd->chqk", grad_mixed_heads, value_heads, preferred_element_type=jnp.float32
    )
    row_inner = jnp.sum(probs * grad_probs, axis=-1, keepdims=True)
    grad_scores = (probs * (grad_probs - row_inner)).astype(jnp.bfloat16)
    inverse_root = 1.0 / math.sqrt(DH)
    grad_query_heads = jnp.einsum(
        "chqk,ckhd->cqhd", grad_scores, key_heads, preferred_element_type=jnp.float32
    )
    grad_queries = (inverse_root * grad_query_heads).reshape(queries.shape).astype(jnp.bfloat16)
    grad_key_heads = jnp.einsum(
        "chqk,cqhd->ckhd", grad_scores, query_heads, preferred_element_type=jnp.float32
    )
    grad_keys = (inverse_root * grad_key_heads).reshape(queries.shape).astype(jnp.bfloat16)
    grad_w_query = contract_rows(rows_one, grad_queries)
    grad_b_query = jnp.sum(grad_queries.astype(jnp.float32), axis=0)
    grad_w_key = contract_rows(rows_one, grad_keys)
    grad_w_value = contract_rows(rows_one, grad_values)
    grad_b_value = jnp.sum(grad_values.astype(jnp.float32), axis=0)
    grad_rows_one = lax.psum_scatter(
        (
            contract_cols(grad_queries, w_query)
            + contract_cols(grad_keys, w_key)
            + contract_cols(grad_values, w_value)
        ).astype(jnp.bfloat16),
        "mp",
        scatter_dimension=0,
        tiled=True,
    ).astype(jnp.float32)
    norm1_value, norm1_back = jax.vjp(layer_norm, inputs, norm1_gain, norm1_bias)
    grad_in_norm, grad_norm1_gain, grad_norm1_bias = norm1_back(grad_rows_one)
    grad_tokens = grad_hidden + grad_in_norm
    small_stack = jnp.stack(
        [
            grad_norm1_gain,
            grad_norm1_bias,
            grad_norm2_gain,
            grad_norm2_bias,
            grad_scale_attn,
            grad_scale_mlp,
            grad_b_out,
            grad_b_down,
        ],
        axis=1,
    )
    small_total = lax.psum(small_stack.astype(jnp.bfloat16), "mp")
    (
        share_wq,
        share_bq,
        share_wk,
        share_wv,
        share_bv,
        share_wo,
        share_up,
        share_bup,
        share_down,
        share_small,
    ) = (
        lax.psum_scatter(
            grad_w_query.astype(jnp.bfloat16), "dp", scatter_dimension=0, tiled=True
        ).astype(jnp.float32),
        lax.psum_scatter(
            grad_b_query.astype(jnp.bfloat16), "dp", scatter_dimension=0, tiled=True
        ).astype(jnp.float32),
        lax.psum_scatter(
            grad_w_key.astype(jnp.bfloat16), "dp", scatter_dimension=0, tiled=True
        ).astype(jnp.float32),
        lax.psum_scatter(
            grad_w_value.astype(jnp.bfloat16), "dp", scatter_dimension=0, tiled=True
        ).astype(jnp.float32),
        lax.psum_scatter(
            grad_b_value.astype(jnp.bfloat16), "dp", scatter_dimension=0, tiled=True
        ).astype(jnp.float32),
        lax.psum_scatter(
            grad_w_out.astype(jnp.bfloat16), "dp", scatter_dimension=0, tiled=True
        ).astype(jnp.float32),
        lax.psum_scatter(
            grad_w_up.astype(jnp.bfloat16), "dp", scatter_dimension=0, tiled=True
        ).astype(jnp.float32),
        lax.psum_scatter(
            grad_b_up.astype(jnp.bfloat16), "dp", scatter_dimension=0, tiled=True
        ).astype(jnp.float32),
        lax.psum_scatter(
            grad_w_down.astype(jnp.bfloat16), "dp", scatter_dimension=0, tiled=True
        ).astype(jnp.float32),
        lax.psum_scatter(small_total, "dp", scatter_dimension=0, tiled=True).astype(jnp.float32),
    )
    (
        full_wq,
        full_bq,
        full_wk,
        full_wv,
        full_bv,
        full_wo,
        full_up,
        full_bup,
        full_down,
        full_small,
    ) = (
        lax.all_gather(share_wq.astype(jnp.bfloat16), "dp", axis=0, tiled=True).astype(
            share_wq.dtype
        ),
        lax.all_gather(share_bq.astype(jnp.bfloat16), "dp", axis=0, tiled=True).astype(
            share_bq.dtype
        ),
        lax.all_gather(share_wk.astype(jnp.bfloat16), "dp", axis=0, tiled=True).astype(
            share_wk.dtype
        ),
        lax.all_gather(share_wv.astype(jnp.bfloat16), "dp", axis=0, tiled=True).astype(
            share_wv.dtype
        ),
        lax.all_gather(share_bv.astype(jnp.bfloat16), "dp", axis=0, tiled=True).astype(
            share_bv.dtype
        ),
        lax.all_gather(share_wo.astype(jnp.bfloat16), "dp", axis=0, tiled=True).astype(
            share_wo.dtype
        ),
        lax.all_gather(share_up.astype(jnp.bfloat16), "dp", axis=0, tiled=True).astype(
            share_up.dtype
        ),
        lax.all_gather(share_bup.astype(jnp.bfloat16), "dp", axis=0, tiled=True).astype(
            share_bup.dtype
        ),
        lax.all_gather(share_down.astype(jnp.bfloat16), "dp", axis=0, tiled=True).astype(
            share_down.dtype
        ),
        lax.all_gather(share_small.astype(jnp.bfloat16), "dp", axis=0, tiled=True).astype(
            share_small.dtype
        ),
    )
    return (
        layer_out,
        grad_tokens,
        full_small[:, 0],
        full_small[:, 1],
        full_wq,
        full_bq,
        full_wk,
        full_wv,
        full_bv,
        full_wo,
        full_small[:, 6],
        full_small[:, 4],
        full_small[:, 2],
        full_small[:, 3],
        full_up,
        full_bup,
        full_down,
        full_small[:, 7],
        full_small[:, 5],
    )


def solution(mesh):
    in_specs = (
        P(("dp", "mp"), None),
        P("dp"),
        P(),
        P(),
        P(None, "mp"),
        P("mp"),
        P(None, "mp"),
        P(None, "mp"),
        P("mp"),
        P("mp", None),
        P(),
        P(),
        P(),
        P(),
        P(None, "mp"),
        P("mp"),
        P("mp", None),
        P(),
        P(),
        P(("dp", "mp"), None),
    )
    out_specs = (
        P(("dp", "mp"), None),
        P(("dp", "mp"), None),
        P(),
        P(),
        P(None, "mp"),
        P("mp"),
        P(None, "mp"),
        P(None, "mp"),
        P("mp"),
        P("mp", None),
        P(),
        P(),
        P(),
        P(),
        P(None, "mp"),
        P("mp"),
        P("mp", None),
        P(),
        P(),
    )
    paired = mesh.shape["dp"] == 8 and mesh.shape["mp"] == 4
    local = local_paired if paired else local_general
    return jax.shard_map(local, mesh=mesh, in_specs=in_specs, out_specs=out_specs, check_vma=False)
```

```python
import functools
import math

import jax
import jax.numpy as jnp
from jax import lax
from jax.experimental import pallas as pl
from jax.experimental.pallas import tpu as pltpu
from jax.sharding import PartitionSpec as P

DH = 64
L = 197
SLIDES_DEV = 2
CROPS_DEV = 8


def layer_norm(values, gain, shift):
    average = jnp.mean(values, axis=-1, keepdims=True)
    centered = values - average
    spread = jnp.mean(centered * centered, axis=-1, keepdims=True)
    return centered * lax.rsqrt(spread + 1e-06) * gain + shift


def gelu_exact(values):
    return jax.nn.gelu(values, approximate=False)


def contract_rows(left, right):
    return lax.dot_general(
        left, right, (((0,), (0,)), ((), ())), preferred_element_type=jnp.float32
    )


def contract_cols(left, right):
    return lax.dot_general(
        left, right, (((1,), (1,)), ((), ())), preferred_element_type=jnp.float32
    )


def to_heads(matrix, heads_here):
    return matrix.reshape(matrix.shape[0] // L, L, heads_here, DH)


def attn_scores(query_heads, key_heads):
    product = jnp.einsum(
        "cqhd,ckhd->chqk", query_heads, key_heads, preferred_element_type=jnp.float32
    )
    return product * (1.0 / math.sqrt(DH))


BLOCK = 128
QUARTER = 256
X_SIDE, Y_SIDE, CORE_SIDE = 2, 4, 1
PLANE = 8
CHIPS = 4
DEPTH = 4
OWN_CORE = CHIPS
FLAGS = CHIPS + 1
GAIN_ONE, SHIFT_ONE, GAIN_TWO, SHIFT_TWO, SCALE_ATTN, SCALE_MLP, BIAS_OUT, BIAS_DOWN = range(8)
VMEM_BYTES = 24 * 2**20
NEAR_BYTES = 28 * 2**20
PARTS_BYTES = 24 * 2**20
PIECES_BYTES = 60 * 2**20


def swap_plane(values, mask):
    return lax.ppermute(values, "dp", [(i, i ^ mask) for i in range(PLANE)])


def swap_depth(values, mask):
    return lax.ppermute(values, "mp", [(i, i ^ mask) for i in range(DEPTH)])


def plane_swaps(values):
    return [swap_plane(values, side) for side in (X_SIDE, Y_SIDE, X_SIDE | Y_SIDE)]


class Order:
    def __init__(self, meta):
        self.meta = meta

    def hold(self, values):
        leaves, tree = jax.tree.flatten(values)
        *leaves, self.meta = lax.optimization_barrier(tuple(leaves) + (self.meta,))
        return jax.tree.unflatten(tree, leaves)

    def land(self, *arrays):
        return self.hold(list(arrays))

    def __call__(self, step, *args):
        return self.hold(step(self.meta, *args))

    def plain(self, step, *args):
        return self.hold(step(*self.hold(args)))


def dot_nt(left, right):
    return lax.dot_general(left, right, (((1,), (1,)), ((), ())), preferred_element_type=jnp.float32)


def dot_tn(left, right):
    return lax.dot_general(left, right, (((0,), (0,)), ((), ())), preferred_element_type=jnp.float32)


def dot_nn(left, right):
    return lax.dot_general(left, right, (((1,), (0,)), ((), ())), preferred_element_type=jnp.float32)


def add_low(*values):
    return sum(value.astype(jnp.float32) for value in values).astype(jnp.bfloat16)


def crop_ranges(rows):
    ranges = []
    for crop in range(rows // L):
        low = crop * L // 16 * 16
        high = min((crop + 1) * L + 15, rows + 15) // 16 * 16
        ranges.append((low, min(high, rows), crop * L - low))
    return ranges


def add_parts(meta, *sums):
    rows = [len(parts) for parts in sums]
    flat = [part for parts in sums for part in parts]
    heights = [min(array.shape[0] - start for array, start in parts) for parts in sums]

    def body(meta_ref, *refs):
        at = 0
        for count, out_ref in zip(rows, refs[len(flat) :]):
            out_ref[...] = add_low(*[ref[...] for ref in refs[at : at + count]])
            at += count

    in_specs, out = [], []
    for parts, height in zip(sums, heights):
        for array, start in parts:
            in_specs.append(pl.BlockSpec((height, array.shape[1]), lambda i, m, b=start // height: (b, 0)))
        out.append(shape_of(height, parts[0][0].shape[1]))
    return kernel_call(
        body, "add_parts", meta, [array for array, _ in flat], in_specs, out, [whole(o) for o in out], vmem=PARTS_BYTES
    )


def level_pieces(meta, kept, got, last):
    half = kept[0].shape[1] // 2

    def body(meta_ref, *refs):
        own_ref, pair_ref, send_ref = refs[6:]
        for lane, near_ref in enumerate((own_ref, pair_ref)):
            total = add_low(*[ref[...] for ref in refs[3 * lane : 3 * lane + 3]])
            near_ref[...] = total[:, :half]
            send_ref[lane] = total[:, half:]

    first = pl.BlockSpec((QUARTER, 2 * half), lambda i, m: (0, 0))
    args = [array for triple in zip(kept, got, last) for array in triple]
    out = [shape_of(QUARTER, half)] * 2 + [shape_of(2, QUARTER, half)]
    return kernel_call(
        body, "level_pieces", meta, args, [first] * 6, out, [whole(o) for o in out], vmem=PIECES_BYTES
    )


def whole(array):
    zeros = (0,) * array.ndim
    return pl.BlockSpec(array.shape, lambda *_: zeros)


def kernel_call(body, name, meta, args, in_specs, out_shape, out_specs, grid=(1,), scratch=(), flops=1000, vmem=VMEM_BYTES):
    return pl.pallas_call(
        body,
        grid_spec=pltpu.PrefetchScalarGridSpec(
            num_scalar_prefetch=1,
            grid=grid,
            in_specs=in_specs,
            out_specs=out_specs,
            scratch_shapes=list(scratch),
        ),
        out_shape=out_shape,
        compiler_params=pltpu.CompilerParams(vmem_limit_bytes=vmem),
        cost_estimate=pl.CostEstimate(flops=flops, bytes_accessed=1000, transcendentals=0),
        name=name,
    )(meta, *args)


def shape_of(*dims, dtype=jnp.bfloat16):
    return jax.ShapeDtypeStruct(dims, dtype)


def normalized(values):
    centered = values - jnp.mean(values, axis=-1, keepdims=True)
    inverse = lax.rsqrt(jnp.mean(centered * centered, axis=-1, keepdims=True) + 1e-06)
    return centered * inverse, inverse


def norm_gradient(unit, inverse, gain, grad):
    wide = grad * gain
    return inverse * (
        wide - jnp.mean(wide, axis=-1, keepdims=True) - unit * jnp.mean(wide * unit, axis=-1, keepdims=True)
    )


def valid_column(meta_ref, rows):
    row = lax.broadcasted_iota(jnp.int32, (rows, 1), 0)
    valid = jnp.zeros((rows, 1), jnp.float32)
    for crop in range(rows // L):
        inside = (row >= crop * L) & (row < (crop + 1) * L)
        valid = jnp.where(inside, meta_ref[FLAGS + crop].astype(jnp.float32), valid)
    return valid


def quarter_of(meta_ref, side):
    return pl.ds(pl.multiple_of(meta_ref[side] * QUARTER, QUARTER), QUARTER)


def slice_weights(meta, w_query, w_key, w_value, w_out, w_up, w_down, b_query, b_value, b_up):
    half_h, half_u = w_query.shape[1] // 2, w_up.shape[1] // 2
    n_h, n_u = half_h // BLOCK, half_u // BLOCK

    def body(meta_ref, q_ref, k_ref, v_ref, o_ref, up_ref, down_ref, bq_ref, bv_ref, bu_ref, attn_ref, rest_ref):
        core = meta_ref[OWN_CORE]
        for which, ref in enumerate((q_ref, k_ref, v_ref)):
            attn_ref[which * QUARTER : (which + 1) * QUARTER, :] = ref[...]
        for b in range(2):
            row = 3 * QUARTER + b * half_h
            attn_ref[row : row + half_h, :] = o_ref[:, b * BLOCK : (b + 1) * BLOCK]
        picked = jnp.concatenate(
            [
                bq_ref[pl.ds(core * n_h, n_h), :],
                bv_ref[pl.ds(core * n_h, n_h), :],
                bu_ref[pl.ds(core * n_u, n_u), :],
            ],
            axis=0,
        )
        high = picked.astype(jnp.bfloat16)
        low = (picked - high.astype(jnp.float32)).astype(jnp.bfloat16)
        spare = jnp.zeros((16 - 2 * picked.shape[0], BLOCK), jnp.bfloat16)
        attn_ref[4 * QUARTER :, :] = jnp.concatenate([high, low, spare], axis=0)
        for b in range(n_u):
            rest_ref[b * QUARTER : (b + 1) * QUARTER, :] = up_ref[:, b * BLOCK : (b + 1) * BLOCK]
        for b in range(2):
            row = n_u * QUARTER + b * half_u
            rest_ref[row : row + half_u, :] = down_ref[:, b * BLOCK : (b + 1) * BLOCK]

    args = (w_query, w_key, w_value, w_out, w_up, w_down, b_query, b_value, b_up)
    out = [shape_of(4 * QUARTER + 16, BLOCK), shape_of(2 * n_u * QUARTER, BLOCK)]
    return kernel_call(
        body,
        "slice_weights",
        meta,
        args,
        [pl.BlockSpec((QUARTER, half_h), lambda i, m: (m[0], m[OWN_CORE]))] * 3
        + [
            pl.BlockSpec((half_h, QUARTER), lambda i, m: (m[OWN_CORE], m[0])),
            pl.BlockSpec((QUARTER, half_u), lambda i, m: (m[0], m[OWN_CORE])),
            pl.BlockSpec((half_u, QUARTER), lambda i, m: (m[OWN_CORE], m[0])),
            whole(b_query),
            whole(b_value),
            whole(b_up),
        ],
        out,
        [whole(o) for o in out],
        vmem=60 * 2**20,
    )


def turn_into(meta_ref, values, turned_ref, index=None):
    for side in range(CHIPS):
        rows = slice(side * QUARTER, (side + 1) * QUARTER)
        if index is None:
            turned_ref[rows, :] = values[:, quarter_of(meta_ref, side)].T
        else:
            turned_ref[rows, :] = values[index, :, quarter_of(meta_ref, side)].T


def turn(meta, *arrays):
    def body(meta_ref, *refs):
        for source, target in zip(refs[: len(arrays)], refs[len(arrays) :]):
            turn_into(meta_ref, source, target)

    out = [shape_of(*a.shape[::-1]) for a in arrays]
    return kernel_call(body, "turn", meta, arrays, [whole(a) for a in arrays], out, [whole(o) for o in out])


def prepare(meta, tokens, tokens_other, cotangent, vectors):
    rows, width = tokens.shape

    def body(meta_ref, tokens_ref, other_ref, cot_ref, vec_ref, one_ref, two_ref, grad_ref, sum_ref, *turned):
        for source, target in ((tokens_ref, one_ref), (other_ref, two_ref)):
            unit, _ = normalized(source[...].astype(jnp.float32))
            target[...] = (unit * vec_ref[GAIN_ONE : GAIN_ONE + 1] + vec_ref[SHIFT_ONE : SHIFT_ONE + 1]).astype(
                jnp.bfloat16
            )
        grad = vec_ref[SCALE_MLP : SCALE_MLP + 1] * (valid_column(meta_ref, rows) * cot_ref[...].astype(jnp.float32))
        sum_ref[...] = jnp.sum(grad, axis=0, keepdims=True)
        grad_ref[...] = grad.astype(jnp.bfloat16)
        for source, target in zip((one_ref, two_ref, grad_ref), turned):
            turn_into(meta_ref, source, target)

    args = (tokens, tokens_other, cotangent, vectors)
    out = [shape_of(rows, width)] * 3 + [shape_of(1, width, dtype=jnp.float32)] + [shape_of(width, rows)] * 3
    return kernel_call(body, "prepare", meta, args, [whole(a) for a in args], out, [whole(o) for o in out])


def fill_heads(meta_ref, chip_refs, weight_ref):
    for side, ref in enumerate(chip_refs):
        at = quarter_of(meta_ref, side)
        for which in range(3):
            weight_ref[at, which * BLOCK : (which + 1) * BLOCK] = ref[which * QUARTER : (which + 1) * QUARTER, :]


def head_specs(width, chips, base=0):
    own = [pl.BlockSpec((width, BLOCK), lambda g, m: (0, m[OWN_CORE]))] * 3
    far = [pl.BlockSpec((4 * QUARTER, BLOCK), lambda g, m: (jnp.maximum(base + g - 1, 0), 0))] * len(chips)
    return own, far


def attention_forward(meta, normed, other, w_query, w_key, w_value, b_query, b_value, level_attn, chips, w_count, lane):
    rows, width = normed.shape
    group = 3 * BLOCK
    ranges = crop_ranges(rows)
    span = max(high - low for low, high, _ in ranges)
    scale = 1.0 / math.sqrt(DH)
    count = 2 + w_count
    groups = DEPTH // 2
    base = lane * groups

    def body(meta_ref, normed_ref, other_ref, q_ref, k_ref, v_ref, bq_ref, bv_ref, one_ref, two_ref, three_ref, *refs):
        chip_refs, (qkv_ref, out_ref, prob_ref, weight_ref, sum_ref) = refs[:CHIPS], refs[CHIPS:]
        group_here = base + pl.program_id(0)
        core = meta_ref[OWN_CORE]

        @pl.when(group_here == 0)
        def _():
            for which, ref in enumerate((q_ref, k_ref, v_ref)):
                weight_ref[:, which * BLOCK : (which + 1) * BLOCK] = ref[...]
            sum_ref[0:1, :] = bq_ref[pl.ds(core, 1), :]
            sum_ref[1:2, :] = bv_ref[pl.ds(core, 1), :]

        for index, ref in enumerate((one_ref, two_ref, three_ref)):
            @pl.when(group_here == index + 1)
            def _():
                both = ref[...].astype(jnp.float32)
                sum_ref[0:2, :] = both[0:2] + both[count : count + 2]

        @pl.when(group_here > 0)
        def _():
            fill_heads(meta_ref, chip_refs, weight_ref)

        bias = jnp.concatenate([sum_ref[0:1, :], jnp.zeros((1, BLOCK), jnp.float32), sum_ref[1:2, :]], axis=1)
        for part, rows_ref in enumerate((normed_ref, other_ref)):
            qkv_ref[part] = (dot_nn(rows_ref[...], weight_ref[...]) + bias).astype(jnp.bfloat16)
        for part in range(2):
            for index, (low, high, skip) in enumerate(ranges):
                size = high - low
                query = qkv_ref[part, low:high, 0:BLOCK]
                key = qkv_ref[part, low:high, BLOCK : 2 * BLOCK]
                value = qkv_ref[part, low:high, 2 * BLOCK : 3 * BLOCK]
                lane = lax.broadcasted_iota(jnp.int32, (size, BLOCK), 1)
                row = lax.broadcasted_iota(jnp.int32, (size, size), 0)
                column = lax.broadcasted_iota(jnp.int32, (size, size), 1)
                seen = (column >= skip) & (column < skip + L)
                inside = seen & (row >= skip) & (row < skip + L)
                parts = []
                for head in range(2):
                    own = (lane < DH) if head == 0 else (lane >= DH)
                    scores = dot_nt(jnp.where(own, query, jnp.zeros_like(query)), key) * scale
                    scores = jnp.where(seen, scores, -1e30)
                    top = jnp.max(scores, axis=1, keepdims=True)
                    raised = jnp.exp(scores - top)
                    total = jnp.sum(raised, axis=1, keepdims=True)
                    probs = jnp.where(inside, raised * (1.0 / total), 0.0).astype(jnp.bfloat16)
                    prob_ref[0, part, index, head, 0:size, 0:size] = probs
                    parts.append(dot_nn(probs, value))
                mixed = jnp.where(lane < DH, parts[0], parts[1]).astype(jnp.bfloat16)
                if skip:
                    edge = lax.broadcasted_iota(jnp.int32, (size, BLOCK), 0) >= skip
                    mixed = jnp.where(edge, mixed, out_ref[part, low:high, :])
                out_ref[part, low:high, :] = mixed

    prob_shape = (groups, 2, len(ranges), 2, span, span)
    own_specs, far_specs = head_specs(width, chips, base)
    tail = 4 * QUARTER // 16
    args = (normed, other, w_query, w_key, w_value, b_query, b_value) + tuple(level_attn) + tuple(chips)
    return kernel_call(
        body,
        "attention_forward",
        meta,
        args,
        [whole(normed), whole(other)] + own_specs + [whole(b_query), whole(b_value)] + [pl.BlockSpec((16, BLOCK), lambda g, m: (tail, 0))] * 3 + far_specs,
        [shape_of(2, rows, groups * group), shape_of(2, rows, groups * BLOCK), shape_of(*prob_shape)],
        [
            pl.BlockSpec((2, rows, group), lambda g, m: (0, 0, g)),
            pl.BlockSpec((2, rows, BLOCK), lambda g, m: (0, 0, g)),
            pl.BlockSpec((1,) + prob_shape[1:], lambda g, m: (g, 0, 0, 0, 0, 0)),
        ],
        grid=(groups,),
        scratch=[pltpu.VMEM((width, group), jnp.bfloat16), pltpu.VMEM((8, BLOCK), jnp.float32)],
    )


def attention_out(meta, attended, w_out, chips):
    rows, width = attended[0].shape[1], w_out.shape[1]

    def body(meta_ref, a_ref, b_ref, own_ref, *refs):
        chip_refs, (near_ref, low_ref, high_ref, weight_ref) = refs[:CHIPS], refs[CHIPS:]
        weight_ref[0:BLOCK, :] = own_ref[...]
        for side, ref in enumerate(chip_refs):
            start = pl.multiple_of(meta_ref[side] * QUARTER, QUARTER)
            for index in range(DEPTH - 1):
                for b in range(2):
                    weight_ref[(index + 1) * BLOCK : (index + 2) * BLOCK, pl.ds(start + b * BLOCK, BLOCK)] = ref[
                        index, b * BLOCK : (b + 1) * BLOCK, :
                    ]
        half = weight_ref.shape[0] // 2

        def share(part):
            return dot_nn(a_ref[part], weight_ref[:half, :]) + dot_nn(b_ref[part], weight_ref[half:, :])

        near_ref[...] = share(0)
        across = share(1).astype(jnp.bfloat16)
        low_ref[...] = across[:, : width // 2]
        high_ref[...] = across[:, width // 2 :]

    views = tuple(chip.reshape(DEPTH - 1, 4 * QUARTER, BLOCK) for chip in chips)
    view_spec = pl.BlockSpec((DEPTH - 1, QUARTER, BLOCK), lambda i, m: (0, 3, 0))
    out = [shape_of(rows, width, dtype=jnp.float32)] + [shape_of(rows, width // 2)] * 2
    return kernel_call(
        body, "attention_out", meta, tuple(attended) + (w_out,) + views,
        [whole(a) for a in attended] + [pl.BlockSpec((BLOCK, width), lambda i, m: (m[OWN_CORE], 0))] + [view_spec] * CHIPS,
        out, [whole(o) for o in out], scratch=[pltpu.VMEM((DEPTH * BLOCK, width), jnp.bfloat16)],
    )


def attention_norm(meta, near, low, high, tokens, vectors):
    rows, width = tokens.shape

    def body(meta_ref, near_ref, low_ref, high_ref, tokens_ref, vec_ref, hidden_ref, branch_ref, normed_ref):
        got = jnp.concatenate([low_ref[...], high_ref[...]], axis=1).astype(jnp.float32)
        branch = near_ref[...] + got + vec_ref[BIAS_OUT : BIAS_OUT + 1]
        branch_ref[...] = branch
        hidden = tokens_ref[...].astype(jnp.float32) + vec_ref[SCALE_ATTN : SCALE_ATTN + 1] * branch
        hidden_ref[...] = hidden
        unit, _ = normalized(hidden)
        normed = (unit * vec_ref[GAIN_TWO : GAIN_TWO + 1] + vec_ref[SHIFT_TWO : SHIFT_TWO + 1]).astype(jnp.bfloat16)
        normed_ref[...] = normed

    args = (near, low, high, tokens, vectors)
    out = [shape_of(rows, width, dtype=jnp.float32)] * 2 + [shape_of(rows, width)]
    return kernel_call(body, "attention_norm", meta, args, [whole(a) for a in args], out, [whole(o) for o in out])


def feed_rows(normed_pieces, grad, up_weight, down_weight, bias, act_ref, gup_ref, low, high):
    width = up_weight.shape[0]
    deep = width // len(normed_pieces)
    pre = bias[:, low:high] + sum(
        dot_nn(piece[...], up_weight[k * deep : (k + 1) * deep, low:high]) for k, piece in enumerate(normed_pieces)
    )
    spread = 0.5 * (1.0 + lax.erf(pre * (1.0 / math.sqrt(2.0))))
    act_ref[:, low:high] = (pre * spread).astype(jnp.bfloat16)
    slope = spread + pre * jnp.exp(-0.5 * pre * pre) * (1.0 / math.sqrt(2.0 * math.pi))
    grad_up = (dot_nt(grad[...], down_weight[low:high, :]) * slope).astype(jnp.bfloat16)
    gup_ref[:, low:high] = grad_up
    return jnp.sum(grad_up.astype(jnp.float32), axis=0, keepdims=True)


def feed_near(meta, normed, grads, w_up, w_down, bias_up, chips):
    rows, width = grads[0].shape
    normed = [part if isinstance(part, (list, tuple)) else [part] for part in normed]
    flat = [piece for part in normed for piece in part]
    half_u = w_up.shape[1] // 2
    n_u = half_u // BLOCK
    count = len(normed)
    copies = len(flat) + count + 2 + CHIPS * (n_u + 2)

    def body(meta_ref, *refs):
        bias_ref, flat_hbm, refs = refs[0], refs[1 : 1 + len(flat)], refs[1 + len(flat) :]
        grad_hbm, refs = refs[:count], refs[count:]
        up_hbm, down_hbm, chip_refs, refs = refs[0], refs[1], refs[2 : 2 + CHIPS], refs[2 + CHIPS :]
        act_refs, gup_refs, back_refs, refs = refs[:count], refs[count : 2 * count], refs[2 * count : 3 * count], refs[3 * count :]
        sum_ref, up_weight, down_weight, normed_ref, grad_ref, sems = refs
        half = pl.ds(pl.multiple_of(meta_ref[OWN_CORE] * half_u, half_u), half_u)
        pieces = []
        for part, cut in enumerate(normed):
            deep = width // len(cut)
            for k in range(len(cut)):
                pieces.append((part, (flat_hbm[len(pieces)], normed_ref.at[part, :, pl.ds(k * deep, deep)])))
        moves = [move for part, move in pieces if part == 0]
        moves += [
            (up_hbm.at[:, half], up_weight.at[:, pl.ds(0, half_u)]),
            (grad_hbm[0], grad_ref.at[0]),
            (down_hbm.at[half, :], down_weight.at[pl.ds(0, half_u), :]),
        ]
        for part in range(1, count):
            moves += [move for owner, move in pieces if owner == part] + [(grad_hbm[part], grad_ref.at[part])]
        near_moves = len(moves)
        for side, ref in enumerate(chip_refs):
            start = pl.multiple_of(meta_ref[side] * QUARTER, QUARTER)
            for b in range(n_u):
                moves.append(
                    (
                        ref.at[pl.ds(b * QUARTER, QUARTER), :],
                        up_weight.at[pl.ds(start, QUARTER), pl.ds(half_u + b * BLOCK, BLOCK)],
                    )
                )
            for b in range(2):
                moves.append(
                    (
                        ref.at[pl.ds(n_u * QUARTER + b * half_u, half_u), :],
                        down_weight.at[pl.ds(half_u, half_u), pl.ds(start + b * BLOCK, BLOCK)],
                    )
                )
        handles = [pltpu.make_async_copy(source, target, sems.at[k]) for k, (source, target) in enumerate(moves)]
        for handle in handles:
            handle.start()
        for tile, waits in enumerate((handles[:near_moves], handles[near_moves:])):
            for handle in waits:
                handle.wait()
            low, high = tile * half_u, (tile + 1) * half_u
            sums = [
                feed_rows([normed_ref.at[p]], grad_ref.at[p], up_weight, down_weight, bias_ref, act_refs[p], gup_refs[p], low, high)
                for p in range(count)
            ]
            sum_ref[:, low:high] = sum(sums)
        for part in range(count):
            back_refs[part][...] = dot_nt(gup_refs[part][...], up_weight[...]).astype(jnp.bfloat16)

    anywhere = pl.BlockSpec(memory_space=pl.ANY)
    out = [shape_of(rows, 2 * half_u)] * (2 * count) + [shape_of(rows, width)] * count
    out += [shape_of(1, 2 * half_u, dtype=jnp.float32), shape_of(width, 2 * half_u), shape_of(2 * half_u, width)]
    args = tuple(flat) + tuple(grads) + (w_up, w_down) + tuple(chips)
    outs = kernel_call(
        body, "feed_near", meta, (bias_up,) + args, [whole(bias_up)] + [anywhere] * len(args), out, [whole(o) for o in out],
        scratch=[pltpu.VMEM((count, rows, width), jnp.bfloat16)] * 2 + [pltpu.SemaphoreType.DMA((copies,))],
        vmem=NEAR_BYTES,
    )
    return outs[:count], outs[count : 2 * count], outs[2 * count : 3 * count], outs[3 * count], outs[3 * count + 1], outs[3 * count + 2]


def feed_far(meta, normed, grad, bias_up, full_up, full_down):
    rows, width = grad.shape
    units = full_up.shape[1]
    pieces = len(normed)

    def body(meta_ref, *refs):
        normed_refs = refs[:pieces]
        grad_ref, bias_ref, up_ref, down_ref, act_ref, gup_ref, back_ref, sum_ref = refs[pieces:]
        for tile in range(2):
            low, high = tile * units // 2, (tile + 1) * units // 2
            sum_ref[:, low:high] = feed_rows(
                normed_refs, grad_ref, up_ref, down_ref, bias_ref, act_ref, gup_ref, low, high
            )
        back_ref[...] = dot_nt(gup_ref[...], up_ref[...]).astype(jnp.bfloat16)

    args = tuple(normed) + (grad, bias_up, full_up, full_down)
    out = [shape_of(rows, units)] * 2 + [shape_of(rows, width), shape_of(1, units, dtype=jnp.float32)]
    return kernel_call(body, "feed_far", meta, args, [whole(a) for a in args], out, [whole(o) for o in out])


def feed_down(meta, acts, full_down):
    rows, width = acts[0].shape[0], full_down.shape[1]
    count = len(acts)

    def body(meta_ref, *refs):
        weight_ref = refs[count]
        for act_ref, out_ref in zip(refs[:count], refs[count + 1 :]):
            out_ref[...] = dot_nn(act_ref[...], weight_ref[...]).astype(jnp.bfloat16)

    args = tuple(acts) + (full_down,)
    out = [shape_of(rows, width)] * count
    return kernel_call(body, "feed_down", meta, args, [whole(a) for a in args], out, [whole(o) for o in out])


def put_sides(lane, values, keep_ref, send_ref, at):
    keep, send = ((0, 2), (1, 3)) if lane == 0 else ((0, 1), (2, 3))
    for ref, sides in ((keep_ref, keep), (send_ref, send)):
        for index, side in enumerate(sides):
            ref[index * QUARTER : (index + 1) * QUARTER, at] = values[side * QUARTER : (side + 1) * QUARTER].astype(
                jnp.bfloat16
            )


def feed_gradients(meta, normed, turned_grads, gups, acts):
    normed = [part if isinstance(part, (list, tuple)) else [part] for part in normed]
    flat = [piece for part in normed for piece in part]
    rows = flat[0].shape[0]
    width = turned_grads[0].shape[0]
    half_u = gups[0].shape[1] // 2
    n = len(gups)

    def body(meta_ref, *refs):
        normed_refs, refs = refs[: len(flat)], refs[len(flat) :]
        turned_refs, gup_refs, act_refs, refs = refs[:n], refs[n : 2 * n], refs[2 * n : 3 * n], refs[3 * n :]
        outs, own_turned, whole_ref = refs[:4], refs[4:-1], refs[-1]
        step = pl.program_id(0)

        @pl.when(step == 0)
        def _():
            at = 0
            for part, target in zip(normed, own_turned):
                if len(part) == 1:
                    turn_into(meta_ref, normed_refs[at], target)
                else:
                    deep = width // len(part)
                    for k in range(len(part)):
                        whole_ref[:, k * deep : (k + 1) * deep] = normed_refs[at + k][...]
                    turn_into(meta_ref, whole_ref, target)
                at += len(part)

        def product(lefts, rights):
            return sum(dot_nn(left[...], right[...]) for left, right in zip(lefts, rights))

        for lane in range(2):
            kept, sent = outs[2 * lane : 2 * lane + 2]

            @pl.when(step == 2 * lane)
            def _():
                put_sides(lane, product(own_turned, gup_refs), kept, sent, slice(None))

            @pl.when(step == 2 * lane + 1)
            def _():
                put_sides(lane, product(turned_refs, act_refs), kept, sent, slice(None))

    args = tuple(flat) + tuple(turned_grads)
    by_lane = [pl.BlockSpec((rows, half_u), lambda g, m: (0, g >> 1))] * (2 * n)
    out_specs = [pl.BlockSpec((2 * QUARTER, half_u), lambda g, m: (0, jnp.minimum(g, 1)))] * 2
    out_specs += [pl.BlockSpec((2 * QUARTER, half_u), lambda g, m: (0, jnp.maximum(g - 2, 0)))] * 2
    outs = kernel_call(
        body, "feed_gradients", meta, args + tuple(gups) + tuple(acts),
        [whole(a) for a in args] + by_lane, [shape_of(2 * QUARTER, 2 * half_u)] * 4, out_specs, grid=(4,),
        scratch=[pltpu.VMEM((width, rows), jnp.bfloat16)] * 4 + [pltpu.VMEM((rows, width), jnp.bfloat16)],
    )
    return outs[:2], outs[2:]


def hidden_gradient(meta, backs, hidden, branch, cotangent, vectors):
    rows, width = hidden.shape

    def body(meta_ref, *refs):
        back_refs, (hidden_ref, branch_ref, cot_ref, vec_ref, dh_ref, e1_ref, sum_ref) = refs[: len(backs)], refs[len(backs) :]
        grad = sum(ref[...].astype(jnp.float32) for ref in back_refs)
        unit, inverse = normalized(hidden_ref[...])
        sum_ref[0:1, :] = jnp.sum(grad * unit, axis=0, keepdims=True)
        sum_ref[1:2, :] = jnp.sum(grad, axis=0, keepdims=True)
        total = valid_column(meta_ref, rows) * cot_ref[...].astype(jnp.float32) + norm_gradient(
            unit, inverse, vec_ref[GAIN_TWO : GAIN_TWO + 1], grad
        )
        dh_ref[...] = total
        sum_ref[2:3, :] = jnp.sum(total * branch_ref[...], axis=0, keepdims=True)
        scaled = vec_ref[SCALE_ATTN : SCALE_ATTN + 1] * total
        sum_ref[3:4, :] = jnp.sum(scaled, axis=0, keepdims=True)
        e1_ref[...] = scaled.astype(jnp.bfloat16)

    args = tuple(backs) + (hidden, branch, cotangent, vectors)
    out = [shape_of(rows, width, dtype=jnp.float32), shape_of(rows, width), shape_of(4, width, dtype=jnp.float32)]
    return kernel_call(body, "hidden_gradient", meta, args, [whole(a) for a in args], out, [whole(o) for o in out])


def attention_backward(meta, qkv, probs, attended, grads, turned_normed, w_out, chips, lane):
    rows, width = grads[0].shape
    group = 3 * BLOCK
    ranges = crop_ranges(rows)
    groups = DEPTH // 2
    scale = 1.0 / math.sqrt(DH)
    base = lane * groups

    def body(meta_ref, qkv_ref, prob_ref, mixed_ref, e1_ref, e1_other_ref, n_ref, n_other_ref, own_ref, *refs):
        chip_refs, (out_ref, keep_ref, send_ref, weight_ref, grad_ref, turned_e, turned_other) = refs[:CHIPS], refs[CHIPS:]
        step = pl.program_id(0)

        @pl.when(step == 0)
        def _():
            turn_into(meta_ref, e1_ref, turned_e)
            turn_into(meta_ref, e1_other_ref, turned_other)

        def far_weights():
            for side, ref in enumerate(chip_refs):
                start = pl.multiple_of(meta_ref[side] * QUARTER, QUARTER)
                for b in range(2):
                    weight_ref[:, pl.ds(start + b * BLOCK, BLOCK)] = ref[0, b * BLOCK : (b + 1) * BLOCK, :]

        if lane == 0:
            @pl.when(step == 0)
            def _():
                weight_ref[...] = own_ref[...]

            pl.when(step > 0)(far_weights)
        else:
            far_weights()
        for part, ref in enumerate((e1_ref, e1_other_ref)):
            grad_ref[part] = dot_nt(ref[...], weight_ref[...]).astype(jnp.bfloat16)
        for part in range(2):
            for index, (low, high, skip) in enumerate(ranges):
                size = high - low
                query = qkv_ref[part, low:high, 0:BLOCK]
                key = qkv_ref[part, low:high, BLOCK : 2 * BLOCK]
                value = qkv_ref[part, low:high, 2 * BLOCK : 3 * BLOCK]
                grad = grad_ref[part, low:high, :]
                lane_of = lax.broadcasted_iota(jnp.int32, (size, BLOCK), 1)
                row = lax.broadcasted_iota(jnp.int32, (size, BLOCK), 0)
                parts = []
                for head in range(2):
                    own = (lane_of < DH) if head == 0 else (lane_of >= DH)
                    low_probs = prob_ref[0, part, index, head, 0:size, 0:size]
                    grad_value = dot_tn(low_probs, grad)
                    grad_probs = dot_nt(jnp.where(own, grad, jnp.zeros_like(grad)), value)
                    wide = low_probs.astype(jnp.float32)
                    weighted = wide * grad_probs
                    inner = jnp.sum(weighted, axis=1, keepdims=True)
                    grad_scores = (weighted - wide * inner).astype(jnp.bfloat16)
                    parts.append(
                        (dot_nn(grad_scores, key) * scale, dot_tn(grad_scores, query) * scale, grad_value)
                    )
                for which in range(3):
                    at = slice(which * BLOCK, (which + 1) * BLOCK)
                    joined = jnp.where(lane_of < DH, parts[0][which], parts[1][which]).astype(jnp.bfloat16)
                    if skip:
                        joined = jnp.where(row >= skip, joined, out_ref[part, low:high, at])
                    out_ref[part, low:high, at] = joined
        both = dot_nn(n_ref[...], out_ref[0]) + dot_nn(n_other_ref[...], out_ref[1])
        put_sides(lane, both, keep_ref, send_ref, slice(0, group))
        both = dot_nn(turned_e[...], mixed_ref[0]) + dot_nn(turned_other[...], mixed_ref[1])
        put_sides(lane, both, keep_ref, send_ref, slice(group, group + BLOCK))

    views = tuple(chip.reshape(DEPTH - 1, 4 * QUARTER, BLOCK) for chip in chips)
    args = (qkv, probs, attended) + tuple(grads) + tuple(turned_normed) + (w_out,) + views
    return kernel_call(
        body,
        "attention_backward",
        meta,
        args,
        [
            pl.BlockSpec((2, rows, group), lambda g, m: (0, 0, g)),
            pl.BlockSpec((1,) + probs.shape[1:], lambda g, m: (g, 0, 0, 0, 0, 0)),
            pl.BlockSpec((2, rows, BLOCK), lambda g, m: (0, 0, g)),
            whole(grads[0]),
            whole(grads[1]),
            whole(turned_normed[0]),
            whole(turned_normed[1]),
            pl.BlockSpec((BLOCK, width), lambda g, m: (m[OWN_CORE], 0)),
        ]
        + [pl.BlockSpec((1, QUARTER, BLOCK), lambda g, m: (jnp.maximum(base + g - 1, 0), 3, 0))] * CHIPS,
        [shape_of(2, rows, groups * group)] + [shape_of(width // 2, groups * 4 * BLOCK)] * 2,
        [pl.BlockSpec((2, rows, group), lambda g, m: (0, 0, g))]
        + [pl.BlockSpec((width // 2, 4 * BLOCK), lambda g, m: (0, g))] * 2,
        grid=(groups,),
        scratch=[
            pltpu.VMEM((BLOCK, width), jnp.bfloat16),
            pltpu.VMEM((2, rows, BLOCK), jnp.bfloat16),
            pltpu.VMEM((width, rows), jnp.bfloat16),
            pltpu.VMEM((width, rows), jnp.bfloat16),
        ],
    )


def token_shares(meta, grads, w_query, w_key, w_value, chips):
    rows = grads[0].shape[1]
    width = w_query.shape[0]
    group = 3 * BLOCK

    def body(meta_ref, low_ref, high_ref, q_ref, k_ref, v_ref, *refs):
        chip_refs, (near_ref, across_ref, bias_ref, weight_ref, total_ref) = refs[:CHIPS], refs[CHIPS:]
        step = pl.program_id(0)

        @pl.when(step == 0)
        def _():
            for which, ref in enumerate((q_ref, k_ref, v_ref)):
                weight_ref[:, which * BLOCK : (which + 1) * BLOCK] = ref[...]

        @pl.when(step > 0)
        def _():
            fill_heads(meta_ref, chip_refs, weight_ref)

        def add(ref):
            sums = jnp.sum(ref[0].astype(jnp.float32), axis=0, keepdims=True)
            bias_ref[0] = sums + jnp.sum(ref[1].astype(jnp.float32), axis=0, keepdims=True)
            for part in range(2):
                share = dot_nt(ref[part], weight_ref[...])

                @pl.when(step == 0)
                def _():
                    total_ref[part] = share

                @pl.when(step > 0)
                def _():
                    total_ref[part] += share

        pl.when(step < 2)(lambda: add(low_ref))
        pl.when(step >= 2)(lambda: add(high_ref))

        @pl.when(step == DEPTH - 1)
        def _():
            near_ref[...] = total_ref[0]
            across_ref[...] = total_ref[1].astype(jnp.bfloat16)

    own_specs, far_specs = head_specs(width, chips)
    out = [shape_of(rows, width, dtype=jnp.float32), shape_of(rows, width)]
    return kernel_call(
        body,
        "token_shares",
        meta,
        tuple(grads) + (w_query, w_key, w_value) + tuple(chips),
        [
            pl.BlockSpec((2, rows, group), lambda g, m: (0, 0, jnp.minimum(g, 1))),
            pl.BlockSpec((2, rows, group), lambda g, m: (0, 0, jnp.maximum(g - 2, 0))),
        ]
        + own_specs
        + far_specs,
        out + [shape_of(DEPTH, 1, group, dtype=jnp.float32)],
        [whole(o) for o in out] + [pl.BlockSpec((1, 1, group), lambda g, m: (g, 0, 0))],
        grid=(DEPTH,),
        scratch=[pltpu.VMEM((width, group), jnp.bfloat16), pltpu.VMEM((2, rows, width), jnp.float32)],
    )


def token_gradient(meta, near, got, tokens, dh, vectors):
    rows, width = tokens.shape

    def body(meta_ref, near_ref, got_ref, tokens_ref, dh_ref, vec_ref, out_ref, sum_ref):
        grad = near_ref[...] + got_ref[...].astype(jnp.float32)
        unit, inverse = normalized(tokens_ref[...].astype(jnp.float32))
        sum_ref[0:1, :] = jnp.sum(grad * unit, axis=0, keepdims=True)
        sum_ref[1:2, :] = jnp.sum(grad, axis=0, keepdims=True)
        out_ref[...] = dh_ref[...] + norm_gradient(unit, inverse, vec_ref[GAIN_ONE : GAIN_ONE + 1], grad)

    args = (near, got, tokens, dh, vectors)
    out = [shape_of(rows, width, dtype=jnp.float32), shape_of(2, width, dtype=jnp.float32)]
    return kernel_call(body, "token_gradient", meta, args, [whole(a) for a in args], out, [whole(o) for o in out])


def layer_result(meta, downs, hidden, cotangent, vectors):
    rows, width = hidden.shape

    def body(meta_ref, *refs):
        down_refs, (hidden_ref, cot_ref, vec_ref, out_ref, sum_ref) = refs[: len(downs)], refs[len(downs) :]
        branch = sum(ref[...].astype(jnp.float32) for ref in down_refs) + vec_ref[BIAS_DOWN : BIAS_DOWN + 1]
        valid = valid_column(meta_ref, rows)
        out_ref[...] = valid * (hidden_ref[...] + vec_ref[SCALE_MLP : SCALE_MLP + 1] * branch)
        sum_ref[...] = jnp.sum(valid * cot_ref[...].astype(jnp.float32) * branch, axis=0, keepdims=True)

    args = tuple(downs) + (hidden, cotangent, vectors)
    out = [shape_of(rows, width, dtype=jnp.float32), shape_of(1, width, dtype=jnp.float32)]
    return kernel_call(body, "layer_result", meta, args, [whole(a) for a in args], out, [whole(o) for o in out])


def finish(meta, mine, other, kinds, name):
    width = CHIPS * QUARTER

    def body(meta_ref, mine_ref, other_ref, *outs):
        core = meta_ref[OWN_CORE]
        for ref, half in ((mine_ref, core), (other_ref, 1 - core)):
            at = 0
            for out_ref, (units, turned) in zip(outs, kinds):
                values = ref[0, :, at : at + units].astype(jnp.float32)
                place = pl.ds(pl.multiple_of(half * units, units), units)
                if turned:
                    out_ref[place, :] = values.T
                else:
                    out_ref[:, place] = values
                at += units

    side = pl.BlockSpec((1,) + mine.shape[1:], lambda j, m: (j, 0, 0))
    out, specs = [], []
    for units, turned in kinds:
        shape = (2 * units, width) if turned else (width, 2 * units)
        block = (2 * units, QUARTER) if turned else (QUARTER, 2 * units)
        out.append(shape_of(*shape, dtype=jnp.float32))
        specs.append(pl.BlockSpec(block, (lambda j, m: (0, m[j])) if turned else (lambda j, m: (m[j], 0))))
    return kernel_call(body, name, meta, (mine, other), [side, side], out, specs, grid=(CHIPS,))


def local_paired(
    tokens,
    slide_tiles,
    norm1_gain,
    norm1_bias,
    w_query,
    b_query,
    w_key,
    w_value,
    b_value,
    w_out,
    b_out,
    scale_attn,
    norm2_gain,
    norm2_bias,
    w_up,
    b_up,
    w_down,
    b_down,
    scale_mlp,
    cotangent,
):
    row_count, width = tokens.shape
    half_u = w_up.shape[1] // 2
    here = lax.axis_index("dp")
    level = lax.axis_index("mp")
    crops_here = row_count // L
    per_slide = CROPS_DEV // SLIDES_DEV
    crop = level * crops_here + jnp.arange(crops_here, dtype=jnp.int32)
    owner = (crop // per_slide)[:, None] == jnp.arange(SLIDES_DEV, dtype=jnp.int32)[None, :]
    limit = jnp.sum(jnp.where(owner, slide_tiles[None, :], 0), axis=1)
    valid = (crop % per_slide < limit).astype(jnp.int32)
    core = here & 1
    sides = jnp.stack([(here >> 1) ^ side for side in range(CHIPS)] + [core]).astype(jnp.int32)
    meta = jnp.concatenate([sides, valid])
    bias_q, bias_v, bias_u = [values.reshape(-1, BLOCK) for values in (b_query, b_value, b_up)]
    vectors = jnp.stack([norm1_gain, norm1_bias, norm2_gain, norm2_bias, scale_attn, scale_mlp, b_out, b_down])
    first, second = (X_SIDE, Y_SIDE), (Y_SIDE, X_SIDE)

    order = Order(meta)

    tokens_other = swap_plane(tokens, CORE_SIDE)
    slice_attn, slice_rest = order(slice_weights, w_query, w_key, w_value, w_out, w_up, w_down, bias_q, bias_v, bias_u)
    level_attn = [swap_depth(slice_attn, mask) for mask in (1, 2, 3)]
    one, one_other, grad, grad_b_down, one_turned, one_other_turned, grad_turned = order(
        prepare, tokens, tokens_other, cotangent, vectors
    )
    level_attn = order.land(*level_attn)
    far_attn = order.plain(lambda *parts: jnp.concatenate([part[: 4 * QUARTER] for part in parts], axis=0), *level_attn)
    attn_x, attn_y = swap_plane(far_attn, X_SIDE), swap_plane(far_attn, Y_SIDE)
    level_rest = swap_depth(order.hold(slice_rest), 2)
    attn_x, attn_y = order.land(attn_x, attn_y)
    half = far_attn.shape[0] // 2
    low, high = order.hold((attn_y[:half], attn_x[half:]))
    low, high = swap_plane(low, X_SIDE), swap_plane(high, Y_SIDE)
    level_rest, low, high = order.land(level_rest, low, high)
    corner = order.plain(lambda *parts: jnp.concatenate(parts), low, high)
    chips_attn = [far_attn, attn_x, attn_y, corner]
    level_rest, grad, grad_far = order.hold((level_rest, grad, grad))
    plane_rest = plane_swaps(level_rest)
    grad_other = swap_plane(grad, CORE_SIDE)
    grad_far = swap_depth(grad_far, 1)
    n_u = half_u // BLOCK
    low_qkv, low_attended, low_probs = order(
        attention_forward, one, one_other, w_query, w_key, w_value, bias_q, bias_v, level_attn, chips_attn, n_u, 0
    )
    high_qkv, high_attended, high_probs = order(
        attention_forward, one, one_other, w_query, w_key, w_value, bias_q, bias_v, level_attn, chips_attn, n_u, 1
    )
    grad_other, grad_far = order.land(grad_other, grad_far)
    out_near, *out_across = order(attention_out, (low_attended, high_attended), w_out, chips_attn)
    out_got = [swap_plane(part, CORE_SIDE) for part in out_across]
    plane_rest = order.land(*plane_rest)
    chips_rest = [level_rest] + plane_rest
    hidden, branch, normed = order(attention_norm, out_near, *out_got, tokens, vectors)
    normed_far = swap_depth(normed, 1)
    normed_other = swap_plane(normed, CORE_SIDE)
    grad_far_other = swap_plane(order.hold(grad_far), CORE_SIDE)

    pair_rows = level_attn[1][4 * QUARTER :].astype(jnp.float32)
    pair_bias = (pair_rows[2 : 2 + n_u] + pair_rows[4 + n_u : 4 + 2 * n_u]).reshape(-1)
    bias_up = jnp.concatenate([lax.dynamic_slice_in_dim(b_up, core * half_u, half_u), pair_bias])[None, :]
    *near, full_up, full_down = order(
        feed_near, (normed, normed_other), (grad, grad_other), w_up, w_down, bias_up, chips_rest
    )
    (normed_far,) = order.land(normed_far)
    normed_far, back_near = order.hold((normed_far, near[2][1]))
    normed_far_other = swap_plane(normed_far, CORE_SIDE)
    back_near = swap_plane(back_near, CORE_SIDE)
    far = order(feed_far, (normed_far,), grad_far, bias_up, full_up, full_down)
    far_other = order(feed_far, (normed_far_other,), grad_far_other, bias_up, full_up, full_down)
    acts, gups, backs = [list(a) + [b, c] for a, b, c in zip(near[:3], far[:3], far_other[:3])]
    grad_b_up = near[3] + far[3] + far_other[3]
    back_got, back_near = order.land(swap_plane(backs[3], CORE_SIDE), back_near)
    back_far = swap_depth(order.plain(add_low, backs[2], back_got), 1)
    grads_turned = [grad_turned] + list(order(turn, grad_other, grad_far, grad_far_other))
    rest_sides = order(
        feed_gradients, (normed, normed_other, normed_far, normed_far_other), grads_turned, gups, acts
    )
    downs = order(feed_down, acts, full_down)
    down_near, down_far = swap_plane(downs[1], CORE_SIDE), swap_plane(downs[3], CORE_SIDE)
    (back_far,) = order.land(back_far)
    rest_sent = order.hold([sent for _, sent in rest_sides])
    rest_got = [swap_plane(sent, side) for sent, side in zip(rest_sent, first)]
    dh, e1, sums_two = order(
        hidden_gradient, (backs[0], back_near, back_far), hidden, branch, cotangent, vectors
    )
    e1_other = swap_plane(e1, CORE_SIDE)
    down_near, down_far = order.land(down_near, down_far)
    down_far = order(lambda meta, *parts: add_parts(meta, [(part, 0) for part in parts])[0], downs[2], down_far)
    (e1_other,) = order.land(e1_other)
    down_far = swap_depth(order.hold(down_far), 1)
    low_grads, low_kept, low_sent = order(
        attention_backward, low_qkv, low_probs, low_attended, (e1, e1_other), (one_turned, one_other_turned), w_out, chips_attn, 0
    )
    high_grads, high_kept, high_sent = order(
        attention_backward, high_qkv, high_probs, high_attended, (e1, e1_other), (one_turned, one_other_turned), w_out, chips_attn, 1
    )
    *rest_got, down_far = order.land(*rest_got, down_far)

    def onward(kept, got):
        return order(
            lambda meta, *args: add_parts(meta, *[((args[2 * k], QUARTER), (args[2 * k + 1], QUARTER)) for k in range(2)]),
            *[array for pair in zip(kept, got) for array in pair],
        )

    def arrived(kept, got, last):
        return order(
            lambda meta, *args: add_parts(meta, *[[(part, 0) for part in args[3 * k : 3 * k + 3]] for k in range(2)]),
            *[array for triple in zip(kept, got, last) for array in triple],
        )

    rest_kept = [kept for kept, _ in rest_sides]
    rest_sent = order.hold(onward(rest_kept, rest_got))
    rest_last = [swap_plane(sent, side) for sent, side in zip(rest_sent, second)]
    one_near, one_across, sums_qkv = order(
        token_shares, (low_grads, high_grads), w_query, w_key, w_value, chips_attn
    )
    rest_last = order.land(*rest_last)
    rest_own, rest_pair = arrived(rest_kept, rest_got, rest_last)
    low_sent, high_sent, rest_pair = order.hold((low_sent, high_sent, rest_pair))
    attn_got = [swap_plane(sent, side) for sent, side in zip((low_sent, high_sent), first)]
    rest_pair = swap_depth(rest_pair, 2)
    layer_out, grad_scale_mlp = order(
        layer_result, (downs[0], down_near, down_far), hidden, cotangent, vectors
    )
    *attn_got, rest_pair = order.land(*attn_got, rest_pair)
    attn_kept = (low_kept, high_kept)
    attn_sent, one_across = order.hold((onward(attn_kept, attn_got), one_across))
    attn_last = [swap_plane(sent, side) for sent, side in zip(attn_sent, second)]
    one_got = swap_plane(one_across, CORE_SIDE)
    grad_rest = order(lambda meta, *parts: add_parts(meta, [(part, 0) for part in parts])[0], rest_own, rest_pair)
    (one_got,) = order.land(one_got)
    grad_tokens, sums_one = order(token_gradient, one_near, one_got, tokens, dh, vectors)

    def gather_small(sums_qkv, grad_b_up, *small):
        sums_qkv = sums_qkv.reshape(DEPTH, 3, BLOCK)
        nothing = jnp.zeros((1, half_u), jnp.float32)
        sums_up = jnp.concatenate([grad_b_up[:, :half_u], nothing, grad_b_up[:, half_u:], nothing], axis=0)
        shared = jnp.concatenate([sums_qkv[:, 0], sums_qkv[:, 2], sums_up], axis=1)
        shared = jnp.concatenate(
            [lax.dynamic_slice_in_dim(shared, level ^ index, 1, 0) for index in range(DEPTH)]
        ).reshape(1, -1, BLOCK)
        shared = jnp.concatenate([jnp.where(core == half, shared, 0.0) for half in range(2)])
        return jnp.concatenate([value.reshape(-1, BLOCK) for value in small] + [shared.reshape(-1, BLOCK)])

    totals = order.plain(gather_small, sums_qkv, grad_b_up, sums_one, sums_two, grad_scale_mlp, grad_b_down)
    totals_got = swap_plane(totals, X_SIDE)
    *attn_last, totals_got = order.land(*attn_last, totals_got)
    own_piece, pair_piece, level_sent = order(level_pieces, attn_kept, attn_got, attn_last)
    level_got = swap_depth(level_sent, 1)
    totals = order.plain(jnp.add, totals, totals_got)
    totals_got, grad_rest = order.hold((totals, grad_rest))
    rest_x, rest_y = swap_plane(grad_rest, X_SIDE), swap_plane(grad_rest, Y_SIDE)
    totals_got = swap_plane(totals_got, Y_SIDE)
    level_got, rest_x, rest_y, totals_got = order.land(level_got, rest_x, rest_y, totals_got)
    level_kept, level_sent = order.plain(
        lambda own, pair, got: (add_low(own, got[0]), add_low(pair, got[1])), own_piece, pair_piece, level_got
    )
    totals = order.plain(jnp.add, totals, totals_got)
    totals_got, grad_rest, level_sent = order.hold((totals, grad_rest, level_sent))
    level_got = swap_depth(level_sent, 2)
    rest_corner = swap_plane(grad_rest, X_SIDE | Y_SIDE)
    totals_got = swap_depth(totals_got, 1)
    level_got, rest_corner, totals_got = order.land(level_got, rest_corner, totals_got)
    grad_attn = order.plain(add_low, level_kept, level_got)
    totals = order.plain(jnp.add, totals, totals_got)
    plane_attn = plane_swaps(order.hold(grad_attn))
    totals_got = swap_depth(order.hold(totals), 2)
    rest_mine = order.plain(lambda *parts: jnp.stack(parts), grad_rest, rest_x, rest_y, rest_corner)
    rest_other = swap_plane(order.hold(rest_mine), CORE_SIDE)
    (rest_other,) = order.land(rest_other)
    full_grad_up, full_grad_down = order(
        finish, rest_mine, rest_other, ((half_u, False), (half_u, True)), "finish_rest"
    )
    *plane_attn, totals_got = order.land(*plane_attn, totals_got)
    attn_mine = order.plain(lambda *parts: jnp.stack(parts), grad_attn, *plane_attn)
    attn_other = swap_plane(order.hold(attn_mine), CORE_SIDE)
    totals = order.plain(jnp.add, totals, totals_got)
    totals_got = swap_plane(totals, CORE_SIDE)
    (attn_other,) = order.land(attn_other)
    full_grad_q, full_grad_k, full_grad_v, full_grad_o = order(
        finish, attn_mine, attn_other, ((BLOCK, False),) * 3 + ((BLOCK, True),), "finish_attn"
    )
    totals = order.plain(jnp.add, totals, totals_got)
    lines = width // BLOCK
    small_total = totals[: 8 * lines].reshape(8, width)
    shared_total = totals[8 * lines :].reshape(2, DEPTH, -1)
    shared_total = lax.dynamic_index_in_dim(shared_total, level, 1, keepdims=False)
    return (
        layer_out,
        grad_tokens,
        small_total[0],
        small_total[1],
        full_grad_q,
        shared_total[:, :BLOCK].reshape(-1),
        full_grad_k,
        full_grad_v,
        shared_total[:, BLOCK : 2 * BLOCK].reshape(-1),
        full_grad_o,
        small_total[5],
        small_total[4],
        small_total[2],
        small_total[3],
        full_grad_up,
        shared_total[:, 2 * BLOCK :].reshape(-1),
        full_grad_down,
        small_total[7],
        small_total[6],
    )


def local_general(
    tokens,
    slide_tiles,
    norm1_gain,
    norm1_bias,
    w_query,
    b_query,
    w_key,
    w_value,
    b_value,
    w_out,
    b_out,
    scale_attn,
    norm2_gain,
    norm2_bias,
    w_up,
    b_up,
    w_down,
    b_down,
    scale_mlp,
    cotangent,
):
    row_count = tokens.shape[0]
    per_slide = CROPS_DEV // SLIDES_DEV
    crop_index = (lax.axis_index("mp") * row_count + jnp.arange(row_count, dtype=jnp.int32)) // L
    slide_index = crop_index // per_slide
    owner = slide_index[:, None] == jnp.arange(SLIDES_DEV, dtype=jnp.int32)[None, :]
    limit_rows = jnp.sum(jnp.where(owner, slide_tiles[None, :], 0), axis=1)
    valid_rows = (crop_index % per_slide < limit_rows).astype(jnp.float32)[:, None]
    inputs = tokens.astype(jnp.float32)
    normed_one = layer_norm(inputs, norm1_gain, norm1_bias).astype(jnp.bfloat16)
    rows_one = lax.all_gather(normed_one, "mp", axis=0, tiled=True)
    queries = (jnp.dot(rows_one, w_query, preferred_element_type=jnp.float32) + b_query).astype(
        jnp.bfloat16
    )
    keys_all = jnp.dot(rows_one, w_key, preferred_element_type=jnp.float32).astype(jnp.bfloat16)
    values_all = (jnp.dot(rows_one, w_value, preferred_element_type=jnp.float32) + b_value).astype(
        jnp.bfloat16
    )
    heads_here = w_query.shape[1] // DH
    query_heads = to_heads(queries, heads_here)
    key_heads = to_heads(keys_all, heads_here)
    value_heads = to_heads(values_all, heads_here)
    scores = attn_scores(query_heads, key_heads)
    top_score = jnp.max(scores, axis=-1, keepdims=True)
    log_total = top_score + jnp.log(jnp.sum(jnp.exp(scores - top_score), axis=-1, keepdims=True))
    weights_low = jnp.exp(scores - log_total).astype(jnp.bfloat16)
    mixed_heads = jnp.einsum(
        "chqk,ckhd->cqhd", weights_low, value_heads, preferred_element_type=jnp.float32
    )
    attended = mixed_heads.reshape(queries.shape).astype(jnp.bfloat16)
    attn_sum = lax.psum_scatter(
        jnp.dot(attended, w_out, preferred_element_type=jnp.float32).astype(jnp.bfloat16),
        "mp",
        scatter_dimension=0,
        tiled=True,
    ).astype(jnp.float32)
    branch_one = attn_sum + b_out
    hidden_state = inputs + scale_attn * branch_one
    normed_two = layer_norm(hidden_state, norm2_gain, norm2_bias).astype(jnp.bfloat16)
    rows_two = lax.all_gather(normed_two, "mp", axis=0, tiled=True)
    up_pre = jnp.dot(rows_two, w_up, preferred_element_type=jnp.float32) + b_up
    activated = gelu_exact(up_pre).astype(jnp.bfloat16)
    down_sum = lax.psum_scatter(
        jnp.dot(activated, w_down, preferred_element_type=jnp.float32).astype(jnp.bfloat16),
        "mp",
        scatter_dimension=0,
        tiled=True,
    ).astype(jnp.float32)
    branch_two = down_sum + b_down
    layer_out = valid_rows * (hidden_state + scale_mlp * branch_two)
    grad_out = valid_rows * cotangent.astype(jnp.float32)
    grad_scale_mlp = jnp.sum(grad_out * branch_two, axis=0)
    grad_branch_two = scale_mlp * grad_out
    grad_b_down = jnp.sum(grad_branch_two, axis=0)
    grad_down_low = grad_branch_two.astype(jnp.bfloat16)
    gelu_value, gelu_back = jax.vjp(gelu_exact, up_pre)
    grad_down_rows = lax.all_gather(grad_down_low, "mp", axis=0, tiled=True)
    grad_act = contract_cols(grad_down_rows, w_down)
    grad_up = gelu_back(grad_act)[0].astype(jnp.bfloat16)
    grad_w_up = contract_rows(rows_two, grad_up)
    grad_w_down = contract_rows(activated, grad_down_rows)
    grad_b_up = jnp.sum(grad_up.astype(jnp.float32), axis=0)
    grad_rows_two = lax.psum_scatter(
        contract_cols(grad_up, w_up).astype(jnp.bfloat16), "mp", scatter_dimension=0, tiled=True
    ).astype(jnp.float32)
    norm2_value, norm2_back = jax.vjp(layer_norm, hidden_state, norm2_gain, norm2_bias)
    grad_hidden_norm, grad_norm2_gain, grad_norm2_bias = norm2_back(grad_rows_two)
    grad_hidden = grad_out + grad_hidden_norm
    grad_scale_attn = jnp.sum(grad_hidden * branch_one, axis=0)
    grad_branch_one = scale_attn * grad_hidden
    grad_b_out = jnp.sum(grad_branch_one, axis=0)
    grad_attn_low = grad_branch_one.astype(jnp.bfloat16)
    grad_attn_rows = lax.all_gather(grad_attn_low, "mp", axis=0, tiled=True)
    grad_w_out = contract_rows(attended, grad_attn_rows)
    grad_mixed = contract_cols(grad_attn_rows, w_out).astype(jnp.bfloat16)
    grad_mixed_heads = to_heads(grad_mixed, heads_here)
    scores_again = attn_scores(query_heads, key_heads)
    probs = jnp.exp(scores_again - log_total)
    probs_low = probs.astype(jnp.bfloat16)
    grad_value_heads = jnp.einsum(
        "chqk,cqhd->ckhd", probs_low, grad_mixed_heads, preferred_element_type=jnp.float32
    )
    grad_values = grad_value_heads.reshape(queries.shape).astype(jnp.bfloat16)
    grad_probs = jnp.einsum(
        "cqhd,ckhd->chqk", grad_mixed_heads, value_heads, preferred_element_type=jnp.float32
    )
    row_inner = jnp.sum(probs * grad_probs, axis=-1, keepdims=True)
    grad_scores = (probs * (grad_probs - row_inner)).astype(jnp.bfloat16)
    inverse_root = 1.0 / math.sqrt(DH)
    grad_query_heads = jnp.einsum(
        "chqk,ckhd->cqhd", grad_scores, key_heads, preferred_element_type=jnp.float32
    )
    grad_queries = (inverse_root * grad_query_heads).reshape(queries.shape).astype(jnp.bfloat16)
    grad_key_heads = jnp.einsum(
        "chqk,cqhd->ckhd", grad_scores, query_heads, preferred_element_type=jnp.float32
    )
    grad_keys = (inverse_root * grad_key_heads).reshape(queries.shape).astype(jnp.bfloat16)
    grad_w_query = contract_rows(rows_one, grad_queries)
    grad_b_query = jnp.sum(grad_queries.astype(jnp.float32), axis=0)
    grad_w_key = contract_rows(rows_one, grad_keys)
    grad_w_value = contract_rows(rows_one, grad_values)
    grad_b_value = jnp.sum(grad_values.astype(jnp.float32), axis=0)
    grad_rows_one = lax.psum_scatter(
        (
            contract_cols(grad_queries, w_query)
            + contract_cols(grad_keys, w_key)
            + contract_cols(grad_values, w_value)
        ).astype(jnp.bfloat16),
        "mp",
        scatter_dimension=0,
        tiled=True,
    ).astype(jnp.float32)
    norm1_value, norm1_back = jax.vjp(layer_norm, inputs, norm1_gain, norm1_bias)
    grad_in_norm, grad_norm1_gain, grad_norm1_bias = norm1_back(grad_rows_one)
    grad_tokens = grad_hidden + grad_in_norm
    small_stack = jnp.stack(
        [
            grad_norm1_gain,
            grad_norm1_bias,
            grad_norm2_gain,
            grad_norm2_bias,
            grad_scale_attn,
            grad_scale_mlp,
            grad_b_out,
            grad_b_down,
        ],
        axis=1,
    )
    small_total = lax.psum(small_stack.astype(jnp.bfloat16), "mp")
    (
        share_wq,
        share_bq,
        share_wk,
        share_wv,
        share_bv,
        share_wo,
        share_up,
        share_bup,
        share_down,
        share_small,
    ) = (
        lax.psum_scatter(
            grad_w_query.astype(jnp.bfloat16), "dp", scatter_dimension=0, tiled=True
        ).astype(jnp.float32),
        lax.psum_scatter(
            grad_b_query.astype(jnp.bfloat16), "dp", scatter_dimension=0, tiled=True
        ).astype(jnp.float32),
        lax.psum_scatter(
            grad_w_key.astype(jnp.bfloat16), "dp", scatter_dimension=0, tiled=True
        ).astype(jnp.float32),
        lax.psum_scatter(
            grad_w_value.astype(jnp.bfloat16), "dp", scatter_dimension=0, tiled=True
        ).astype(jnp.float32),
        lax.psum_scatter(
            grad_b_value.astype(jnp.bfloat16), "dp", scatter_dimension=0, tiled=True
        ).astype(jnp.float32),
        lax.psum_scatter(
            grad_w_out.astype(jnp.bfloat16), "dp", scatter_dimension=0, tiled=True
        ).astype(jnp.float32),
        lax.psum_scatter(
            grad_w_up.astype(jnp.bfloat16), "dp", scatter_dimension=0, tiled=True
        ).astype(jnp.float32),
        lax.psum_scatter(
            grad_b_up.astype(jnp.bfloat16), "dp", scatter_dimension=0, tiled=True
        ).astype(jnp.float32),
        lax.psum_scatter(
            grad_w_down.astype(jnp.bfloat16), "dp", scatter_dimension=0, tiled=True
        ).astype(jnp.float32),
        lax.psum_scatter(small_total, "dp", scatter_dimension=0, tiled=True).astype(jnp.float32),
    )
    (
        full_wq,
        full_bq,
        full_wk,
        full_wv,
        full_bv,
        full_wo,
        full_up,
        full_bup,
        full_down,
        full_small,
    ) = (
        lax.all_gather(share_wq.astype(jnp.bfloat16), "dp", axis=0, tiled=True).astype(
            share_wq.dtype
        ),
        lax.all_gather(share_bq.astype(jnp.bfloat16), "dp", axis=0, tiled=True).astype(
            share_bq.dtype
        ),
        lax.all_gather(share_wk.astype(jnp.bfloat16), "dp", axis=0, tiled=True).astype(
            share_wk.dtype
        ),
        lax.all_gather(share_wv.astype(jnp.bfloat16), "dp", axis=0, tiled=True).astype(
            share_wv.dtype
        ),
        lax.all_gather(share_bv.astype(jnp.bfloat16), "dp", axis=0, tiled=True).astype(
            share_bv.dtype
        ),
        lax.all_gather(share_wo.astype(jnp.bfloat16), "dp", axis=0, tiled=True).astype(
            share_wo.dtype
        ),
        lax.all_gather(share_up.astype(jnp.bfloat16), "dp", axis=0, tiled=True).astype(
            share_up.dtype
        ),
        lax.all_gather(share_bup.astype(jnp.bfloat16), "dp", axis=0, tiled=True).astype(
            share_bup.dtype
        ),
        lax.all_gather(share_down.astype(jnp.bfloat16), "dp", axis=0, tiled=True).astype(
            share_down.dtype
        ),
        lax.all_gather(share_small.astype(jnp.bfloat16), "dp", axis=0, tiled=True).astype(
            share_small.dtype
        ),
    )
    return (
        layer_out,
        grad_tokens,
        full_small[:, 0],
        full_small[:, 1],
        full_wq,
        full_bq,
        full_wk,
        full_wv,
        full_bv,
        full_wo,
        full_small[:, 6],
        full_small[:, 4],
        full_small[:, 2],
        full_small[:, 3],
        full_up,
        full_bup,
        full_down,
        full_small[:, 7],
        full_small[:, 5],
    )


def solution(mesh):
    in_specs = (
        P(("dp", "mp"), None),
        P("dp"),
        P(),
        P(),
        P(None, "mp"),
        P("mp"),
        P(None, "mp"),
        P(None, "mp"),
        P("mp"),
        P("mp", None),
        P(),
        P(),
        P(),
        P(),
        P(None, "mp"),
        P("mp"),
        P("mp", None),
        P(),
        P(),
        P(("dp", "mp"), None),
    )
    out_specs = (
        P(("dp", "mp"), None),
        P(("dp", "mp"), None),
        P(),
        P(),
        P(None, "mp"),
        P("mp"),
        P(None, "mp"),
        P(None, "mp"),
        P("mp"),
        P("mp", None),
        P(),
        P(),
        P(),
        P(),
        P(None, "mp"),
        P("mp"),
        P("mp", None),
        P(),
        P(),
    )
    paired = mesh.shape["dp"] == 8 and mesh.shape["mp"] == 4
    local = local_paired if paired else local_general
    return jax.shard_map(local, mesh=mesh, in_specs=in_specs, out_specs=out_specs, check_vma=False)
```

```python
import functools
import math

import jax
import jax.numpy as jnp
from jax import lax
from jax.experimental import pallas as pl
from jax.experimental.pallas import tpu as pltpu
from jax.sharding import PartitionSpec as P

DH = 64
L = 197
SLIDES_DEV = 2
CROPS_DEV = 8


def layer_norm(values, gain, shift):
    average = jnp.mean(values, axis=-1, keepdims=True)
    centered = values - average
    spread = jnp.mean(centered * centered, axis=-1, keepdims=True)
    return centered * lax.rsqrt(spread + 1e-06) * gain + shift


def gelu_exact(values):
    return jax.nn.gelu(values, approximate=False)


def contract_rows(left, right):
    return lax.dot_general(
        left, right, (((0,), (0,)), ((), ())), preferred_element_type=jnp.float32
    )


def contract_cols(left, right):
    return lax.dot_general(
        left, right, (((1,), (1,)), ((), ())), preferred_element_type=jnp.float32
    )


def to_heads(matrix, heads_here):
    return matrix.reshape(matrix.shape[0] // L, L, heads_here, DH)


def attn_scores(query_heads, key_heads):
    product = jnp.einsum(
        "cqhd,ckhd->chqk", query_heads, key_heads, preferred_element_type=jnp.float32
    )
    return product * (1.0 / math.sqrt(DH))


BLOCK = 128
QUARTER = 256
X_SIDE, Y_SIDE, CORE_SIDE = 2, 4, 1
PLANE = 8
CHIPS = 4
DEPTH = 4
OWN_CORE = CHIPS
OWN_LEVEL = CHIPS + 1
FLAGS = CHIPS + 2
GAIN_ONE, SHIFT_ONE, GAIN_TWO, SHIFT_TWO, SCALE_ATTN, SCALE_MLP, BIAS_OUT, BIAS_DOWN = range(8)
VMEM_BYTES = 24 * 2**20
NEAR_BYTES = 28 * 2**20
PARTS_BYTES = 24 * 2**20
NORM_BYTES = 24 * 2**20
PIECES_BYTES = 24 * 2**20


def swap_plane(values, mask):
    return lax.ppermute(values, "dp", [(i, i ^ mask) for i in range(PLANE)])


def swap_depth(values, mask):
    return lax.ppermute(values, "mp", [(i, i ^ mask) for i in range(DEPTH)])


def plane_swaps(values):
    return [swap_plane(values, side) for side in (X_SIDE, Y_SIDE, X_SIDE | Y_SIDE)]


class Order:
    def __init__(self, meta):
        self.meta = meta

    def hold(self, values):
        leaves, tree = jax.tree.flatten(values)
        *leaves, self.meta = lax.optimization_barrier(tuple(leaves) + (self.meta,))
        return jax.tree.unflatten(tree, leaves)

    def land(self, *arrays):
        return self.hold(list(arrays))

    def __call__(self, step, *args):
        return self.hold(step(self.meta, *args))

    def plain(self, step, *args):
        return self.hold(step(*self.hold(args)))


def dot_nt(left, right):
    return lax.dot_general(left, right, (((1,), (1,)), ((), ())), preferred_element_type=jnp.float32)


def dot_tn(left, right):
    return lax.dot_general(left, right, (((0,), (0,)), ((), ())), preferred_element_type=jnp.float32)


def dot_nn(left, right):
    return lax.dot_general(left, right, (((1,), (0,)), ((), ())), preferred_element_type=jnp.float32)


def add_low(*values):
    return sum(value.astype(jnp.float32) for value in values).astype(jnp.bfloat16)


def crop_ranges(rows):
    ranges = []
    for crop in range(rows // L):
        low = crop * L // 16 * 16
        high = min((crop + 1) * L + 15, rows + 15) // 16 * 16
        ranges.append((low, min(high, rows), crop * L - low))
    return ranges


def add_parts(meta, *sums):
    rows = [len(parts) for parts in sums]
    flat = [part for parts in sums for part in parts]
    heights = [min(array.shape[0] - start for array, start in parts) for parts in sums]

    def body(meta_ref, *refs):
        at = 0
        for count, out_ref in zip(rows, refs[len(flat) :]):
            out_ref[...] = add_low(*[ref[...] for ref in refs[at : at + count]])
            at += count

    in_specs, out = [], []
    for parts, height in zip(sums, heights):
        for array, start in parts:
            in_specs.append(pl.BlockSpec((height, array.shape[1]), lambda i, m, b=start // height: (b, 0)))
        out.append(shape_of(height, parts[0][0].shape[1]))
    return kernel_call(
        body, "add_parts", meta, [array for array, _ in flat], in_specs, out, [whole(o) for o in out], vmem=PARTS_BYTES
    )


def level_pieces(meta, kept, got, last):
    half = kept[0].shape[1] // 2

    def body(meta_ref, *refs):
        own_ref, pair_ref, send_ref = refs[6:]
        for lane, near_ref in enumerate((own_ref, pair_ref)):
            total = add_low(*[ref[...] for ref in refs[3 * lane : 3 * lane + 3]])
            near_ref[...] = total[:, :half]
            send_ref[lane] = total[:, half:]

    first = pl.BlockSpec((QUARTER, 2 * half), lambda i, m: (0, 0))
    args = [array for triple in zip(kept, got, last) for array in triple]
    out = [shape_of(QUARTER, half)] * 2 + [shape_of(2, QUARTER, half)]
    return kernel_call(
        body, "level_pieces", meta, args, [first] * 6, out, [whole(o) for o in out], vmem=PIECES_BYTES
    )


def whole(array):
    zeros = (0,) * array.ndim
    return pl.BlockSpec(array.shape, lambda *_: zeros)


def kernel_call(body, name, meta, args, in_specs, out_shape, out_specs, grid=(1,), scratch=(), flops=1000, vmem=VMEM_BYTES):
    return pl.pallas_call(
        body,
        grid_spec=pltpu.PrefetchScalarGridSpec(
            num_scalar_prefetch=1,
            grid=grid,
            in_specs=in_specs,
            out_specs=out_specs,
            scratch_shapes=list(scratch),
        ),
        out_shape=out_shape,
        compiler_params=pltpu.CompilerParams(vmem_limit_bytes=vmem),
        cost_estimate=pl.CostEstimate(flops=flops, bytes_accessed=1000, transcendentals=0),
        name=name,
    )(meta, *args)


def shape_of(*dims, dtype=jnp.bfloat16):
    return jax.ShapeDtypeStruct(dims, dtype)


def normalized(values):
    centered = values - jnp.mean(values, axis=-1, keepdims=True)
    inverse = lax.rsqrt(jnp.mean(centered * centered, axis=-1, keepdims=True) + 1e-06)
    return centered * inverse, inverse


def norm_gradient(unit, inverse, gain, grad):
    wide = grad * gain
    return inverse * (
        wide - jnp.mean(wide, axis=-1, keepdims=True) - unit * jnp.mean(wide * unit, axis=-1, keepdims=True)
    )


def valid_column(meta_ref, rows):
    row = lax.broadcasted_iota(jnp.int32, (rows, 1), 0)
    valid = jnp.zeros((rows, 1), jnp.float32)
    for crop in range(rows // L):
        inside = (row >= crop * L) & (row < (crop + 1) * L)
        valid = jnp.where(inside, meta_ref[FLAGS + crop].astype(jnp.float32), valid)
    return valid


def quarter_of(meta_ref, side):
    return pl.ds(pl.multiple_of(meta_ref[side] * QUARTER, QUARTER), QUARTER)


def slice_weights(meta, w_query, w_key, w_value, w_out, w_up, w_down, b_query, b_value, b_up):
    half_h, half_u = w_query.shape[1] // 2, w_up.shape[1] // 2
    n_h, n_u = half_h // BLOCK, half_u // BLOCK

    def body(meta_ref, q_ref, k_ref, v_ref, o_ref, up_ref, down_ref, bq_ref, bv_ref, bu_ref, attn_ref, rest_ref):
        core = meta_ref[OWN_CORE]
        for which, ref in enumerate((q_ref, k_ref, v_ref)):
            attn_ref[which * QUARTER : (which + 1) * QUARTER, :] = ref[...]
        for b in range(2):
            row = 3 * QUARTER + b * half_h
            attn_ref[row : row + half_h, :] = o_ref[:, b * BLOCK : (b + 1) * BLOCK]
        picked = jnp.concatenate(
            [
                bq_ref[pl.ds(core * n_h, n_h), :],
                bv_ref[pl.ds(core * n_h, n_h), :],
                bu_ref[pl.ds(core * n_u, n_u), :],
            ],
            axis=0,
        )
        high = picked.astype(jnp.bfloat16)
        low = (picked - high.astype(jnp.float32)).astype(jnp.bfloat16)
        spare = jnp.zeros((16 - 2 * picked.shape[0], BLOCK), jnp.bfloat16)
        attn_ref[4 * QUARTER :, :] = jnp.concatenate([high, low, spare], axis=0)
        for b in range(n_u):
            rest_ref[b * QUARTER : (b + 1) * QUARTER, :] = up_ref[:, b * BLOCK : (b + 1) * BLOCK]
        for b in range(2):
            row = n_u * QUARTER + b * half_u
            rest_ref[row : row + half_u, :] = down_ref[:, b * BLOCK : (b + 1) * BLOCK]

    args = (w_query, w_key, w_value, w_out, w_up, w_down, b_query, b_value, b_up)
    out = [shape_of(4 * QUARTER + 16, BLOCK), shape_of(2 * n_u * QUARTER, BLOCK)]
    return kernel_call(
        body,
        "slice_weights",
        meta,
        args,
        [pl.BlockSpec((QUARTER, half_h), lambda i, m: (m[0], m[OWN_CORE]))] * 3
        + [
            pl.BlockSpec((half_h, QUARTER), lambda i, m: (m[OWN_CORE], m[0])),
            pl.BlockSpec((QUARTER, half_u), lambda i, m: (m[0], m[OWN_CORE])),
            pl.BlockSpec((half_u, QUARTER), lambda i, m: (m[OWN_CORE], m[0])),
            whole(b_query),
            whole(b_value),
            whole(b_up),
        ],
        out,
        [whole(o) for o in out],
        vmem=60 * 2**20,
    )


def turn_into(meta_ref, values, turned_ref, index=None):
    for side in range(CHIPS):
        rows = slice(side * QUARTER, (side + 1) * QUARTER)
        if index is None:
            turned_ref[rows, :] = values[:, quarter_of(meta_ref, side)].T
        else:
            turned_ref[rows, :] = values[index, :, quarter_of(meta_ref, side)].T


def turn(meta, *arrays):
    def body(meta_ref, *refs):
        for source, target in zip(refs[: len(arrays)], refs[len(arrays) :]):
            turn_into(meta_ref, source, target)

    out = [shape_of(*a.shape[::-1]) for a in arrays]
    return kernel_call(body, "turn", meta, arrays, [whole(a) for a in arrays], out, [whole(o) for o in out])


def prepare(meta, tokens, tokens_other, cotangent, vectors):
    rows, width = tokens.shape

    def body(meta_ref, tokens_ref, other_ref, cot_ref, vec_ref, one_ref, two_ref, grad_ref, sum_ref, *turned):
        for source, target in ((tokens_ref, one_ref), (other_ref, two_ref)):
            unit, _ = normalized(source[...].astype(jnp.float32))
            target[...] = (unit * vec_ref[GAIN_ONE : GAIN_ONE + 1] + vec_ref[SHIFT_ONE : SHIFT_ONE + 1]).astype(
                jnp.bfloat16
            )
        grad = vec_ref[SCALE_MLP : SCALE_MLP + 1] * (valid_column(meta_ref, rows) * cot_ref[...].astype(jnp.float32))
        sum_ref[...] = jnp.sum(grad, axis=0, keepdims=True)
        grad_ref[...] = grad.astype(jnp.bfloat16)
        for source, target in zip((one_ref, two_ref, grad_ref), turned):
            turn_into(meta_ref, source, target)

    args = (tokens, tokens_other, cotangent, vectors)
    out = [shape_of(rows, width)] * 3 + [shape_of(1, width, dtype=jnp.float32)] + [shape_of(width, rows)] * 3
    return kernel_call(body, "prepare", meta, args, [whole(a) for a in args], out, [whole(o) for o in out])


def fill_heads(meta_ref, chip_refs, weight_ref):
    for side, ref in enumerate(chip_refs):
        at = quarter_of(meta_ref, side)
        for which in range(3):
            weight_ref[at, which * BLOCK : (which + 1) * BLOCK] = ref[which * QUARTER : (which + 1) * QUARTER, :]


def head_specs(width, chips, base=0):
    own = [pl.BlockSpec((width, BLOCK), lambda g, m: (0, m[OWN_CORE]))] * 3
    far = [pl.BlockSpec((4 * QUARTER, BLOCK), lambda g, m: (jnp.maximum(base + g - 1, 0), 0))] * len(chips)
    return own, far


def attention_forward(meta, normed, other, w_query, w_key, w_value, b_query, b_value, level_attn, chips, w_count, lane):
    rows, width = normed.shape
    group = 3 * BLOCK
    ranges = crop_ranges(rows)
    span = max(high - low for low, high, _ in ranges)
    scale = 1.0 / math.sqrt(DH)
    count = 2 + w_count
    groups = DEPTH // 2
    base = lane * groups

    def body(meta_ref, normed_ref, other_ref, q_ref, k_ref, v_ref, bq_ref, bv_ref, one_ref, two_ref, three_ref, *refs):
        chip_refs, (qkv_ref, out_ref, prob_ref, weight_ref, sum_ref) = refs[:CHIPS], refs[CHIPS:]
        group_here = base + pl.program_id(0)
        core = meta_ref[OWN_CORE]

        @pl.when(group_here == 0)
        def _():
            for which, ref in enumerate((q_ref, k_ref, v_ref)):
                weight_ref[:, which * BLOCK : (which + 1) * BLOCK] = ref[...]
            sum_ref[0:1, :] = bq_ref[pl.ds(core, 1), :]
            sum_ref[1:2, :] = bv_ref[pl.ds(core, 1), :]

        for index, ref in enumerate((one_ref, two_ref, three_ref)):
            @pl.when(group_here == index + 1)
            def _():
                both = ref[...].astype(jnp.float32)
                sum_ref[0:2, :] = both[0:2] + both[count : count + 2]

        @pl.when(group_here > 0)
        def _():
            fill_heads(meta_ref, chip_refs, weight_ref)

        bias = jnp.concatenate([sum_ref[0:1, :], jnp.zeros((1, BLOCK), jnp.float32), sum_ref[1:2, :]], axis=1)
        for part, rows_ref in enumerate((normed_ref, other_ref)):
            qkv_ref[part] = (dot_nn(rows_ref[...], weight_ref[...]) + bias).astype(jnp.bfloat16)
        for part in range(2):
            for index, (low, high, skip) in enumerate(ranges):
                size = high - low
                query = qkv_ref[part, low:high, 0:BLOCK]
                key = qkv_ref[part, low:high, BLOCK : 2 * BLOCK]
                value = qkv_ref[part, low:high, 2 * BLOCK : 3 * BLOCK]
                lane = lax.broadcasted_iota(jnp.int32, (size, BLOCK), 1)
                row = lax.broadcasted_iota(jnp.int32, (size, size), 0)
                column = lax.broadcasted_iota(jnp.int32, (size, size), 1)
                seen = (column >= skip) & (column < skip + L)
                inside = seen & (row >= skip) & (row < skip + L)
                parts = []
                for head in range(2):
                    own = (lane < DH) if head == 0 else (lane >= DH)
                    scores = dot_nt(jnp.where(own, query, jnp.zeros_like(query)), key) * scale
                    scores = jnp.where(seen, scores, -1e30)
                    top = jnp.max(scores, axis=1, keepdims=True)
                    raised = jnp.exp(scores - top)
                    total = jnp.sum(raised, axis=1, keepdims=True)
                    probs = jnp.where(inside, raised * (1.0 / total), 0.0).astype(jnp.bfloat16)
                    prob_ref[0, part, index, head, 0:size, 0:size] = probs
                    parts.append(dot_nn(probs, value))
                mixed = jnp.where(lane < DH, parts[0], parts[1]).astype(jnp.bfloat16)
                if skip:
                    edge = lax.broadcasted_iota(jnp.int32, (size, BLOCK), 0) >= skip
                    mixed = jnp.where(edge, mixed, out_ref[part, low:high, :])
                out_ref[part, low:high, :] = mixed

    prob_shape = (groups, 2, len(ranges), 2, span, span)
    own_specs, far_specs = head_specs(width, chips, base)
    tail = 4 * QUARTER // 16
    args = (normed, other, w_query, w_key, w_value, b_query, b_value) + tuple(level_attn) + tuple(chips)
    return kernel_call(
        body,
        "attention_forward",
        meta,
        args,
        [whole(normed), whole(other)] + own_specs + [whole(b_query), whole(b_value)] + [pl.BlockSpec((16, BLOCK), lambda g, m: (tail, 0))] * 3 + far_specs,
        [shape_of(2, rows, groups * group), shape_of(2, rows, groups * BLOCK), shape_of(*prob_shape)],
        [
            pl.BlockSpec((2, rows, group), lambda g, m: (0, 0, g)),
            pl.BlockSpec((2, rows, BLOCK), lambda g, m: (0, 0, g)),
            pl.BlockSpec((1,) + prob_shape[1:], lambda g, m: (g, 0, 0, 0, 0, 0)),
        ],
        grid=(groups,),
        scratch=[pltpu.VMEM((width, group), jnp.bfloat16), pltpu.VMEM((8, BLOCK), jnp.float32)],
    )


def attention_out(meta, attended, w_out, chips):
    rows, width = attended[0].shape[1], w_out.shape[1]

    def body(meta_ref, a_ref, b_ref, own_ref, *refs):
        chip_refs, (near_ref, low_ref, high_ref, weight_ref) = refs[:CHIPS], refs[CHIPS:]
        weight_ref[0:BLOCK, :] = own_ref[...]
        for side, ref in enumerate(chip_refs):
            start = pl.multiple_of(meta_ref[side] * QUARTER, QUARTER)
            for index in range(DEPTH - 1):
                for b in range(2):
                    weight_ref[(index + 1) * BLOCK : (index + 2) * BLOCK, pl.ds(start + b * BLOCK, BLOCK)] = ref[
                        index, b * BLOCK : (b + 1) * BLOCK, :
                    ]
        half = weight_ref.shape[0] // 2

        def share(part):
            return dot_nn(a_ref[part], weight_ref[:half, :]) + dot_nn(b_ref[part], weight_ref[half:, :])

        near_ref[...] = share(0)
        across = share(1).astype(jnp.bfloat16)
        low_ref[...] = across[:, : width // 2]
        high_ref[...] = across[:, width // 2 :]

    views = tuple(chip.reshape(DEPTH - 1, 4 * QUARTER, BLOCK) for chip in chips)
    view_spec = pl.BlockSpec((DEPTH - 1, QUARTER, BLOCK), lambda i, m: (0, 3, 0))
    out = [shape_of(rows, width, dtype=jnp.float32)] + [shape_of(rows, width // 2)] * 2
    return kernel_call(
        body, "attention_out", meta, tuple(attended) + (w_out,) + views,
        [whole(a) for a in attended] + [pl.BlockSpec((BLOCK, width), lambda i, m: (m[OWN_CORE], 0))] + [view_spec] * CHIPS,
        out, [whole(o) for o in out], scratch=[pltpu.VMEM((DEPTH * BLOCK, width), jnp.bfloat16)],
    )


def attention_norm(meta, near, low, high, tokens, vectors):
    rows, width = tokens.shape

    def body(meta_ref, near_ref, low_ref, high_ref, tokens_ref, vec_ref, hidden_ref, branch_ref, normed_ref):
        got = jnp.concatenate([low_ref[...], high_ref[...]], axis=1).astype(jnp.float32)
        branch = near_ref[...] + got + vec_ref[BIAS_OUT : BIAS_OUT + 1]
        branch_ref[...] = branch
        hidden = tokens_ref[...].astype(jnp.float32) + vec_ref[SCALE_ATTN : SCALE_ATTN + 1] * branch
        hidden_ref[...] = hidden
        unit, _ = normalized(hidden)
        normed = (unit * vec_ref[GAIN_TWO : GAIN_TWO + 1] + vec_ref[SHIFT_TWO : SHIFT_TWO + 1]).astype(jnp.bfloat16)
        normed_ref[...] = normed

    args = (near, low, high, tokens, vectors)
    out = [shape_of(rows, width, dtype=jnp.float32)] * 2 + [shape_of(rows, width)]
    return kernel_call(body, "attention_norm", meta, args, [whole(a) for a in args], out, [whole(o) for o in out], vmem=NORM_BYTES)


def feed_rows(normed_pieces, grad, up_weight, down_weight, bias, act_ref, gup_ref, low, high):
    width = up_weight.shape[0]
    deep = width // len(normed_pieces)
    pre = bias[:, low:high] + sum(
        dot_nn(piece[...], up_weight[k * deep : (k + 1) * deep, low:high]) for k, piece in enumerate(normed_pieces)
    )
    spread = 0.5 * (1.0 + lax.erf(pre * (1.0 / math.sqrt(2.0))))
    act_ref[:, low:high] = (pre * spread).astype(jnp.bfloat16)
    slope = spread + pre * jnp.exp(-0.5 * pre * pre) * (1.0 / math.sqrt(2.0 * math.pi))
    grad_up = (dot_nt(grad[...], down_weight[low:high, :]) * slope).astype(jnp.bfloat16)
    gup_ref[:, low:high] = grad_up
    return jnp.sum(grad_up.astype(jnp.float32), axis=0, keepdims=True)


def feed_near(meta, normed, grads, w_up, w_down, bias_up, chips):
    rows, width = grads[0].shape
    normed = [part if isinstance(part, (list, tuple)) else [part] for part in normed]
    flat = [piece for part in normed for piece in part]
    half_u = w_up.shape[1] // 2
    n_u = half_u // BLOCK
    count = len(normed)
    copies = len(flat) + count + 2 + CHIPS * (n_u + 2)

    def body(meta_ref, *refs):
        bias_ref, flat_hbm, refs = refs[0], refs[1 : 1 + len(flat)], refs[1 + len(flat) :]
        grad_hbm, refs = refs[:count], refs[count:]
        up_hbm, down_hbm, chip_refs, refs = refs[0], refs[1], refs[2 : 2 + CHIPS], refs[2 + CHIPS :]
        act_refs, gup_refs, back_refs, refs = refs[:count], refs[count : 2 * count], refs[2 * count : 3 * count], refs[3 * count :]
        sum_ref, up_weight, down_weight, normed_ref, grad_ref, sems = refs
        half = pl.ds(pl.multiple_of(meta_ref[OWN_CORE] * half_u, half_u), half_u)
        pieces = []
        for part, cut in enumerate(normed):
            deep = width // len(cut)
            for k in range(len(cut)):
                pieces.append((part, (flat_hbm[len(pieces)], normed_ref.at[part, :, pl.ds(k * deep, deep)])))
        moves = [move for part, move in pieces if part == 0]
        moves += [
            (up_hbm.at[:, half], up_weight.at[:, pl.ds(0, half_u)]),
            (grad_hbm[0], grad_ref.at[0]),
            (down_hbm.at[half, :], down_weight.at[pl.ds(0, half_u), :]),
        ]
        for part in range(1, count):
            moves += [move for owner, move in pieces if owner == part] + [(grad_hbm[part], grad_ref.at[part])]
        near_moves = len(moves)
        for side, ref in enumerate(chip_refs):
            start = pl.multiple_of(meta_ref[side] * QUARTER, QUARTER)
            for b in range(n_u):
                moves.append(
                    (
                        ref.at[pl.ds(b * QUARTER, QUARTER), :],
                        up_weight.at[pl.ds(start, QUARTER), pl.ds(half_u + b * BLOCK, BLOCK)],
                    )
                )
            for b in range(2):
                moves.append(
                    (
                        ref.at[pl.ds(n_u * QUARTER + b * half_u, half_u), :],
                        down_weight.at[pl.ds(half_u, half_u), pl.ds(start + b * BLOCK, BLOCK)],
                    )
                )
        handles = [pltpu.make_async_copy(source, target, sems.at[k]) for k, (source, target) in enumerate(moves)]
        for handle in handles:
            handle.start()
        for tile, waits in enumerate((handles[:near_moves], handles[near_moves:])):
            for handle in waits:
                handle.wait()
            low, high = tile * half_u, (tile + 1) * half_u
            sums = [
                feed_rows([normed_ref.at[p]], grad_ref.at[p], up_weight, down_weight, bias_ref, act_refs[p], gup_refs[p], low, high)
                for p in range(count)
            ]
            sum_ref[:, low:high] = sum(sums)
        for part in range(count):
            back_refs[part][...] = dot_nt(gup_refs[part][...], up_weight[...]).astype(jnp.bfloat16)

    anywhere = pl.BlockSpec(memory_space=pl.ANY)
    out = [shape_of(rows, 2 * half_u)] * (2 * count) + [shape_of(rows, width)] * count
    out += [shape_of(1, 2 * half_u, dtype=jnp.float32), shape_of(width, 2 * half_u), shape_of(2 * half_u, width)]
    args = tuple(flat) + tuple(grads) + (w_up, w_down) + tuple(chips)
    outs = kernel_call(
        body, "feed_near", meta, (bias_up,) + args, [whole(bias_up)] + [anywhere] * len(args), out, [whole(o) for o in out],
        scratch=[pltpu.VMEM((count, rows, width), jnp.bfloat16)] * 2 + [pltpu.SemaphoreType.DMA((copies,))],
        vmem=NEAR_BYTES,
    )
    return outs[:count], outs[count : 2 * count], outs[2 * count : 3 * count], outs[3 * count], outs[3 * count + 1], outs[3 * count + 2]


def feed_far(meta, normed, grad, bias_up, full_up, full_down):
    rows, width = grad.shape
    units = full_up.shape[1]
    pieces = len(normed)

    def body(meta_ref, *refs):
        normed_refs = refs[:pieces]
        grad_ref, bias_ref, up_ref, down_ref, act_ref, gup_ref, back_ref, sum_ref = refs[pieces:]
        for tile in range(2):
            low, high = tile * units // 2, (tile + 1) * units // 2
            sum_ref[:, low:high] = feed_rows(
                normed_refs, grad_ref, up_ref, down_ref, bias_ref, act_ref, gup_ref, low, high
            )
        back_ref[...] = dot_nt(gup_ref[...], up_ref[...]).astype(jnp.bfloat16)

    args = tuple(normed) + (grad, bias_up, full_up, full_down)
    out = [shape_of(rows, units)] * 2 + [shape_of(rows, width), shape_of(1, units, dtype=jnp.float32)]
    return kernel_call(body, "feed_far", meta, args, [whole(a) for a in args], out, [whole(o) for o in out])


def feed_down(meta, acts, full_down):
    rows, width = acts[0].shape[0], full_down.shape[1]
    count = len(acts)

    def body(meta_ref, *refs):
        weight_ref = refs[count]
        for act_ref, out_ref in zip(refs[:count], refs[count + 1 :]):
            out_ref[...] = dot_nn(act_ref[...], weight_ref[...]).astype(jnp.bfloat16)

    args = tuple(acts) + (full_down,)
    out = [shape_of(rows, width)] * count
    return kernel_call(body, "feed_down", meta, args, [whole(a) for a in args], out, [whole(o) for o in out])


def put_sides(lane, values, keep_ref, send_ref, at):
    keep, send = ((0, 2), (1, 3)) if lane == 0 else ((0, 1), (2, 3))
    for ref, sides in ((keep_ref, keep), (send_ref, send)):
        for index, side in enumerate(sides):
            ref[index * QUARTER : (index + 1) * QUARTER, at] = values[side * QUARTER : (side + 1) * QUARTER].astype(
                jnp.bfloat16
            )


def feed_gradients(meta, normed, turned_grads, gups, acts):
    normed = [part if isinstance(part, (list, tuple)) else [part] for part in normed]
    flat = [piece for part in normed for piece in part]
    rows = flat[0].shape[0]
    width = turned_grads[0].shape[0]
    half_u = gups[0].shape[1] // 2
    n = len(gups)

    def body(meta_ref, *refs):
        normed_refs, refs = refs[: len(flat)], refs[len(flat) :]
        turned_refs, gup_refs, act_refs, refs = refs[:n], refs[n : 2 * n], refs[2 * n : 3 * n], refs[3 * n :]
        outs, own_turned, whole_ref = refs[:4], refs[4:-1], refs[-1]
        step = pl.program_id(0)

        @pl.when(step == 0)
        def _():
            at = 0
            for part, target in zip(normed, own_turned):
                if len(part) == 1:
                    turn_into(meta_ref, normed_refs[at], target)
                else:
                    deep = width // len(part)
                    for k in range(len(part)):
                        whole_ref[:, k * deep : (k + 1) * deep] = normed_refs[at + k][...]
                    turn_into(meta_ref, whole_ref, target)
                at += len(part)

        def product(lefts, rights):
            return sum(dot_nn(left[...], right[...]) for left, right in zip(lefts, rights))

        for lane in range(2):
            kept, sent = outs[2 * lane : 2 * lane + 2]

            @pl.when(step == 2 * lane)
            def _():
                put_sides(lane, product(own_turned, gup_refs), kept, sent, slice(None))

            @pl.when(step == 2 * lane + 1)
            def _():
                put_sides(lane, product(turned_refs, act_refs), kept, sent, slice(None))

    args = tuple(flat) + tuple(turned_grads)
    by_lane = [pl.BlockSpec((rows, half_u), lambda g, m: (0, g >> 1))] * (2 * n)
    out_specs = [pl.BlockSpec((2 * QUARTER, half_u), lambda g, m: (0, jnp.minimum(g, 1)))] * 2
    out_specs += [pl.BlockSpec((2 * QUARTER, half_u), lambda g, m: (0, jnp.maximum(g - 2, 0)))] * 2
    outs = kernel_call(
        body, "feed_gradients", meta, args + tuple(gups) + tuple(acts),
        [whole(a) for a in args] + by_lane, [shape_of(2 * QUARTER, 2 * half_u)] * 4, out_specs, grid=(4,),
        scratch=[pltpu.VMEM((width, rows), jnp.bfloat16)] * 4 + [pltpu.VMEM((rows, width), jnp.bfloat16)],
    )
    return outs[:2], outs[2:]


def hidden_gradient(meta, backs, hidden, branch, cotangent, vectors):
    rows, width = hidden.shape

    def body(meta_ref, *refs):
        back_refs, (hidden_ref, branch_ref, cot_ref, vec_ref, dh_ref, e1_ref, sum_ref) = refs[: len(backs)], refs[len(backs) :]
        grad = sum(ref[...].astype(jnp.float32) for ref in back_refs)
        unit, inverse = normalized(hidden_ref[...])
        sum_ref[0:1, :] = jnp.sum(grad * unit, axis=0, keepdims=True)
        sum_ref[1:2, :] = jnp.sum(grad, axis=0, keepdims=True)
        total = valid_column(meta_ref, rows) * cot_ref[...].astype(jnp.float32) + norm_gradient(
            unit, inverse, vec_ref[GAIN_TWO : GAIN_TWO + 1], grad
        )
        dh_ref[...] = total
        sum_ref[2:3, :] = jnp.sum(total * branch_ref[...], axis=0, keepdims=True)
        scaled = vec_ref[SCALE_ATTN : SCALE_ATTN + 1] * total
        sum_ref[3:4, :] = jnp.sum(scaled, axis=0, keepdims=True)
        e1_ref[...] = scaled.astype(jnp.bfloat16)

    args = tuple(backs) + (hidden, branch, cotangent, vectors)
    out = [shape_of(rows, width, dtype=jnp.float32), shape_of(rows, width), shape_of(4, width, dtype=jnp.float32)]
    return kernel_call(body, "hidden_gradient", meta, args, [whole(a) for a in args], out, [whole(o) for o in out])


def attention_backward(meta, qkv, probs, attended, grads, turned_normed, w_out, chips, lane):
    rows, width = grads[0].shape
    group = 3 * BLOCK
    ranges = crop_ranges(rows)
    groups = DEPTH // 2
    scale = 1.0 / math.sqrt(DH)
    base = lane * groups

    def body(meta_ref, qkv_ref, prob_ref, mixed_ref, e1_ref, e1_other_ref, n_ref, n_other_ref, own_ref, *refs):
        chip_refs, (out_ref, keep_ref, send_ref, weight_ref, grad_ref, turned_e, turned_other) = refs[:CHIPS], refs[CHIPS:]
        step = pl.program_id(0)

        @pl.when(step == 0)
        def _():
            turn_into(meta_ref, e1_ref, turned_e)
            turn_into(meta_ref, e1_other_ref, turned_other)

        def far_weights():
            for side, ref in enumerate(chip_refs):
                start = pl.multiple_of(meta_ref[side] * QUARTER, QUARTER)
                for b in range(2):
                    weight_ref[:, pl.ds(start + b * BLOCK, BLOCK)] = ref[0, b * BLOCK : (b + 1) * BLOCK, :]

        if lane == 0:
            @pl.when(step == 0)
            def _():
                weight_ref[...] = own_ref[...]

            pl.when(step > 0)(far_weights)
        else:
            far_weights()
        for part, ref in enumerate((e1_ref, e1_other_ref)):
            grad_ref[part] = dot_nt(ref[...], weight_ref[...]).astype(jnp.bfloat16)
        for part in range(2):
            for index, (low, high, skip) in enumerate(ranges):
                size = high - low
                query = qkv_ref[part, low:high, 0:BLOCK]
                key = qkv_ref[part, low:high, BLOCK : 2 * BLOCK]
                value = qkv_ref[part, low:high, 2 * BLOCK : 3 * BLOCK]
                grad = grad_ref[part, low:high, :]
                lane_of = lax.broadcasted_iota(jnp.int32, (size, BLOCK), 1)
                row = lax.broadcasted_iota(jnp.int32, (size, BLOCK), 0)
                parts = []
                for head in range(2):
                    own = (lane_of < DH) if head == 0 else (lane_of >= DH)
                    low_probs = prob_ref[0, part, index, head, 0:size, 0:size]
                    grad_value = dot_tn(low_probs, grad)
                    grad_probs = dot_nt(jnp.where(own, grad, jnp.zeros_like(grad)), value)
                    wide = low_probs.astype(jnp.float32)
                    weighted = wide * grad_probs
                    inner = jnp.sum(weighted, axis=1, keepdims=True)
                    grad_scores = (weighted - wide * inner).astype(jnp.bfloat16)
                    parts.append(
                        (dot_nn(grad_scores, key) * scale, dot_tn(grad_scores, query) * scale, grad_value)
                    )
                for which in range(3):
                    at = slice(which * BLOCK, (which + 1) * BLOCK)
                    joined = jnp.where(lane_of < DH, parts[0][which], parts[1][which]).astype(jnp.bfloat16)
                    if skip:
                        joined = jnp.where(row >= skip, joined, out_ref[part, low:high, at])
                    out_ref[part, low:high, at] = joined
        both = dot_nn(n_ref[...], out_ref[0]) + dot_nn(n_other_ref[...], out_ref[1])
        put_sides(lane, both, keep_ref, send_ref, slice(0, group))
        both = dot_nn(turned_e[...], mixed_ref[0]) + dot_nn(turned_other[...], mixed_ref[1])
        put_sides(lane, both, keep_ref, send_ref, slice(group, group + BLOCK))

    views = tuple(chip.reshape(DEPTH - 1, 4 * QUARTER, BLOCK) for chip in chips)
    args = (qkv, probs, attended) + tuple(grads) + tuple(turned_normed) + (w_out,) + views
    return kernel_call(
        body,
        "attention_backward",
        meta,
        args,
        [
            pl.BlockSpec((2, rows, group), lambda g, m: (0, 0, g)),
            pl.BlockSpec((1,) + probs.shape[1:], lambda g, m: (g, 0, 0, 0, 0, 0)),
            pl.BlockSpec((2, rows, BLOCK), lambda g, m: (0, 0, g)),
            whole(grads[0]),
            whole(grads[1]),
            whole(turned_normed[0]),
            whole(turned_normed[1]),
            pl.BlockSpec((BLOCK, width), lambda g, m: (m[OWN_CORE], 0)),
        ]
        + [pl.BlockSpec((1, QUARTER, BLOCK), lambda g, m: (jnp.maximum(base + g - 1, 0), 3, 0))] * CHIPS,
        [shape_of(2, rows, groups * group)] + [shape_of(width // 2, groups * 4 * BLOCK)] * 2,
        [pl.BlockSpec((2, rows, group), lambda g, m: (0, 0, g))]
        + [pl.BlockSpec((width // 2, 4 * BLOCK), lambda g, m: (0, g))] * 2,
        grid=(groups,),
        scratch=[
            pltpu.VMEM((BLOCK, width), jnp.bfloat16),
            pltpu.VMEM((2, rows, BLOCK), jnp.bfloat16),
            pltpu.VMEM((width, rows), jnp.bfloat16),
            pltpu.VMEM((width, rows), jnp.bfloat16),
        ],
    )


def token_shares(meta, grads, w_query, w_key, w_value, chips):
    rows = grads[0].shape[1]
    width = w_query.shape[0]
    group = 3 * BLOCK

    def body(meta_ref, low_ref, high_ref, q_ref, k_ref, v_ref, *refs):
        chip_refs, (near_ref, left_ref, right_ref, bias_ref, weight_ref, total_ref) = refs[:CHIPS], refs[CHIPS:]
        step = pl.program_id(0)

        @pl.when(step == 0)
        def _():
            for which, ref in enumerate((q_ref, k_ref, v_ref)):
                weight_ref[:, which * BLOCK : (which + 1) * BLOCK] = ref[...]

        @pl.when(step > 0)
        def _():
            fill_heads(meta_ref, chip_refs, weight_ref)

        def add(ref):
            sums = jnp.sum(ref[0].astype(jnp.float32), axis=0, keepdims=True)
            bias_ref[0] = sums + jnp.sum(ref[1].astype(jnp.float32), axis=0, keepdims=True)
            for part in range(2):
                share = dot_nt(ref[part], weight_ref[...])

                @pl.when(step == 0)
                def _():
                    total_ref[part] = share

                @pl.when(step > 0)
                def _():
                    total_ref[part] += share

        pl.when(step < 2)(lambda: add(low_ref))
        pl.when(step >= 2)(lambda: add(high_ref))

        @pl.when(step == DEPTH - 1)
        def _():
            near_ref[...] = total_ref[0]
            left_ref[...] = total_ref[1, :, : width // 2].astype(jnp.bfloat16)
            right_ref[...] = total_ref[1, :, width // 2 :].astype(jnp.bfloat16)

    own_specs, far_specs = head_specs(width, chips)
    out = [shape_of(rows, width, dtype=jnp.float32)] + [shape_of(rows, width // 2)] * 2
    return kernel_call(
        body,
        "token_shares",
        meta,
        tuple(grads) + (w_query, w_key, w_value) + tuple(chips),
        [
            pl.BlockSpec((2, rows, group), lambda g, m: (0, 0, jnp.minimum(g, 1))),
            pl.BlockSpec((2, rows, group), lambda g, m: (0, 0, jnp.maximum(g - 2, 0))),
        ]
        + own_specs
        + far_specs,
        out + [shape_of(DEPTH, 1, group, dtype=jnp.float32)],
        [whole(o) for o in out] + [pl.BlockSpec((1, 1, group), lambda g, m: (g, 0, 0))],
        grid=(DEPTH,),
        scratch=[pltpu.VMEM((width, group), jnp.bfloat16), pltpu.VMEM((2, rows, width), jnp.float32)],
    )


def token_gradient(meta, near, left, right, tokens, dh, vectors):
    rows, width = tokens.shape

    def body(meta_ref, near_ref, left_ref, right_ref, tokens_ref, dh_ref, vec_ref, out_ref, sum_ref):
        got = jnp.concatenate([left_ref[...], right_ref[...]], axis=1).astype(jnp.float32)
        grad = near_ref[...] + got
        unit, inverse = normalized(tokens_ref[...].astype(jnp.float32))
        sum_ref[0:1, :] = jnp.sum(grad * unit, axis=0, keepdims=True)
        sum_ref[1:2, :] = jnp.sum(grad, axis=0, keepdims=True)
        out_ref[...] = dh_ref[...] + norm_gradient(unit, inverse, vec_ref[GAIN_ONE : GAIN_ONE + 1], grad)

    args = (near, left, right, tokens, dh, vectors)
    out = [shape_of(rows, width, dtype=jnp.float32), shape_of(2, width, dtype=jnp.float32)]
    return kernel_call(body, "token_gradient", meta, args, [whole(a) for a in args], out, [whole(o) for o in out])


def layer_result(meta, downs, hidden, cotangent, vectors):
    rows, width = hidden.shape

    def body(meta_ref, *refs):
        down_refs, (hidden_ref, cot_ref, vec_ref, out_ref, sum_ref) = refs[: len(downs)], refs[len(downs) :]
        branch = sum(ref[...].astype(jnp.float32) for ref in down_refs) + vec_ref[BIAS_DOWN : BIAS_DOWN + 1]
        valid = valid_column(meta_ref, rows)
        out_ref[...] = valid * (hidden_ref[...] + vec_ref[SCALE_MLP : SCALE_MLP + 1] * branch)
        sum_ref[...] = jnp.sum(valid * cot_ref[...].astype(jnp.float32) * branch, axis=0, keepdims=True)

    args = tuple(downs) + (hidden, cotangent, vectors)
    out = [shape_of(rows, width, dtype=jnp.float32), shape_of(1, width, dtype=jnp.float32)]
    return kernel_call(body, "layer_result", meta, args, [whole(a) for a in args], out, [whole(o) for o in out])


def pack_small(meta, wide, sums_qkv, sums_up):
    lines = wide[0].shape[1] // BLOCK
    n_u = sums_up[0].shape[1] // 2 // BLOCK
    share = 2 + n_u
    rows = sum(value.shape[0] for value in wide) * lines
    total = rows + 2 * DEPTH * share

    def body(meta_ref, *refs):
        wide_refs, qkv_ref, up_refs, out_ref = refs[: len(wide)], refs[len(wide)], refs[len(wide) + 1 : -1], refs[-1]
        at = 0
        for ref in wide_refs:
            for index in range(ref.shape[0]):
                for k in range(lines):
                    out_ref[at : at + 1, :] = ref[index : index + 1, k * BLOCK : (k + 1) * BLOCK]
                    at += 1
        out_ref[rows:, :] = jnp.zeros((total - rows, BLOCK), jnp.float32)
        core, level = meta_ref[OWN_CORE], meta_ref[OWN_LEVEL]
        for index in range(DEPTH):
            start = rows + core * (DEPTH * share) + (level ^ index) * share
            out_ref[pl.ds(start, 1), :] = qkv_ref[index, :, 0:BLOCK]
            out_ref[pl.ds(start + 1, 1), :] = qkv_ref[index, :, 2 * BLOCK : 3 * BLOCK]
            if index in (0, 2):
                for k in range(n_u):
                    column = (index // 2 * n_u + k) * BLOCK
                    out_ref[pl.ds(start + 2 + k, 1), :] = sum(ref[:, column : column + BLOCK] for ref in up_refs)

    args = tuple(wide) + (sums_qkv,) + tuple(sums_up)
    out = shape_of(total, BLOCK, dtype=jnp.float32)
    return kernel_call(body, "pack_small", meta, args, [whole(a) for a in args], out, whole(out))


def finish(meta, mine, other, kinds, name):
    width = CHIPS * QUARTER

    def body(meta_ref, mine_ref, other_ref, *outs):
        core = meta_ref[OWN_CORE]
        for ref, half in ((mine_ref, core), (other_ref, 1 - core)):
            at = 0
            for out_ref, (units, turned) in zip(outs, kinds):
                values = ref[0, :, at : at + units].astype(jnp.float32)
                place = pl.ds(pl.multiple_of(half * units, units), units)
                if turned:
                    out_ref[place, :] = values.T
                else:
                    out_ref[:, place] = values
                at += units

    side = pl.BlockSpec((1,) + mine.shape[1:], lambda j, m: (j, 0, 0))
    out, specs = [], []
    for units, turned in kinds:
        shape = (2 * units, width) if turned else (width, 2 * units)
        block = (2 * units, QUARTER) if turned else (QUARTER, 2 * units)
        out.append(shape_of(*shape, dtype=jnp.float32))
        specs.append(pl.BlockSpec(block, (lambda j, m: (0, m[j])) if turned else (lambda j, m: (m[j], 0))))
    return kernel_call(body, name, meta, (mine, other), [side, side], out, specs, grid=(CHIPS,))


def local_paired(
    tokens,
    slide_tiles,
    norm1_gain,
    norm1_bias,
    w_query,
    b_query,
    w_key,
    w_value,
    b_value,
    w_out,
    b_out,
    scale_attn,
    norm2_gain,
    norm2_bias,
    w_up,
    b_up,
    w_down,
    b_down,
    scale_mlp,
    cotangent,
):
    row_count, width = tokens.shape
    half_u = w_up.shape[1] // 2
    here = lax.axis_index("dp")
    level = lax.axis_index("mp")
    crops_here = row_count // L
    per_slide = CROPS_DEV // SLIDES_DEV
    crop = level * crops_here + jnp.arange(crops_here, dtype=jnp.int32)
    owner = (crop // per_slide)[:, None] == jnp.arange(SLIDES_DEV, dtype=jnp.int32)[None, :]
    limit = jnp.sum(jnp.where(owner, slide_tiles[None, :], 0), axis=1)
    valid = (crop % per_slide < limit).astype(jnp.int32)
    core = here & 1
    sides = jnp.stack([(here >> 1) ^ side for side in range(CHIPS)] + [core, level]).astype(jnp.int32)
    meta = jnp.concatenate([sides, valid])
    bias_q, bias_v, bias_u = [values.reshape(-1, BLOCK) for values in (b_query, b_value, b_up)]
    vectors = jnp.stack([norm1_gain, norm1_bias, norm2_gain, norm2_bias, scale_attn, scale_mlp, b_out, b_down])
    first, second = (X_SIDE, Y_SIDE), (Y_SIDE, X_SIDE)

    order = Order(meta)

    tokens_other = swap_plane(tokens, CORE_SIDE)
    slice_attn, slice_rest = order(slice_weights, w_query, w_key, w_value, w_out, w_up, w_down, bias_q, bias_v, bias_u)
    level_attn = [swap_depth(slice_attn, mask) for mask in (1, 2, 3)]
    one, one_other, grad, grad_b_down, one_turned, one_other_turned, grad_turned = order(
        prepare, tokens, tokens_other, cotangent, vectors
    )
    level_attn = order.land(*level_attn)
    far_attn = order.plain(lambda *parts: jnp.concatenate([part[: 4 * QUARTER] for part in parts], axis=0), *level_attn)
    attn_x, attn_y = swap_plane(far_attn, X_SIDE), swap_plane(far_attn, Y_SIDE)
    level_rest = swap_depth(order.hold(slice_rest), 2)
    n_u = half_u // BLOCK

    def unit_bias(rows, own):
        rows = rows[4 * QUARTER :].astype(jnp.float32)
        pair = (rows[2 : 2 + n_u] + rows[4 + n_u : 4 + 2 * n_u]).reshape(-1)
        return jnp.concatenate([lax.dynamic_slice_in_dim(own, core * half_u, half_u), pair])[None, :]

    bias_up = order.plain(unit_bias, level_attn[1], b_up)
    attn_x, attn_y = order.land(attn_x, attn_y)
    half = far_attn.shape[0] // 2
    low, high = order.hold((attn_y[:half], attn_x[half:]))
    low, high = swap_plane(low, X_SIDE), swap_plane(high, Y_SIDE)
    level_rest, low, high = order.land(level_rest, low, high)
    corner = order.plain(lambda *parts: jnp.concatenate(parts), low, high)
    chips_attn = [far_attn, attn_x, attn_y, corner]
    level_rest, grad, grad_far = order.hold((level_rest, grad, grad))
    plane_rest = plane_swaps(level_rest)
    grad_other = swap_plane(grad, CORE_SIDE)
    grad_far = swap_depth(grad_far, 1)
    low_qkv, low_attended, low_probs = order(
        attention_forward, one, one_other, w_query, w_key, w_value, bias_q, bias_v, level_attn, chips_attn, n_u, 0
    )
    high_qkv, high_attended, high_probs = order(
        attention_forward, one, one_other, w_query, w_key, w_value, bias_q, bias_v, level_attn, chips_attn, n_u, 1
    )
    grad_other, grad_far = order.land(grad_other, grad_far)
    out_near, *out_across = order(attention_out, (low_attended, high_attended), w_out, chips_attn)
    out_got = [swap_plane(part, CORE_SIDE) for part in out_across]
    plane_rest = order.land(*plane_rest)
    chips_rest = [level_rest] + plane_rest
    hidden, branch, normed = order(attention_norm, out_near, *out_got, tokens, vectors)
    normed_far = swap_depth(normed, 1)
    normed_other = swap_plane(normed, CORE_SIDE)
    grad_far_other = swap_plane(order.hold(grad_far), CORE_SIDE)

    *near, full_up, full_down = order(
        feed_near, (normed, normed_other), (grad, grad_other), w_up, w_down, bias_up, chips_rest
    )
    (normed_far,) = order.land(normed_far)
    normed_far, back_near = order.hold((normed_far, near[2][1]))
    normed_far_other = swap_plane(normed_far, CORE_SIDE)
    back_near = swap_plane(back_near, CORE_SIDE)
    far = order(feed_far, (normed_far,), grad_far, bias_up, full_up, full_down)
    far_other = order(feed_far, (normed_far_other,), grad_far_other, bias_up, full_up, full_down)
    acts, gups, backs = [list(a) + [b, c] for a, b, c in zip(near[:3], far[:3], far_other[:3])]
    back_got, back_near = order.land(swap_plane(backs[3], CORE_SIDE), back_near)
    back_far = swap_depth(order.plain(add_low, backs[2], back_got), 1)
    grads_turned = [grad_turned] + list(order(turn, grad_other, grad_far, grad_far_other))
    rest_sides = order(
        feed_gradients, (normed, normed_other, normed_far, normed_far_other), grads_turned, gups, acts
    )
    downs = order(feed_down, acts, full_down)
    down_near, down_far = swap_plane(downs[1], CORE_SIDE), swap_plane(downs[3], CORE_SIDE)
    (back_far,) = order.land(back_far)
    rest_sent = order.hold([sent for _, sent in rest_sides])
    rest_got = [swap_plane(sent, side) for sent, side in zip(rest_sent, first)]
    dh, e1, sums_two = order(
        hidden_gradient, (backs[0], back_near, back_far), hidden, branch, cotangent, vectors
    )
    e1_other = swap_plane(e1, CORE_SIDE)
    down_near, down_far = order.land(down_near, down_far)
    down_far = order(lambda meta, *parts: add_parts(meta, [(part, 0) for part in parts])[0], downs[2], down_far)
    (e1_other,) = order.land(e1_other)
    down_far = swap_depth(order.hold(down_far), 1)
    low_grads, low_kept, low_sent = order(
        attention_backward, low_qkv, low_probs, low_attended, (e1, e1_other), (one_turned, one_other_turned), w_out, chips_attn, 0
    )
    high_grads, high_kept, high_sent = order(
        attention_backward, high_qkv, high_probs, high_attended, (e1, e1_other), (one_turned, one_other_turned), w_out, chips_attn, 1
    )
    *rest_got, down_far = order.land(*rest_got, down_far)

    def onward(kept, got):
        return order(
            lambda meta, *args: add_parts(meta, *[((args[2 * k], QUARTER), (args[2 * k + 1], QUARTER)) for k in range(2)]),
            *[array for pair in zip(kept, got) for array in pair],
        )

    def arrived(kept, got, last):
        return order(
            lambda meta, *args: add_parts(meta, *[[(part, 0) for part in args[3 * k : 3 * k + 3]] for k in range(2)]),
            *[array for triple in zip(kept, got, last) for array in triple],
        )

    rest_kept = [kept for kept, _ in rest_sides]
    rest_sent = order.hold(onward(rest_kept, rest_got))
    rest_last = [swap_plane(sent, side) for sent, side in zip(rest_sent, second)]
    one_near, *one_across, sums_qkv = order(
        token_shares, (low_grads, high_grads), w_query, w_key, w_value, chips_attn
    )
    one_got = [swap_plane(part, CORE_SIDE) for part in one_across]
    *rest_last, one_got[0], one_got[1] = order.land(*rest_last, *one_got)
    rest_own, rest_pair = arrived(rest_kept, rest_got, rest_last)
    low_sent, high_sent, rest_pair = order.hold((low_sent, high_sent, rest_pair))
    attn_got = [swap_plane(sent, side) for sent, side in zip((low_sent, high_sent), first)]
    rest_pair = swap_depth(rest_pair, 2)
    layer_out, grad_scale_mlp = order(
        layer_result, (downs[0], down_near, down_far), hidden, cotangent, vectors
    )
    grad_tokens, sums_one = order(token_gradient, one_near, *one_got, tokens, dh, vectors)

    totals = order(
        pack_small, (sums_one, sums_two, grad_scale_mlp, grad_b_down), sums_qkv, (near[3], far[3], far_other[3])
    )
    totals_got = swap_plane(totals, X_SIDE)
    *attn_got, rest_pair, totals_got = order.land(*attn_got, rest_pair, totals_got)
    attn_kept = (low_kept, high_kept)
    attn_sent = onward(attn_kept, attn_got)
    attn_last = [swap_plane(sent, side) for sent, side in zip(attn_sent, second)]
    grad_rest = order(lambda meta, *parts: add_parts(meta, [(part, 0) for part in parts])[0], rest_own, rest_pair)

    totals = order.plain(jnp.add, totals, totals_got)
    totals_got = swap_plane(totals, Y_SIDE)
    *attn_last, totals_got = order.land(*attn_last, totals_got)
    own_piece, pair_piece, level_sent = order(level_pieces, attn_kept, attn_got, attn_last)
    level_got = swap_depth(level_sent, 1)
    totals = order.plain(jnp.add, totals, totals_got)
    totals_got, grad_rest = order.hold((totals, grad_rest))
    rest_x, rest_y = swap_plane(grad_rest, X_SIDE), swap_plane(grad_rest, Y_SIDE)
    totals_got = swap_depth(totals_got, 1)
    level_got, rest_x, rest_y, totals_got = order.land(level_got, rest_x, rest_y, totals_got)
    level_kept, level_sent = order.plain(
        lambda own, pair, got: (add_low(own, got[0]), add_low(pair, got[1])), own_piece, pair_piece, level_got
    )
    totals = order.plain(jnp.add, totals, totals_got)
    totals_got, grad_rest, level_sent = order.hold((totals, grad_rest, level_sent))
    level_got = swap_depth(level_sent, 2)
    rest_corner = swap_plane(grad_rest, X_SIDE | Y_SIDE)
    totals_got = swap_depth(totals_got, 2)
    level_got, rest_corner, totals_got = order.land(level_got, rest_corner, totals_got)
    grad_attn = order.plain(add_low, level_kept, level_got)
    totals = order.plain(jnp.add, totals, totals_got)
    plane_attn = plane_swaps(order.hold(grad_attn))
    totals_got = swap_plane(order.hold(totals), CORE_SIDE)
    rest_mine = order.plain(lambda *parts: jnp.stack(parts), grad_rest, rest_x, rest_y, rest_corner)
    rest_other = swap_plane(order.hold(rest_mine), CORE_SIDE)
    (rest_other,) = order.land(rest_other)
    full_grad_up, full_grad_down = order(
        finish, rest_mine, rest_other, ((half_u, False), (half_u, True)), "finish_rest"
    )
    *plane_attn, totals_got = order.land(*plane_attn, totals_got)
    attn_mine = order.plain(lambda *parts: jnp.stack(parts), grad_attn, *plane_attn)
    attn_other = swap_plane(order.hold(attn_mine), CORE_SIDE)
    totals = order.plain(jnp.add, totals, totals_got)
    (attn_other,) = order.land(attn_other)
    full_grad_q, full_grad_k, full_grad_v, full_grad_o = order(
        finish, attn_mine, attn_other, ((BLOCK, False),) * 3 + ((BLOCK, True),), "finish_attn"
    )
    lines = width // BLOCK
    small_total = totals[: 8 * lines].reshape(8, width)
    shared_total = totals[8 * lines :].reshape(2, DEPTH, -1)
    shared_total = lax.dynamic_index_in_dim(shared_total, level, 1, keepdims=False)
    return (
        layer_out,
        grad_tokens,
        small_total[0],
        small_total[1],
        full_grad_q,
        shared_total[:, :BLOCK].reshape(-1),
        full_grad_k,
        full_grad_v,
        shared_total[:, BLOCK : 2 * BLOCK].reshape(-1),
        full_grad_o,
        small_total[5],
        small_total[4],
        small_total[2],
        small_total[3],
        full_grad_up,
        shared_total[:, 2 * BLOCK :].reshape(-1),
        full_grad_down,
        small_total[7],
        small_total[6],
    )


def local_general(
    tokens,
    slide_tiles,
    norm1_gain,
    norm1_bias,
    w_query,
    b_query,
    w_key,
    w_value,
    b_value,
    w_out,
    b_out,
    scale_attn,
    norm2_gain,
    norm2_bias,
    w_up,
    b_up,
    w_down,
    b_down,
    scale_mlp,
    cotangent,
):
    row_count = tokens.shape[0]
    per_slide = CROPS_DEV // SLIDES_DEV
    crop_index = (lax.axis_index("mp") * row_count + jnp.arange(row_count, dtype=jnp.int32)) // L
    slide_index = crop_index // per_slide
    owner = slide_index[:, None] == jnp.arange(SLIDES_DEV, dtype=jnp.int32)[None, :]
    limit_rows = jnp.sum(jnp.where(owner, slide_tiles[None, :], 0), axis=1)
    valid_rows = (crop_index % per_slide < limit_rows).astype(jnp.float32)[:, None]
    inputs = tokens.astype(jnp.float32)
    normed_one = layer_norm(inputs, norm1_gain, norm1_bias).astype(jnp.bfloat16)
    rows_one = lax.all_gather(normed_one, "mp", axis=0, tiled=True)
    queries = (jnp.dot(rows_one, w_query, preferred_element_type=jnp.float32) + b_query).astype(
        jnp.bfloat16
    )
    keys_all = jnp.dot(rows_one, w_key, preferred_element_type=jnp.float32).astype(jnp.bfloat16)
    values_all = (jnp.dot(rows_one, w_value, preferred_element_type=jnp.float32) + b_value).astype(
        jnp.bfloat16
    )
    heads_here = w_query.shape[1] // DH
    query_heads = to_heads(queries, heads_here)
    key_heads = to_heads(keys_all, heads_here)
    value_heads = to_heads(values_all, heads_here)
    scores = attn_scores(query_heads, key_heads)
    top_score = jnp.max(scores, axis=-1, keepdims=True)
    log_total = top_score + jnp.log(jnp.sum(jnp.exp(scores - top_score), axis=-1, keepdims=True))
    weights_low = jnp.exp(scores - log_total).astype(jnp.bfloat16)
    mixed_heads = jnp.einsum(
        "chqk,ckhd->cqhd", weights_low, value_heads, preferred_element_type=jnp.float32
    )
    attended = mixed_heads.reshape(queries.shape).astype(jnp.bfloat16)
    attn_sum = lax.psum_scatter(
        jnp.dot(attended, w_out, preferred_element_type=jnp.float32).astype(jnp.bfloat16),
        "mp",
        scatter_dimension=0,
        tiled=True,
    ).astype(jnp.float32)
    branch_one = attn_sum + b_out
    hidden_state = inputs + scale_attn * branch_one
    normed_two = layer_norm(hidden_state, norm2_gain, norm2_bias).astype(jnp.bfloat16)
    rows_two = lax.all_gather(normed_two, "mp", axis=0, tiled=True)
    up_pre = jnp.dot(rows_two, w_up, preferred_element_type=jnp.float32) + b_up
    activated = gelu_exact(up_pre).astype(jnp.bfloat16)
    down_sum = lax.psum_scatter(
        jnp.dot(activated, w_down, preferred_element_type=jnp.float32).astype(jnp.bfloat16),
        "mp",
        scatter_dimension=0,
        tiled=True,
    ).astype(jnp.float32)
    branch_two = down_sum + b_down
    layer_out = valid_rows * (hidden_state + scale_mlp * branch_two)
    grad_out = valid_rows * cotangent.astype(jnp.float32)
    grad_scale_mlp = jnp.sum(grad_out * branch_two, axis=0)
    grad_branch_two = scale_mlp * grad_out
    grad_b_down = jnp.sum(grad_branch_two, axis=0)
    grad_down_low = grad_branch_two.astype(jnp.bfloat16)
    gelu_value, gelu_back = jax.vjp(gelu_exact, up_pre)
    grad_down_rows = lax.all_gather(grad_down_low, "mp", axis=0, tiled=True)
    grad_act = contract_cols(grad_down_rows, w_down)
    grad_up = gelu_back(grad_act)[0].astype(jnp.bfloat16)
    grad_w_up = contract_rows(rows_two, grad_up)
    grad_w_down = contract_rows(activated, grad_down_rows)
    grad_b_up = jnp.sum(grad_up.astype(jnp.float32), axis=0)
    grad_rows_two = lax.psum_scatter(
        contract_cols(grad_up, w_up).astype(jnp.bfloat16), "mp", scatter_dimension=0, tiled=True
    ).astype(jnp.float32)
    norm2_value, norm2_back = jax.vjp(layer_norm, hidden_state, norm2_gain, norm2_bias)
    grad_hidden_norm, grad_norm2_gain, grad_norm2_bias = norm2_back(grad_rows_two)
    grad_hidden = grad_out + grad_hidden_norm
    grad_scale_attn = jnp.sum(grad_hidden * branch_one, axis=0)
    grad_branch_one = scale_attn * grad_hidden
    grad_b_out = jnp.sum(grad_branch_one, axis=0)
    grad_attn_low = grad_branch_one.astype(jnp.bfloat16)
    grad_attn_rows = lax.all_gather(grad_attn_low, "mp", axis=0, tiled=True)
    grad_w_out = contract_rows(attended, grad_attn_rows)
    grad_mixed = contract_cols(grad_attn_rows, w_out).astype(jnp.bfloat16)
    grad_mixed_heads = to_heads(grad_mixed, heads_here)
    scores_again = attn_scores(query_heads, key_heads)
    probs = jnp.exp(scores_again - log_total)
    probs_low = probs.astype(jnp.bfloat16)
    grad_value_heads = jnp.einsum(
        "chqk,cqhd->ckhd", probs_low, grad_mixed_heads, preferred_element_type=jnp.float32
    )
    grad_values = grad_value_heads.reshape(queries.shape).astype(jnp.bfloat16)
    grad_probs = jnp.einsum(
        "cqhd,ckhd->chqk", grad_mixed_heads, value_heads, preferred_element_type=jnp.float32
    )
    row_inner = jnp.sum(probs * grad_probs, axis=-1, keepdims=True)
    grad_scores = (probs * (grad_probs - row_inner)).astype(jnp.bfloat16)
    inverse_root = 1.0 / math.sqrt(DH)
    grad_query_heads = jnp.einsum(
        "chqk,ckhd->cqhd", grad_scores, key_heads, preferred_element_type=jnp.float32
    )
    grad_queries = (inverse_root * grad_query_heads).reshape(queries.shape).astype(jnp.bfloat16)
    grad_key_heads = jnp.einsum(
        "chqk,cqhd->ckhd", grad_scores, query_heads, preferred_element_type=jnp.float32
    )
    grad_keys = (inverse_root * grad_key_heads).reshape(queries.shape).astype(jnp.bfloat16)
    grad_w_query = contract_rows(rows_one, grad_queries)
    grad_b_query = jnp.sum(grad_queries.astype(jnp.float32), axis=0)
    grad_w_key = contract_rows(rows_one, grad_keys)
    grad_w_value = contract_rows(rows_one, grad_values)
    grad_b_value = jnp.sum(grad_values.astype(jnp.float32), axis=0)
    grad_rows_one = lax.psum_scatter(
        (
            contract_cols(grad_queries, w_query)
            + contract_cols(grad_keys, w_key)
            + contract_cols(grad_values, w_value)
        ).astype(jnp.bfloat16),
        "mp",
        scatter_dimension=0,
        tiled=True,
    ).astype(jnp.float32)
    norm1_value, norm1_back = jax.vjp(layer_norm, inputs, norm1_gain, norm1_bias)
    grad_in_norm, grad_norm1_gain, grad_norm1_bias = norm1_back(grad_rows_one)
    grad_tokens = grad_hidden + grad_in_norm
    small_stack = jnp.stack(
        [
            grad_norm1_gain,
            grad_norm1_bias,
            grad_norm2_gain,
            grad_norm2_bias,
            grad_scale_attn,
            grad_scale_mlp,
            grad_b_out,
            grad_b_down,
        ],
        axis=1,
    )
    small_total = lax.psum(small_stack.astype(jnp.bfloat16), "mp")
    (
        share_wq,
        share_bq,
        share_wk,
        share_wv,
        share_bv,
        share_wo,
        share_up,
        share_bup,
        share_down,
        share_small,
    ) = (
        lax.psum_scatter(
            grad_w_query.astype(jnp.bfloat16), "dp", scatter_dimension=0, tiled=True
        ).astype(jnp.float32),
        lax.psum_scatter(
            grad_b_query.astype(jnp.bfloat16), "dp", scatter_dimension=0, tiled=True
        ).astype(jnp.float32),
        lax.psum_scatter(
            grad_w_key.astype(jnp.bfloat16), "dp", scatter_dimension=0, tiled=True
        ).astype(jnp.float32),
        lax.psum_scatter(
            grad_w_value.astype(jnp.bfloat16), "dp", scatter_dimension=0, tiled=True
        ).astype(jnp.float32),
        lax.psum_scatter(
            grad_b_value.astype(jnp.bfloat16), "dp", scatter_dimension=0, tiled=True
        ).astype(jnp.float32),
        lax.psum_scatter(
            grad_w_out.astype(jnp.bfloat16), "dp", scatter_dimension=0, tiled=True
        ).astype(jnp.float32),
        lax.psum_scatter(
            grad_w_up.astype(jnp.bfloat16), "dp", scatter_dimension=0, tiled=True
        ).astype(jnp.float32),
        lax.psum_scatter(
            grad_b_up.astype(jnp.bfloat16), "dp", scatter_dimension=0, tiled=True
        ).astype(jnp.float32),
        lax.psum_scatter(
            grad_w_down.astype(jnp.bfloat16), "dp", scatter_dimension=0, tiled=True
        ).astype(jnp.float32),
        lax.psum_scatter(small_total, "dp", scatter_dimension=0, tiled=True).astype(jnp.float32),
    )
    (
        full_wq,
        full_bq,
        full_wk,
        full_wv,
        full_bv,
        full_wo,
        full_up,
        full_bup,
        full_down,
        full_small,
    ) = (
        lax.all_gather(share_wq.astype(jnp.bfloat16), "dp", axis=0, tiled=True).astype(
            share_wq.dtype
        ),
        lax.all_gather(share_bq.astype(jnp.bfloat16), "dp", axis=0, tiled=True).astype(
            share_bq.dtype
        ),
        lax.all_gather(share_wk.astype(jnp.bfloat16), "dp", axis=0, tiled=True).astype(
            share_wk.dtype
        ),
        lax.all_gather(share_wv.astype(jnp.bfloat16), "dp", axis=0, tiled=True).astype(
            share_wv.dtype
        ),
        lax.all_gather(share_bv.astype(jnp.bfloat16), "dp", axis=0, tiled=True).astype(
            share_bv.dtype
        ),
        lax.all_gather(share_wo.astype(jnp.bfloat16), "dp", axis=0, tiled=True).astype(
            share_wo.dtype
        ),
        lax.all_gather(share_up.astype(jnp.bfloat16), "dp", axis=0, tiled=True).astype(
            share_up.dtype
        ),
        lax.all_gather(share_bup.astype(jnp.bfloat16), "dp", axis=0, tiled=True).astype(
            share_bup.dtype
        ),
        lax.all_gather(share_down.astype(jnp.bfloat16), "dp", axis=0, tiled=True).astype(
            share_down.dtype
        ),
        lax.all_gather(share_small.astype(jnp.bfloat16), "dp", axis=0, tiled=True).astype(
            share_small.dtype
        ),
    )
    return (
        layer_out,
        grad_tokens,
        full_small[:, 0],
        full_small[:, 1],
        full_wq,
        full_bq,
        full_wk,
        full_wv,
        full_bv,
        full_wo,
        full_small[:, 6],
        full_small[:, 4],
        full_small[:, 2],
        full_small[:, 3],
        full_up,
        full_bup,
        full_down,
        full_small[:, 7],
        full_small[:, 5],
    )


def solution(mesh):
    in_specs = (
        P(("dp", "mp"), None),
        P("dp"),
        P(),
        P(),
        P(None, "mp"),
        P("mp"),
        P(None, "mp"),
        P(None, "mp"),
        P("mp"),
        P("mp", None),
        P(),
        P(),
        P(),
        P(),
        P(None, "mp"),
        P("mp"),
        P("mp", None),
        P(),
        P(),
        P(("dp", "mp"), None),
    )
    out_specs = (
        P(("dp", "mp"), None),
        P(("dp", "mp"), None),
        P(),
        P(),
        P(None, "mp"),
        P("mp"),
        P(None, "mp"),
        P(None, "mp"),
        P("mp"),
        P("mp", None),
        P(),
        P(),
        P(),
        P(),
        P(None, "mp"),
        P("mp"),
        P("mp", None),
        P(),
        P(),
    )
    paired = mesh.shape["dp"] == 8 and mesh.shape["mp"] == 4
    local = local_paired if paired else local_general
    return jax.shard_map(local, mesh=mesh, in_specs=in_specs, out_specs=out_specs, check_vma=False)
```

```python
import functools
import math

import jax
import jax.numpy as jnp
from jax import lax
from jax.experimental import pallas as pl
from jax.experimental.pallas import tpu as pltpu
from jax.sharding import PartitionSpec as P

DH = 64
L = 197
SLIDES_DEV = 2
CROPS_DEV = 8


def layer_norm(values, gain, shift):
    average = jnp.mean(values, axis=-1, keepdims=True)
    centered = values - average
    spread = jnp.mean(centered * centered, axis=-1, keepdims=True)
    return centered * lax.rsqrt(spread + 1e-06) * gain + shift


def gelu_exact(values):
    return jax.nn.gelu(values, approximate=False)


def contract_rows(left, right):
    return lax.dot_general(
        left, right, (((0,), (0,)), ((), ())), preferred_element_type=jnp.float32
    )


def contract_cols(left, right):
    return lax.dot_general(
        left, right, (((1,), (1,)), ((), ())), preferred_element_type=jnp.float32
    )


def to_heads(matrix, heads_here):
    return matrix.reshape(matrix.shape[0] // L, L, heads_here, DH)


def attn_scores(query_heads, key_heads):
    product = jnp.einsum(
        "cqhd,ckhd->chqk", query_heads, key_heads, preferred_element_type=jnp.float32
    )
    return product * (1.0 / math.sqrt(DH))


BLOCK = 128
QUARTER = 256
X_SIDE, Y_SIDE, CORE_SIDE = 2, 4, 1
PLANE = 8
CHIPS = 4
DEPTH = 4
OWN_CORE = CHIPS
OWN_LEVEL = CHIPS + 1
FLAGS = CHIPS + 2
GAIN_ONE, SHIFT_ONE, GAIN_TWO, SHIFT_TWO, SCALE_ATTN, SCALE_MLP, BIAS_OUT, BIAS_DOWN = range(8)
VMEM_BYTES = 24 * 2**20
NEAR_BYTES = 28 * 2**20
PARTS_BYTES = 24 * 2**20
NORM_BYTES = 24 * 2**20
BACK_BYTES = 24 * 2**20
PIECES_BYTES = 24 * 2**20


def swap_plane(values, mask):
    return lax.ppermute(values, "dp", [(i, i ^ mask) for i in range(PLANE)])


def swap_depth(values, mask):
    return lax.ppermute(values, "mp", [(i, i ^ mask) for i in range(DEPTH)])


def plane_swaps(values):
    return [swap_plane(values, side) for side in (X_SIDE, Y_SIDE, X_SIDE | Y_SIDE)]


class Order:
    def __init__(self, meta):
        self.meta = meta

    def hold(self, values):
        leaves, tree = jax.tree.flatten(values)
        *leaves, self.meta = lax.optimization_barrier(tuple(leaves) + (self.meta,))
        return jax.tree.unflatten(tree, leaves)

    def land(self, *arrays):
        return self.hold(list(arrays))

    def __call__(self, step, *args):
        return self.hold(step(self.meta, *args))

    def plain(self, step, *args):
        return self.hold(step(*self.hold(args)))


def dot_nt(left, right):
    return lax.dot_general(left, right, (((1,), (1,)), ((), ())), preferred_element_type=jnp.float32)


def dot_tn(left, right):
    return lax.dot_general(left, right, (((0,), (0,)), ((), ())), preferred_element_type=jnp.float32)


def dot_nn(left, right):
    return lax.dot_general(left, right, (((1,), (0,)), ((), ())), preferred_element_type=jnp.float32)


def add_low(*values):
    return sum(value.astype(jnp.float32) for value in values).astype(jnp.bfloat16)


def crop_ranges(rows):
    ranges = []
    for crop in range(rows // L):
        low = crop * L // 16 * 16
        high = min((crop + 1) * L + 15, rows + 15) // 16 * 16
        ranges.append((low, min(high, rows), crop * L - low))
    return ranges


def add_parts(meta, *sums):
    rows = [len(parts) for parts in sums]
    flat = [part for parts in sums for part in parts]
    heights = [min(array.shape[0] - start for array, start in parts) for parts in sums]

    def body(meta_ref, *refs):
        at = 0
        for count, out_ref in zip(rows, refs[len(flat) :]):
            out_ref[...] = add_low(*[ref[...] for ref in refs[at : at + count]])
            at += count

    in_specs, out = [], []
    for parts, height in zip(sums, heights):
        for array, start in parts:
            in_specs.append(pl.BlockSpec((height, array.shape[1]), lambda i, m, b=start // height: (b, 0)))
        out.append(shape_of(height, parts[0][0].shape[1]))
    return kernel_call(
        body, "add_parts", meta, [array for array, _ in flat], in_specs, out, [whole(o) for o in out], vmem=PARTS_BYTES
    )


def level_pieces(meta, kept, got, last):
    half = kept[0].shape[1] // 2

    def body(meta_ref, *refs):
        own_ref, pair_ref, send_ref = refs[6:]
        for lane, near_ref in enumerate((own_ref, pair_ref)):
            total = add_low(*[ref[...] for ref in refs[3 * lane : 3 * lane + 3]])
            heads = 3 * half // 4
            near_ref[:, :heads] = total[:, :heads]
            near_ref[:, heads:] = total[:, 2 * heads : heads + half]
            send_ref[lane, :, :heads] = total[:, heads : 2 * heads]
            send_ref[lane, :, heads:] = total[:, heads + half :]

    first = pl.BlockSpec((QUARTER, 2 * half), lambda i, m: (0, 0))
    args = [array for triple in zip(kept, got, last) for array in triple]
    out = [shape_of(QUARTER, half)] * 2 + [shape_of(2, QUARTER, half)]
    return kernel_call(
        body, "level_pieces", meta, args, [first] * 6, out, [whole(o) for o in out], vmem=PIECES_BYTES
    )


def whole(array):
    zeros = (0,) * array.ndim
    return pl.BlockSpec(array.shape, lambda *_: zeros)


def kernel_call(body, name, meta, args, in_specs, out_shape, out_specs, grid=(1,), scratch=(), flops=1000, vmem=VMEM_BYTES):
    return pl.pallas_call(
        body,
        grid_spec=pltpu.PrefetchScalarGridSpec(
            num_scalar_prefetch=1,
            grid=grid,
            in_specs=in_specs,
            out_specs=out_specs,
            scratch_shapes=list(scratch),
        ),
        out_shape=out_shape,
        compiler_params=pltpu.CompilerParams(vmem_limit_bytes=vmem),
        cost_estimate=pl.CostEstimate(flops=flops, bytes_accessed=1000, transcendentals=0),
        name=name,
    )(meta, *args)


def shape_of(*dims, dtype=jnp.bfloat16):
    return jax.ShapeDtypeStruct(dims, dtype)


def normalized(values):
    centered = values - jnp.mean(values, axis=-1, keepdims=True)
    inverse = lax.rsqrt(jnp.mean(centered * centered, axis=-1, keepdims=True) + 1e-06)
    return centered * inverse, inverse


def norm_gradient(unit, inverse, gain, grad):
    wide = grad * gain
    return inverse * (
        wide - jnp.mean(wide, axis=-1, keepdims=True) - unit * jnp.mean(wide * unit, axis=-1, keepdims=True)
    )


def valid_column(meta_ref, rows):
    row = lax.broadcasted_iota(jnp.int32, (rows, 1), 0)
    valid = jnp.zeros((rows, 1), jnp.float32)
    for crop in range(rows // L):
        inside = (row >= crop * L) & (row < (crop + 1) * L)
        valid = jnp.where(inside, meta_ref[FLAGS + crop].astype(jnp.float32), valid)
    return valid


def quarter_of(meta_ref, side):
    return pl.ds(pl.multiple_of(meta_ref[side] * QUARTER, QUARTER), QUARTER)


def slice_weights(meta, w_query, w_key, w_value, w_out, w_up, w_down, b_query, b_value, b_up):
    half_h, half_u = w_query.shape[1] // 2, w_up.shape[1] // 2
    n_h, n_u = half_h // BLOCK, half_u // BLOCK

    def body(meta_ref, q_ref, k_ref, v_ref, o_ref, up_ref, down_ref, bq_ref, bv_ref, bu_ref, attn_ref, rest_ref):
        core = meta_ref[OWN_CORE]
        for which, ref in enumerate((q_ref, k_ref, v_ref)):
            attn_ref[which * QUARTER : (which + 1) * QUARTER, :] = ref[...]
        for b in range(2):
            row = 3 * QUARTER + b * half_h
            attn_ref[row : row + half_h, :] = o_ref[:, b * BLOCK : (b + 1) * BLOCK]
        picked = jnp.concatenate(
            [
                bq_ref[pl.ds(core * n_h, n_h), :],
                bv_ref[pl.ds(core * n_h, n_h), :],
                bu_ref[pl.ds(core * n_u, n_u), :],
            ],
            axis=0,
        )
        high = picked.astype(jnp.bfloat16)
        low = (picked - high.astype(jnp.float32)).astype(jnp.bfloat16)
        spare = jnp.zeros((16 - 2 * picked.shape[0], BLOCK), jnp.bfloat16)
        attn_ref[4 * QUARTER :, :] = jnp.concatenate([high, low, spare], axis=0)
        for b in range(n_u):
            rest_ref[b * QUARTER : (b + 1) * QUARTER, :] = up_ref[:, b * BLOCK : (b + 1) * BLOCK]
        for b in range(2):
            row = n_u * QUARTER + b * half_u
            rest_ref[row : row + half_u, :] = down_ref[:, b * BLOCK : (b + 1) * BLOCK]

    args = (w_query, w_key, w_value, w_out, w_up, w_down, b_query, b_value, b_up)
    out = [shape_of(4 * QUARTER + 16, BLOCK), shape_of(2 * n_u * QUARTER, BLOCK)]
    return kernel_call(
        body,
        "slice_weights",
        meta,
        args,
        [pl.BlockSpec((QUARTER, half_h), lambda i, m: (m[0], m[OWN_CORE]))] * 3
        + [
            pl.BlockSpec((half_h, QUARTER), lambda i, m: (m[OWN_CORE], m[0])),
            pl.BlockSpec((QUARTER, half_u), lambda i, m: (m[0], m[OWN_CORE])),
            pl.BlockSpec((half_u, QUARTER), lambda i, m: (m[OWN_CORE], m[0])),
            whole(b_query),
            whole(b_value),
            whole(b_up),
        ],
        out,
        [whole(o) for o in out],
        vmem=60 * 2**20,
    )


def turn_into(meta_ref, values, turned_ref, index=None):
    for side in range(CHIPS):
        rows = slice(side * QUARTER, (side + 1) * QUARTER)
        if index is None:
            turned_ref[rows, :] = values[:, quarter_of(meta_ref, side)].T
        else:
            turned_ref[rows, :] = values[index, :, quarter_of(meta_ref, side)].T


def turn(meta, *arrays):
    def body(meta_ref, *refs):
        for source, target in zip(refs[: len(arrays)], refs[len(arrays) :]):
            turn_into(meta_ref, source, target)

    out = [shape_of(*a.shape[::-1]) for a in arrays]
    return kernel_call(body, "turn", meta, arrays, [whole(a) for a in arrays], out, [whole(o) for o in out])


def prepare(meta, tokens, tokens_other, cotangent, vectors):
    rows, width = tokens.shape

    def body(meta_ref, tokens_ref, other_ref, cot_ref, vec_ref, one_ref, two_ref, grad_ref, sum_ref, *turned):
        for source, target in ((tokens_ref, one_ref), (other_ref, two_ref)):
            unit, _ = normalized(source[...].astype(jnp.float32))
            target[...] = (unit * vec_ref[GAIN_ONE : GAIN_ONE + 1] + vec_ref[SHIFT_ONE : SHIFT_ONE + 1]).astype(
                jnp.bfloat16
            )
        grad = vec_ref[SCALE_MLP : SCALE_MLP + 1] * (valid_column(meta_ref, rows) * cot_ref[...].astype(jnp.float32))
        sum_ref[...] = jnp.sum(grad, axis=0, keepdims=True)
        grad_ref[...] = grad.astype(jnp.bfloat16)
        for source, target in zip((one_ref, two_ref, grad_ref), turned):
            turn_into(meta_ref, source, target)

    args = (tokens, tokens_other, cotangent, vectors)
    out = [shape_of(rows, width)] * 3 + [shape_of(1, width, dtype=jnp.float32)] + [shape_of(width, rows)] * 3
    return kernel_call(body, "prepare", meta, args, [whole(a) for a in args], out, [whole(o) for o in out])


def fill_heads(meta_ref, chip_refs, weight_ref):
    for side, ref in enumerate(chip_refs):
        at = quarter_of(meta_ref, side)
        for which in range(3):
            weight_ref[at, which * BLOCK : (which + 1) * BLOCK] = ref[which * QUARTER : (which + 1) * QUARTER, :]


def head_specs(width, chips):
    own = [pl.BlockSpec((width, BLOCK), lambda g, m: (0, m[OWN_CORE]))] * 3
    far = [pl.BlockSpec((4 * QUARTER, BLOCK), lambda g, m: (jnp.maximum(g - 1, 0), 0))] * len(chips)
    return own, far


def attention_forward(meta, normed, other, w_query, w_key, w_value, b_query, b_value, level_attn, chips, w_count):
    rows, width = normed.shape
    group = 3 * BLOCK
    ranges = crop_ranges(rows)
    span = max(high - low for low, high, _ in ranges)
    scale = 1.0 / math.sqrt(DH)
    count = 2 + w_count

    def body(meta_ref, normed_ref, other_ref, q_ref, k_ref, v_ref, bq_ref, bv_ref, one_ref, two_ref, three_ref, *refs):
        chip_refs, (qkv_ref, out_ref, prob_ref, weight_ref, sum_ref) = refs[:CHIPS], refs[CHIPS:]
        group_here = pl.program_id(0)
        core = meta_ref[OWN_CORE]

        @pl.when(group_here == 0)
        def _():
            for which, ref in enumerate((q_ref, k_ref, v_ref)):
                weight_ref[:, which * BLOCK : (which + 1) * BLOCK] = ref[...]
            sum_ref[0:1, :] = bq_ref[pl.ds(core, 1), :]
            sum_ref[1:2, :] = bv_ref[pl.ds(core, 1), :]

        for index, ref in enumerate((one_ref, two_ref, three_ref)):
            @pl.when(group_here == index + 1)
            def _():
                both = ref[...].astype(jnp.float32)
                sum_ref[0:2, :] = both[0:2] + both[count : count + 2]

        @pl.when(group_here > 0)
        def _():
            fill_heads(meta_ref, chip_refs, weight_ref)

        bias = jnp.concatenate([sum_ref[0:1, :], jnp.zeros((1, BLOCK), jnp.float32), sum_ref[1:2, :]], axis=1)
        for part, rows_ref in enumerate((normed_ref, other_ref)):
            qkv_ref[part] = (dot_nn(rows_ref[...], weight_ref[...]) + bias).astype(jnp.bfloat16)
        for part in range(2):
            for index, (low, high, skip) in enumerate(ranges):
                size = high - low
                query = qkv_ref[part, low:high, 0:BLOCK]
                key = qkv_ref[part, low:high, BLOCK : 2 * BLOCK]
                value = qkv_ref[part, low:high, 2 * BLOCK : 3 * BLOCK]
                lane = lax.broadcasted_iota(jnp.int32, (size, BLOCK), 1)
                row = lax.broadcasted_iota(jnp.int32, (size, size), 0)
                column = lax.broadcasted_iota(jnp.int32, (size, size), 1)
                seen = (column >= skip) & (column < skip + L)
                inside = seen & (row >= skip) & (row < skip + L)
                parts = []
                for head in range(2):
                    own = (lane < DH) if head == 0 else (lane >= DH)
                    scores = dot_nt(jnp.where(own, query, jnp.zeros_like(query)), key) * scale
                    scores = jnp.where(seen, scores, -1e30)
                    top = jnp.max(scores, axis=1, keepdims=True)
                    raised = jnp.exp(scores - top)
                    total = jnp.sum(raised, axis=1, keepdims=True)
                    probs = jnp.where(inside, raised * (1.0 / total), 0.0).astype(jnp.bfloat16)
                    prob_ref[0, part, index, head, 0:size, 0:size] = probs
                    parts.append(dot_nn(probs, value))
                mixed = jnp.where(lane < DH, parts[0], parts[1]).astype(jnp.bfloat16)
                if skip:
                    edge = lax.broadcasted_iota(jnp.int32, (size, BLOCK), 0) >= skip
                    mixed = jnp.where(edge, mixed, out_ref[part, low:high, :])
                out_ref[part, low:high, :] = mixed

    prob_shape = (DEPTH, 2, len(ranges), 2, span, span)
    own_specs, far_specs = head_specs(width, chips)
    tail = 4 * QUARTER // 16
    args = (normed, other, w_query, w_key, w_value, b_query, b_value) + tuple(level_attn) + tuple(chips)
    return kernel_call(
        body,
        "attention_forward",
        meta,
        args,
        [whole(normed), whole(other)] + own_specs + [whole(b_query), whole(b_value)] + [pl.BlockSpec((16, BLOCK), lambda g, m: (tail, 0))] * 3 + far_specs,
        [shape_of(2, rows, DEPTH * group), shape_of(2, rows, DEPTH * BLOCK), shape_of(*prob_shape)],
        [
            pl.BlockSpec((2, rows, group), lambda g, m: (0, 0, g)),
            pl.BlockSpec((2, rows, BLOCK), lambda g, m: (0, 0, g)),
            pl.BlockSpec((1,) + prob_shape[1:], lambda g, m: (g, 0, 0, 0, 0, 0)),
        ],
        grid=(DEPTH,),
        scratch=[pltpu.VMEM((width, group), jnp.bfloat16), pltpu.VMEM((8, BLOCK), jnp.float32)],
    )


def attention_out(meta, attended, w_out, chips):
    rows, width = attended.shape[1], w_out.shape[1]

    def body(meta_ref, attended_ref, own_ref, *refs):
        chip_refs, (near_ref, low_ref, high_ref, weight_ref) = refs[:CHIPS], refs[CHIPS:]
        weight_ref[0:BLOCK, :] = own_ref[...]
        for side, ref in enumerate(chip_refs):
            start = pl.multiple_of(meta_ref[side] * QUARTER, QUARTER)
            for index in range(DEPTH - 1):
                for b in range(2):
                    weight_ref[(index + 1) * BLOCK : (index + 2) * BLOCK, pl.ds(start + b * BLOCK, BLOCK)] = ref[
                        index, b * BLOCK : (b + 1) * BLOCK, :
                    ]
        near_ref[...] = dot_nn(attended_ref[0], weight_ref[...])
        across = dot_nn(attended_ref[1], weight_ref[...]).astype(jnp.bfloat16)
        low_ref[...] = across[:, : width // 2]
        high_ref[...] = across[:, width // 2 :]

    views = tuple(chip.reshape(DEPTH - 1, 4 * QUARTER, BLOCK) for chip in chips)
    view_spec = pl.BlockSpec((DEPTH - 1, QUARTER, BLOCK), lambda i, m: (0, 3, 0))
    out = [shape_of(rows, width, dtype=jnp.float32)] + [shape_of(rows, width // 2)] * 2
    return kernel_call(
        body, "attention_out", meta, (attended, w_out) + views,
        [whole(attended), pl.BlockSpec((BLOCK, width), lambda i, m: (m[OWN_CORE], 0))] + [view_spec] * CHIPS,
        out, [whole(o) for o in out], scratch=[pltpu.VMEM((DEPTH * BLOCK, width), jnp.bfloat16)],
    )


def attention_norm(meta, near, low, high, tokens, vectors):
    rows, width = tokens.shape

    def body(meta_ref, near_ref, low_ref, high_ref, tokens_ref, vec_ref, hidden_ref, branch_ref, normed_ref):
        got = jnp.concatenate([low_ref[...], high_ref[...]], axis=1).astype(jnp.float32)
        branch = near_ref[...] + got + vec_ref[BIAS_OUT : BIAS_OUT + 1]
        branch_ref[...] = branch
        hidden = tokens_ref[...].astype(jnp.float32) + vec_ref[SCALE_ATTN : SCALE_ATTN + 1] * branch
        hidden_ref[...] = hidden
        unit, _ = normalized(hidden)
        normed = (unit * vec_ref[GAIN_TWO : GAIN_TWO + 1] + vec_ref[SHIFT_TWO : SHIFT_TWO + 1]).astype(jnp.bfloat16)
        normed_ref[...] = normed

    args = (near, low, high, tokens, vectors)
    out = [shape_of(rows, width, dtype=jnp.float32)] * 2 + [shape_of(rows, width)]
    return kernel_call(body, "attention_norm", meta, args, [whole(a) for a in args], out, [whole(o) for o in out], vmem=NORM_BYTES)


def feed_rows(normed_pieces, grad, up_weight, down_weight, bias, act_ref, gup_ref, low, high):
    width = up_weight.shape[0]
    deep = width // len(normed_pieces)
    pre = bias[:, low:high] + sum(
        dot_nn(piece[...], up_weight[k * deep : (k + 1) * deep, low:high]) for k, piece in enumerate(normed_pieces)
    )
    spread = 0.5 * (1.0 + lax.erf(pre * (1.0 / math.sqrt(2.0))))
    act_ref[:, low:high] = (pre * spread).astype(jnp.bfloat16)
    slope = spread + pre * jnp.exp(-0.5 * pre * pre) * (1.0 / math.sqrt(2.0 * math.pi))
    grad_up = (dot_nt(grad[...], down_weight[low:high, :]) * slope).astype(jnp.bfloat16)
    gup_ref[:, low:high] = grad_up
    return jnp.sum(grad_up.astype(jnp.float32), axis=0, keepdims=True)


def feed_near(meta, normed, grads, w_up, w_down, bias_up, chips):
    rows, width = grads[0].shape
    normed = [part if isinstance(part, (list, tuple)) else [part] for part in normed]
    flat = [piece for part in normed for piece in part]
    half_u = w_up.shape[1] // 2
    n_u = half_u // BLOCK
    count = len(normed)
    copies = len(flat) + count + 2 + CHIPS * (n_u + 2)

    def body(meta_ref, *refs):
        bias_ref, flat_hbm, refs = refs[0], refs[1 : 1 + len(flat)], refs[1 + len(flat) :]
        grad_hbm, refs = refs[:count], refs[count:]
        up_hbm, down_hbm, chip_refs, refs = refs[0], refs[1], refs[2 : 2 + CHIPS], refs[2 + CHIPS :]
        act_refs, gup_refs, back_refs, refs = refs[:count], refs[count : 2 * count], refs[2 * count : 3 * count], refs[3 * count :]
        sum_ref, up_weight, down_weight, normed_ref, grad_ref, sems = refs
        half = pl.ds(pl.multiple_of(meta_ref[OWN_CORE] * half_u, half_u), half_u)
        pieces = []
        for part, cut in enumerate(normed):
            deep = width // len(cut)
            for k in range(len(cut)):
                pieces.append((part, (flat_hbm[len(pieces)], normed_ref.at[part, :, pl.ds(k * deep, deep)])))
        moves = [move for part, move in pieces if part == 0]
        moves += [
            (up_hbm.at[:, half], up_weight.at[:, pl.ds(0, half_u)]),
            (grad_hbm[0], grad_ref.at[0]),
            (down_hbm.at[half, :], down_weight.at[pl.ds(0, half_u), :]),
        ]
        for part in range(1, count):
            moves += [move for owner, move in pieces if owner == part] + [(grad_hbm[part], grad_ref.at[part])]
        near_moves = len(moves)
        for side, ref in enumerate(chip_refs):
            start = pl.multiple_of(meta_ref[side] * QUARTER, QUARTER)
            for b in range(n_u):
                moves.append(
                    (
                        ref.at[pl.ds(b * QUARTER, QUARTER), :],
                        up_weight.at[pl.ds(start, QUARTER), pl.ds(half_u + b * BLOCK, BLOCK)],
                    )
                )
            for b in range(2):
                moves.append(
                    (
                        ref.at[pl.ds(n_u * QUARTER + b * half_u, half_u), :],
                        down_weight.at[pl.ds(half_u, half_u), pl.ds(start + b * BLOCK, BLOCK)],
                    )
                )
        handles = [pltpu.make_async_copy(source, target, sems.at[k]) for k, (source, target) in enumerate(moves)]
        for handle in handles:
            handle.start()
        for tile, waits in enumerate((handles[:near_moves], handles[near_moves:])):
            for handle in waits:
                handle.wait()
            low, high = tile * half_u, (tile + 1) * half_u
            sums = [
                feed_rows([normed_ref.at[p]], grad_ref.at[p], up_weight, down_weight, bias_ref, act_refs[p], gup_refs[p], low, high)
                for p in range(count)
            ]
            sum_ref[:, low:high] = sum(sums)
        for part in range(count):
            back_refs[part][...] = dot_nt(gup_refs[part][...], up_weight[...]).astype(jnp.bfloat16)

    anywhere = pl.BlockSpec(memory_space=pl.ANY)
    out = [shape_of(rows, 2 * half_u)] * (2 * count) + [shape_of(rows, width)] * count
    out += [shape_of(1, 2 * half_u, dtype=jnp.float32), shape_of(width, 2 * half_u), shape_of(2 * half_u, width)]
    args = tuple(flat) + tuple(grads) + (w_up, w_down) + tuple(chips)
    outs = kernel_call(
        body, "feed_near", meta, (bias_up,) + args, [whole(bias_up)] + [anywhere] * len(args), out, [whole(o) for o in out],
        scratch=[pltpu.VMEM((count, rows, width), jnp.bfloat16)] * 2 + [pltpu.SemaphoreType.DMA((copies,))],
        vmem=NEAR_BYTES,
    )
    return outs[:count], outs[count : 2 * count], outs[2 * count : 3 * count], outs[3 * count], outs[3 * count + 1], outs[3 * count + 2]


def feed_far(meta, normed, grad, bias_up, full_up, full_down):
    rows, width = grad.shape
    units = full_up.shape[1]
    pieces = len(normed)

    def body(meta_ref, *refs):
        normed_refs = refs[:pieces]
        grad_ref, bias_ref, up_ref, down_ref, act_ref, gup_ref, back_ref, sum_ref = refs[pieces:]
        for tile in range(2):
            low, high = tile * units // 2, (tile + 1) * units // 2
            sum_ref[:, low:high] = feed_rows(
                normed_refs, grad_ref, up_ref, down_ref, bias_ref, act_ref, gup_ref, low, high
            )
        back_ref[...] = dot_nt(gup_ref[...], up_ref[...]).astype(jnp.bfloat16)

    args = tuple(normed) + (grad, bias_up, full_up, full_down)
    out = [shape_of(rows, units)] * 2 + [shape_of(rows, width), shape_of(1, units, dtype=jnp.float32)]
    return kernel_call(body, "feed_far", meta, args, [whole(a) for a in args], out, [whole(o) for o in out])


def feed_down(meta, acts, full_down):
    rows, width = acts[0].shape[0], full_down.shape[1]
    count = len(acts)

    def body(meta_ref, *refs):
        weight_ref = refs[count]
        for act_ref, out_ref in zip(refs[:count], refs[count + 1 :]):
            out_ref[...] = dot_nn(act_ref[...], weight_ref[...]).astype(jnp.bfloat16)

    args = tuple(acts) + (full_down,)
    out = [shape_of(rows, width)] * count
    return kernel_call(body, "feed_down", meta, args, [whole(a) for a in args], out, [whole(o) for o in out])


def put_sides(lane, values, keep_ref, send_ref, at):
    keep, send = ((0, 2), (1, 3)) if lane == 0 else ((0, 1), (2, 3))
    for ref, sides in ((keep_ref, keep), (send_ref, send)):
        for index, side in enumerate(sides):
            ref[index * QUARTER : (index + 1) * QUARTER, at] = values[side * QUARTER : (side + 1) * QUARTER].astype(
                jnp.bfloat16
            )


def feed_gradients(meta, normed, turned_grads, gups, acts):
    normed = [part if isinstance(part, (list, tuple)) else [part] for part in normed]
    flat = [piece for part in normed for piece in part]
    rows = flat[0].shape[0]
    width = turned_grads[0].shape[0]
    half_u = gups[0].shape[1] // 2
    n = len(gups)

    def body(meta_ref, *refs):
        normed_refs, refs = refs[: len(flat)], refs[len(flat) :]
        turned_refs, gup_refs, act_refs, refs = refs[:n], refs[n : 2 * n], refs[2 * n : 3 * n], refs[3 * n :]
        outs, own_turned, whole_ref = refs[:4], refs[4:-1], refs[-1]
        step = pl.program_id(0)

        @pl.when(step == 0)
        def _():
            at = 0
            for part, target in zip(normed, own_turned):
                if len(part) == 1:
                    turn_into(meta_ref, normed_refs[at], target)
                else:
                    deep = width // len(part)
                    for k in range(len(part)):
                        whole_ref[:, k * deep : (k + 1) * deep] = normed_refs[at + k][...]
                    turn_into(meta_ref, whole_ref, target)
                at += len(part)

        def product(lefts, rights):
            return sum(dot_nn(left[...], right[...]) for left, right in zip(lefts, rights))

        for lane in range(2):
            kept, sent = outs[2 * lane : 2 * lane + 2]

            @pl.when(step == 2 * lane)
            def _():
                put_sides(lane, product(own_turned, gup_refs), kept, sent, slice(None))

            @pl.when(step == 2 * lane + 1)
            def _():
                put_sides(lane, product(turned_refs, act_refs), kept, sent, slice(None))

    args = tuple(flat) + tuple(turned_grads)
    by_lane = [pl.BlockSpec((rows, half_u), lambda g, m: (0, g >> 1))] * (2 * n)
    out_specs = [pl.BlockSpec((2 * QUARTER, half_u), lambda g, m: (0, jnp.minimum(g, 1)))] * 2
    out_specs += [pl.BlockSpec((2 * QUARTER, half_u), lambda g, m: (0, jnp.maximum(g - 2, 0)))] * 2
    outs = kernel_call(
        body, "feed_gradients", meta, args + tuple(gups) + tuple(acts),
        [whole(a) for a in args] + by_lane, [shape_of(2 * QUARTER, 2 * half_u)] * 4, out_specs, grid=(4,),
        scratch=[pltpu.VMEM((width, rows), jnp.bfloat16)] * 4 + [pltpu.VMEM((rows, width), jnp.bfloat16)],
    )
    return outs[:2], outs[2:]


def hidden_gradient(meta, backs, hidden, branch, cotangent, vectors):
    rows, width = hidden.shape

    def body(meta_ref, *refs):
        back_refs, (hidden_ref, branch_ref, cot_ref, vec_ref, dh_ref, e1_ref, sum_ref) = refs[: len(backs)], refs[len(backs) :]
        grad = sum(ref[...].astype(jnp.float32) for ref in back_refs)
        unit, inverse = normalized(hidden_ref[...])
        sum_ref[0:1, :] = jnp.sum(grad * unit, axis=0, keepdims=True)
        sum_ref[1:2, :] = jnp.sum(grad, axis=0, keepdims=True)
        total = valid_column(meta_ref, rows) * cot_ref[...].astype(jnp.float32) + norm_gradient(
            unit, inverse, vec_ref[GAIN_TWO : GAIN_TWO + 1], grad
        )
        dh_ref[...] = total
        sum_ref[2:3, :] = jnp.sum(total * branch_ref[...], axis=0, keepdims=True)
        scaled = vec_ref[SCALE_ATTN : SCALE_ATTN + 1] * total
        sum_ref[3:4, :] = jnp.sum(scaled, axis=0, keepdims=True)
        e1_ref[...] = scaled.astype(jnp.bfloat16)

    args = tuple(backs) + (hidden, branch, cotangent, vectors)
    out = [shape_of(rows, width, dtype=jnp.float32), shape_of(rows, width), shape_of(4, width, dtype=jnp.float32)]
    return kernel_call(body, "hidden_gradient", meta, args, [whole(a) for a in args], out, [whole(o) for o in out])


def attention_backward(meta, qkv, probs, attended, grads, turned_normed, w_out, chips):
    rows, width = grads[0].shape
    group = 3 * BLOCK
    ranges = crop_ranges(rows)
    scale = 1.0 / math.sqrt(DH)

    def body(meta_ref, qkv_ref, prob_ref, mixed_ref, e1_ref, e1_other_ref, n_ref, n_other_ref, own_ref, *refs):
        chip_refs, out_ref, sides, refs = refs[:CHIPS], refs[CHIPS], refs[CHIPS + 1 : CHIPS + 5], refs[CHIPS + 5 :]
        weight_ref, grad_ref, mixed_all, turned_e, turned_other = refs
        step = pl.program_id(0)
        parity = step & 1

        @pl.when(step == 0)
        def _():
            turn_into(meta_ref, e1_ref, turned_e)
            turn_into(meta_ref, e1_other_ref, turned_other)

        def far_weights():
            for side, ref in enumerate(chip_refs):
                start = pl.multiple_of(meta_ref[side] * QUARTER, QUARTER)
                for b in range(2):
                    weight_ref[:, pl.ds(start + b * BLOCK, BLOCK)] = ref[0, b * BLOCK : (b + 1) * BLOCK, :]

        @pl.when(step == 0)
        def _():
            weight_ref[...] = own_ref[...]

        pl.when(step > 0)(far_weights)
        mixed_all[:, :, pl.ds(pl.multiple_of(parity * BLOCK, BLOCK), BLOCK)] = mixed_ref[...]
        for part, ref in enumerate((e1_ref, e1_other_ref)):
            grad_ref[part] = dot_nt(ref[...], weight_ref[...]).astype(jnp.bfloat16)
        for part in range(2):
            for index, (low, high, skip) in enumerate(ranges):
                size = high - low
                query = qkv_ref[part, low:high, 0:BLOCK]
                key = qkv_ref[part, low:high, BLOCK : 2 * BLOCK]
                value = qkv_ref[part, low:high, 2 * BLOCK : 3 * BLOCK]
                grad = grad_ref[part, low:high, :]
                lane_of = lax.broadcasted_iota(jnp.int32, (size, BLOCK), 1)
                row = lax.broadcasted_iota(jnp.int32, (size, BLOCK), 0)
                parts = []
                for head in range(2):
                    own = (lane_of < DH) if head == 0 else (lane_of >= DH)
                    low_probs = prob_ref[0, part, index, head, 0:size, 0:size]
                    grad_value = dot_tn(low_probs, grad)
                    grad_probs = dot_nt(jnp.where(own, grad, jnp.zeros_like(grad)), value)
                    wide = low_probs.astype(jnp.float32)
                    weighted = wide * grad_probs
                    inner = jnp.sum(weighted, axis=1, keepdims=True)
                    grad_scores = (weighted - wide * inner).astype(jnp.bfloat16)
                    parts.append(
                        (dot_nn(grad_scores, key) * scale, dot_tn(grad_scores, query) * scale, grad_value)
                    )
                for which in range(3):
                    at = pl.ds(pl.multiple_of(parity * group + which * BLOCK, BLOCK), BLOCK)
                    joined = jnp.where(lane_of < DH, parts[0][which], parts[1][which]).astype(jnp.bfloat16)
                    if skip:
                        joined = jnp.where(row >= skip, joined, out_ref[part, low:high, at])
                    out_ref[part, low:high, at] = joined
        for lane in range(2):
            @pl.when(step == 2 * lane + 1)
            def _():
                kept, sent = sides[2 * lane : 2 * lane + 2]
                both = dot_nn(n_ref[...], out_ref[0]) + dot_nn(n_other_ref[...], out_ref[1])
                put_sides(lane, both, kept, sent, slice(0, 2 * group))
                both = dot_nn(turned_e[...], mixed_all[0]) + dot_nn(turned_other[...], mixed_all[1])
                put_sides(lane, both, kept, sent, slice(2 * group, 2 * group + 2 * BLOCK))

    views = tuple(chip.reshape(DEPTH - 1, 4 * QUARTER, BLOCK) for chip in chips)
    args = (qkv, probs, attended) + tuple(grads) + tuple(turned_normed) + (w_out,) + views
    return kernel_call(
        body,
        "attention_backward",
        meta,
        args,
        [
            pl.BlockSpec((2, rows, group), lambda g, m: (0, 0, g)),
            pl.BlockSpec((1,) + probs.shape[1:], lambda g, m: (g, 0, 0, 0, 0, 0)),
            pl.BlockSpec((2, rows, BLOCK), lambda g, m: (0, 0, g)),
            whole(grads[0]),
            whole(grads[1]),
            whole(turned_normed[0]),
            whole(turned_normed[1]),
            pl.BlockSpec((BLOCK, width), lambda g, m: (m[OWN_CORE], 0)),
        ]
        + [pl.BlockSpec((1, QUARTER, BLOCK), lambda g, m: (jnp.maximum(g - 1, 0), 3, 0))] * CHIPS,
        [shape_of(2, rows, DEPTH * group)] + [shape_of(width // 2, 8 * BLOCK)] * 4,
        [pl.BlockSpec((2, rows, 2 * group), lambda g, m: (0, 0, g >> 1))]
        + [pl.BlockSpec((width // 2, 8 * BLOCK), lambda g, m: (0, 0))] * 4,
        grid=(DEPTH,),
        scratch=[
            pltpu.VMEM((BLOCK, width), jnp.bfloat16),
            pltpu.VMEM((2, rows, BLOCK), jnp.bfloat16),
            pltpu.VMEM((2, rows, 2 * BLOCK), jnp.bfloat16),
            pltpu.VMEM((width, rows), jnp.bfloat16),
            pltpu.VMEM((width, rows), jnp.bfloat16),
        ],
        vmem=BACK_BYTES,
    )


def token_shares(meta, grads, w_query, w_key, w_value, chips):
    rows = grads.shape[1]
    width = w_query.shape[0]
    group = 3 * BLOCK

    def body(meta_ref, grad_ref, q_ref, k_ref, v_ref, *refs):
        chip_refs, (near_ref, left_ref, right_ref, bias_ref, weight_ref, total_ref) = refs[:CHIPS], refs[CHIPS:]
        step = pl.program_id(0)

        @pl.when(step == 0)
        def _():
            for which, ref in enumerate((q_ref, k_ref, v_ref)):
                weight_ref[:, which * BLOCK : (which + 1) * BLOCK] = ref[...]

        @pl.when(step > 0)
        def _():
            fill_heads(meta_ref, chip_refs, weight_ref)

        sums = jnp.sum(grad_ref[0].astype(jnp.float32), axis=0, keepdims=True)
        bias_ref[0] = sums + jnp.sum(grad_ref[1].astype(jnp.float32), axis=0, keepdims=True)
        for part in range(2):
            share = dot_nt(grad_ref[part], weight_ref[...])

            @pl.when(step == 0)
            def _():
                total_ref[part] = share

            @pl.when(step > 0)
            def _():
                total_ref[part] += share

        @pl.when(step == DEPTH - 1)
        def _():
            near_ref[...] = total_ref[0]
            left_ref[...] = total_ref[1, :, : width // 2].astype(jnp.bfloat16)
            right_ref[...] = total_ref[1, :, width // 2 :].astype(jnp.bfloat16)

    own_specs, far_specs = head_specs(width, chips)
    out = [shape_of(rows, width, dtype=jnp.float32)] + [shape_of(rows, width // 2)] * 2
    return kernel_call(
        body,
        "token_shares",
        meta,
        (grads, w_query, w_key, w_value) + tuple(chips),
        [pl.BlockSpec((2, rows, group), lambda g, m: (0, 0, g))]
        + own_specs
        + far_specs,
        out + [shape_of(DEPTH, 1, group, dtype=jnp.float32)],
        [whole(o) for o in out] + [pl.BlockSpec((1, 1, group), lambda g, m: (g, 0, 0))],
        grid=(DEPTH,),
        scratch=[pltpu.VMEM((width, group), jnp.bfloat16), pltpu.VMEM((2, rows, width), jnp.float32)],
    )


def token_gradient(meta, near, left, right, tokens, dh, vectors):
    rows, width = tokens.shape

    def body(meta_ref, near_ref, left_ref, right_ref, tokens_ref, dh_ref, vec_ref, out_ref, sum_ref):
        got = jnp.concatenate([left_ref[...], right_ref[...]], axis=1).astype(jnp.float32)
        grad = near_ref[...] + got
        unit, inverse = normalized(tokens_ref[...].astype(jnp.float32))
        sum_ref[0:1, :] = jnp.sum(grad * unit, axis=0, keepdims=True)
        sum_ref[1:2, :] = jnp.sum(grad, axis=0, keepdims=True)
        out_ref[...] = dh_ref[...] + norm_gradient(unit, inverse, vec_ref[GAIN_ONE : GAIN_ONE + 1], grad)

    args = (near, left, right, tokens, dh, vectors)
    out = [shape_of(rows, width, dtype=jnp.float32), shape_of(2, width, dtype=jnp.float32)]
    return kernel_call(body, "token_gradient", meta, args, [whole(a) for a in args], out, [whole(o) for o in out])


def layer_result(meta, downs, hidden, cotangent, vectors):
    rows, width = hidden.shape

    def body(meta_ref, *refs):
        down_refs, (hidden_ref, cot_ref, vec_ref, out_ref, sum_ref) = refs[: len(downs)], refs[len(downs) :]
        branch = sum(ref[...].astype(jnp.float32) for ref in down_refs) + vec_ref[BIAS_DOWN : BIAS_DOWN + 1]
        valid = valid_column(meta_ref, rows)
        out_ref[...] = valid * (hidden_ref[...] + vec_ref[SCALE_MLP : SCALE_MLP + 1] * branch)
        sum_ref[...] = jnp.sum(valid * cot_ref[...].astype(jnp.float32) * branch, axis=0, keepdims=True)

    args = tuple(downs) + (hidden, cotangent, vectors)
    out = [shape_of(rows, width, dtype=jnp.float32), shape_of(1, width, dtype=jnp.float32)]
    return kernel_call(body, "layer_result", meta, args, [whole(a) for a in args], out, [whole(o) for o in out])


def pack_small(meta, wide, sums_qkv, sums_up):
    lines = wide[0].shape[1] // BLOCK
    n_u = sums_up[0].shape[1] // 2 // BLOCK
    share = 2 + n_u
    rows = sum(value.shape[0] for value in wide) * lines
    total = rows + 2 * DEPTH * share

    def body(meta_ref, *refs):
        wide_refs, qkv_ref, up_refs, out_ref = refs[: len(wide)], refs[len(wide)], refs[len(wide) + 1 : -1], refs[-1]
        at = 0
        for ref in wide_refs:
            for index in range(ref.shape[0]):
                for k in range(lines):
                    out_ref[at : at + 1, :] = ref[index : index + 1, k * BLOCK : (k + 1) * BLOCK]
                    at += 1
        out_ref[rows:, :] = jnp.zeros((total - rows, BLOCK), jnp.float32)
        core, level = meta_ref[OWN_CORE], meta_ref[OWN_LEVEL]
        for index in range(DEPTH):
            start = rows + core * (DEPTH * share) + (level ^ index) * share
            out_ref[pl.ds(start, 1), :] = qkv_ref[index, :, 0:BLOCK]
            out_ref[pl.ds(start + 1, 1), :] = qkv_ref[index, :, 2 * BLOCK : 3 * BLOCK]
            if index in (0, 2):
                for k in range(n_u):
                    column = (index // 2 * n_u + k) * BLOCK
                    out_ref[pl.ds(start + 2 + k, 1), :] = sum(ref[:, column : column + BLOCK] for ref in up_refs)

    args = tuple(wide) + (sums_qkv,) + tuple(sums_up)
    out = shape_of(total, BLOCK, dtype=jnp.float32)
    return kernel_call(body, "pack_small", meta, args, [whole(a) for a in args], out, whole(out))


def finish(meta, mine, other, kinds, name):
    width = CHIPS * QUARTER

    def body(meta_ref, mine_ref, other_ref, *outs):
        core = meta_ref[OWN_CORE]
        for ref, half in ((mine_ref, core), (other_ref, 1 - core)):
            at = 0
            for out_ref, (units, turned) in zip(outs, kinds):
                values = ref[0, :, at : at + units].astype(jnp.float32)
                place = pl.ds(pl.multiple_of(half * units, units), units)
                if turned:
                    out_ref[place, :] = values.T
                else:
                    out_ref[:, place] = values
                at += units

    side = pl.BlockSpec((1,) + mine.shape[1:], lambda j, m: (j, 0, 0))
    out, specs = [], []
    for units, turned in kinds:
        shape = (2 * units, width) if turned else (width, 2 * units)
        block = (2 * units, QUARTER) if turned else (QUARTER, 2 * units)
        out.append(shape_of(*shape, dtype=jnp.float32))
        specs.append(pl.BlockSpec(block, (lambda j, m: (0, m[j])) if turned else (lambda j, m: (m[j], 0))))
    return kernel_call(body, name, meta, (mine, other), [side, side], out, specs, grid=(CHIPS,))


def local_paired(
    tokens,
    slide_tiles,
    norm1_gain,
    norm1_bias,
    w_query,
    b_query,
    w_key,
    w_value,
    b_value,
    w_out,
    b_out,
    scale_attn,
    norm2_gain,
    norm2_bias,
    w_up,
    b_up,
    w_down,
    b_down,
    scale_mlp,
    cotangent,
):
    row_count, width = tokens.shape
    half_u = w_up.shape[1] // 2
    here = lax.axis_index("dp")
    level = lax.axis_index("mp")
    crops_here = row_count // L
    per_slide = CROPS_DEV // SLIDES_DEV
    crop = level * crops_here + jnp.arange(crops_here, dtype=jnp.int32)
    owner = (crop // per_slide)[:, None] == jnp.arange(SLIDES_DEV, dtype=jnp.int32)[None, :]
    limit = jnp.sum(jnp.where(owner, slide_tiles[None, :], 0), axis=1)
    valid = (crop % per_slide < limit).astype(jnp.int32)
    core = here & 1
    sides = jnp.stack([(here >> 1) ^ side for side in range(CHIPS)] + [core, level]).astype(jnp.int32)
    meta = jnp.concatenate([sides, valid])
    bias_q, bias_v, bias_u = [values.reshape(-1, BLOCK) for values in (b_query, b_value, b_up)]
    vectors = jnp.stack([norm1_gain, norm1_bias, norm2_gain, norm2_bias, scale_attn, scale_mlp, b_out, b_down])
    first, second = (X_SIDE, Y_SIDE), (Y_SIDE, X_SIDE)

    order = Order(meta)

    tokens_other = swap_plane(tokens, CORE_SIDE)
    slice_attn, slice_rest = order(slice_weights, w_query, w_key, w_value, w_out, w_up, w_down, bias_q, bias_v, bias_u)
    level_attn = [swap_depth(slice_attn, mask) for mask in (1, 2, 3)]
    one, one_other, grad, grad_b_down, one_turned, one_other_turned, grad_turned = order(
        prepare, tokens, tokens_other, cotangent, vectors
    )
    level_attn = order.land(*level_attn)
    far_attn = order.plain(lambda *parts: jnp.concatenate([part[: 4 * QUARTER] for part in parts], axis=0), *level_attn)
    attn_x, attn_y = swap_plane(far_attn, X_SIDE), swap_plane(far_attn, Y_SIDE)
    level_rest = swap_depth(order.hold(slice_rest), 2)
    n_u = half_u // BLOCK

    def unit_bias(rows, own):
        rows = rows[4 * QUARTER :].astype(jnp.float32)
        pair = (rows[2 : 2 + n_u] + rows[4 + n_u : 4 + 2 * n_u]).reshape(-1)
        return jnp.concatenate([lax.dynamic_slice_in_dim(own, core * half_u, half_u), pair])[None, :]

    bias_up = order.plain(unit_bias, level_attn[1], b_up)
    attn_x, attn_y = order.land(attn_x, attn_y)
    half = far_attn.shape[0] // 2
    low, high = order.hold((attn_y[:half], attn_x[half:]))
    low, high = swap_plane(low, X_SIDE), swap_plane(high, Y_SIDE)
    level_rest, low, high = order.land(level_rest, low, high)
    corner = order.plain(lambda *parts: jnp.concatenate(parts), low, high)
    chips_attn = [far_attn, attn_x, attn_y, corner]
    level_rest, grad, grad_far = order.hold((level_rest, grad, grad))
    plane_rest = plane_swaps(level_rest)
    grad_other = swap_plane(grad, CORE_SIDE)
    grad_far = swap_depth(grad_far, 1)
    qkv, attended, probs = order(
        attention_forward, one, one_other, w_query, w_key, w_value, bias_q, bias_v, level_attn, chips_attn, n_u
    )
    grad_other, grad_far = order.land(grad_other, grad_far)
    out_near, *out_across = order(attention_out, attended, w_out, chips_attn)
    out_got = [swap_plane(part, CORE_SIDE) for part in out_across]
    plane_rest = order.land(*plane_rest)
    chips_rest = [level_rest] + plane_rest
    hidden, branch, normed = order(attention_norm, out_near, *out_got, tokens, vectors)
    normed_far = swap_depth(normed, 1)
    normed_other = swap_plane(normed, CORE_SIDE)
    grad_far_other = swap_plane(order.hold(grad_far), CORE_SIDE)

    *near, full_up, full_down = order(
        feed_near, (normed, normed_other), (grad, grad_other), w_up, w_down, bias_up, chips_rest
    )
    (normed_far,) = order.land(normed_far)
    normed_far, back_near = order.hold((normed_far, near[2][1]))
    normed_far_other = swap_plane(normed_far, CORE_SIDE)
    back_near = swap_plane(back_near, CORE_SIDE)
    far = order(feed_far, (normed_far,), grad_far, bias_up, full_up, full_down)
    far_other = order(feed_far, (normed_far_other,), grad_far_other, bias_up, full_up, full_down)
    acts, gups, backs = [list(a) + [b, c] for a, b, c in zip(near[:3], far[:3], far_other[:3])]
    back_got, back_near = order.land(swap_plane(backs[3], CORE_SIDE), back_near)
    back_far = swap_depth(order.plain(add_low, backs[2], back_got), 1)
    grads_turned = [grad_turned] + list(order(turn, grad_other, grad_far, grad_far_other))
    rest_sides = order(
        feed_gradients, (normed, normed_other, normed_far, normed_far_other), grads_turned, gups, acts
    )
    downs = order(feed_down, acts, full_down)
    down_near, down_far = swap_plane(downs[1], CORE_SIDE), swap_plane(downs[3], CORE_SIDE)
    (back_far,) = order.land(back_far)
    rest_sent = order.hold([sent for _, sent in rest_sides])
    rest_got = [swap_plane(sent, side) for sent, side in zip(rest_sent, first)]
    dh, e1, sums_two = order(
        hidden_gradient, (backs[0], back_near, back_far), hidden, branch, cotangent, vectors
    )
    e1_other = swap_plane(e1, CORE_SIDE)
    down_near, down_far = order.land(down_near, down_far)
    down_far = order(lambda meta, *parts: add_parts(meta, [(part, 0) for part in parts])[0], downs[2], down_far)
    (e1_other,) = order.land(e1_other)
    down_far = swap_depth(order.hold(down_far), 1)
    grad_heads, low_kept, low_sent, high_kept, high_sent = order(
        attention_backward, qkv, probs, attended, (e1, e1_other), (one_turned, one_other_turned), w_out, chips_attn
    )
    *rest_got, down_far = order.land(*rest_got, down_far)

    def onward(kept, got):
        return order(
            lambda meta, *args: add_parts(meta, *[((args[2 * k], QUARTER), (args[2 * k + 1], QUARTER)) for k in range(2)]),
            *[array for pair in zip(kept, got) for array in pair],
        )

    def arrived(kept, got, last):
        return order(
            lambda meta, *args: add_parts(meta, *[[(part, 0) for part in args[3 * k : 3 * k + 3]] for k in range(2)]),
            *[array for triple in zip(kept, got, last) for array in triple],
        )

    rest_kept = [kept for kept, _ in rest_sides]
    rest_sent = order.hold(onward(rest_kept, rest_got))
    rest_last = [swap_plane(sent, side) for sent, side in zip(rest_sent, second)]
    one_near, *one_across, sums_qkv = order(
        token_shares, grad_heads, w_query, w_key, w_value, chips_attn
    )
    one_got = [swap_plane(part, CORE_SIDE) for part in one_across]
    *rest_last, one_got[0], one_got[1] = order.land(*rest_last, *one_got)
    rest_own, rest_pair = arrived(rest_kept, rest_got, rest_last)
    low_sent, high_sent, rest_pair = order.hold((low_sent, high_sent, rest_pair))
    attn_got = [swap_plane(sent, side) for sent, side in zip((low_sent, high_sent), first)]
    rest_pair = swap_depth(rest_pair, 2)
    layer_out, grad_scale_mlp = order(
        layer_result, (downs[0], down_near, down_far), hidden, cotangent, vectors
    )
    grad_tokens, sums_one = order(token_gradient, one_near, *one_got, tokens, dh, vectors)

    totals = order(
        pack_small, (sums_one, sums_two, grad_scale_mlp, grad_b_down), sums_qkv, (near[3], far[3], far_other[3])
    )
    totals_got = swap_plane(totals, X_SIDE)
    *attn_got, rest_pair, totals_got = order.land(*attn_got, rest_pair, totals_got)
    attn_kept = (low_kept, high_kept)
    attn_sent = onward(attn_kept, attn_got)
    attn_last = [swap_plane(sent, side) for sent, side in zip(attn_sent, second)]
    grad_rest = order(lambda meta, *parts: add_parts(meta, [(part, 0) for part in parts])[0], rest_own, rest_pair)

    totals = order.plain(jnp.add, totals, totals_got)
    totals_got = swap_plane(totals, Y_SIDE)
    *attn_last, totals_got = order.land(*attn_last, totals_got)
    own_piece, pair_piece, level_sent = order(level_pieces, attn_kept, attn_got, attn_last)
    level_got = swap_depth(level_sent, 1)
    totals = order.plain(jnp.add, totals, totals_got)
    totals_got, grad_rest = order.hold((totals, grad_rest))
    rest_x, rest_y = swap_plane(grad_rest, X_SIDE), swap_plane(grad_rest, Y_SIDE)
    totals_got = swap_depth(totals_got, 1)
    level_got, rest_x, rest_y, totals_got = order.land(level_got, rest_x, rest_y, totals_got)
    level_kept, level_sent = order.plain(
        lambda own, pair, got: (add_low(own, got[0]), add_low(pair, got[1])), own_piece, pair_piece, level_got
    )
    totals = order.plain(jnp.add, totals, totals_got)
    totals_got, grad_rest, level_sent = order.hold((totals, grad_rest, level_sent))
    level_got = swap_depth(level_sent, 2)
    rest_corner = swap_plane(grad_rest, X_SIDE | Y_SIDE)
    totals_got = swap_depth(totals_got, 2)
    level_got, rest_corner, totals_got = order.land(level_got, rest_corner, totals_got)
    grad_attn = order.plain(add_low, level_kept, level_got)
    totals = order.plain(jnp.add, totals, totals_got)
    plane_attn = plane_swaps(order.hold(grad_attn))
    totals_got = swap_plane(order.hold(totals), CORE_SIDE)
    rest_mine = order.plain(lambda *parts: jnp.stack(parts), grad_rest, rest_x, rest_y, rest_corner)
    rest_other = swap_plane(order.hold(rest_mine), CORE_SIDE)
    (rest_other,) = order.land(rest_other)
    full_grad_up, full_grad_down = order(
        finish, rest_mine, rest_other, ((half_u, False), (half_u, True)), "finish_rest"
    )
    *plane_attn, totals_got = order.land(*plane_attn, totals_got)
    attn_mine = order.plain(lambda *parts: jnp.stack(parts), grad_attn, *plane_attn)
    attn_other = swap_plane(order.hold(attn_mine), CORE_SIDE)
    totals = order.plain(jnp.add, totals, totals_got)
    (attn_other,) = order.land(attn_other)
    full_grad_q, full_grad_k, full_grad_v, full_grad_o = order(
        finish, attn_mine, attn_other, ((BLOCK, False),) * 3 + ((BLOCK, True),), "finish_attn"
    )
    lines = width // BLOCK
    small_total = totals[: 8 * lines].reshape(8, width)
    shared_total = totals[8 * lines :].reshape(2, DEPTH, -1)
    shared_total = lax.dynamic_index_in_dim(shared_total, level, 1, keepdims=False)
    return (
        layer_out,
        grad_tokens,
        small_total[0],
        small_total[1],
        full_grad_q,
        shared_total[:, :BLOCK].reshape(-1),
        full_grad_k,
        full_grad_v,
        shared_total[:, BLOCK : 2 * BLOCK].reshape(-1),
        full_grad_o,
        small_total[5],
        small_total[4],
        small_total[2],
        small_total[3],
        full_grad_up,
        shared_total[:, 2 * BLOCK :].reshape(-1),
        full_grad_down,
        small_total[7],
        small_total[6],
    )


def local_general(
    tokens,
    slide_tiles,
    norm1_gain,
    norm1_bias,
    w_query,
    b_query,
    w_key,
    w_value,
    b_value,
    w_out,
    b_out,
    scale_attn,
    norm2_gain,
    norm2_bias,
    w_up,
    b_up,
    w_down,
    b_down,
    scale_mlp,
    cotangent,
):
    row_count = tokens.shape[0]
    per_slide = CROPS_DEV // SLIDES_DEV
    crop_index = (lax.axis_index("mp") * row_count + jnp.arange(row_count, dtype=jnp.int32)) // L
    slide_index = crop_index // per_slide
    owner = slide_index[:, None] == jnp.arange(SLIDES_DEV, dtype=jnp.int32)[None, :]
    limit_rows = jnp.sum(jnp.where(owner, slide_tiles[None, :], 0), axis=1)
    valid_rows = (crop_index % per_slide < limit_rows).astype(jnp.float32)[:, None]
    inputs = tokens.astype(jnp.float32)
    normed_one = layer_norm(inputs, norm1_gain, norm1_bias).astype(jnp.bfloat16)
    rows_one = lax.all_gather(normed_one, "mp", axis=0, tiled=True)
    queries = (jnp.dot(rows_one, w_query, preferred_element_type=jnp.float32) + b_query).astype(
        jnp.bfloat16
    )
    keys_all = jnp.dot(rows_one, w_key, preferred_element_type=jnp.float32).astype(jnp.bfloat16)
    values_all = (jnp.dot(rows_one, w_value, preferred_element_type=jnp.float32) + b_value).astype(
        jnp.bfloat16
    )
    heads_here = w_query.shape[1] // DH
    query_heads = to_heads(queries, heads_here)
    key_heads = to_heads(keys_all, heads_here)
    value_heads = to_heads(values_all, heads_here)
    scores = attn_scores(query_heads, key_heads)
    top_score = jnp.max(scores, axis=-1, keepdims=True)
    log_total = top_score + jnp.log(jnp.sum(jnp.exp(scores - top_score), axis=-1, keepdims=True))
    weights_low = jnp.exp(scores - log_total).astype(jnp.bfloat16)
    mixed_heads = jnp.einsum(
        "chqk,ckhd->cqhd", weights_low, value_heads, preferred_element_type=jnp.float32
    )
    attended = mixed_heads.reshape(queries.shape).astype(jnp.bfloat16)
    attn_sum = lax.psum_scatter(
        jnp.dot(attended, w_out, preferred_element_type=jnp.float32).astype(jnp.bfloat16),
        "mp",
        scatter_dimension=0,
        tiled=True,
    ).astype(jnp.float32)
    branch_one = attn_sum + b_out
    hidden_state = inputs + scale_attn * branch_one
    normed_two = layer_norm(hidden_state, norm2_gain, norm2_bias).astype(jnp.bfloat16)
    rows_two = lax.all_gather(normed_two, "mp", axis=0, tiled=True)
    up_pre = jnp.dot(rows_two, w_up, preferred_element_type=jnp.float32) + b_up
    activated = gelu_exact(up_pre).astype(jnp.bfloat16)
    down_sum = lax.psum_scatter(
        jnp.dot(activated, w_down, preferred_element_type=jnp.float32).astype(jnp.bfloat16),
        "mp",
        scatter_dimension=0,
        tiled=True,
    ).astype(jnp.float32)
    branch_two = down_sum + b_down
    layer_out = valid_rows * (hidden_state + scale_mlp * branch_two)
    grad_out = valid_rows * cotangent.astype(jnp.float32)
    grad_scale_mlp = jnp.sum(grad_out * branch_two, axis=0)
    grad_branch_two = scale_mlp * grad_out
    grad_b_down = jnp.sum(grad_branch_two, axis=0)
    grad_down_low = grad_branch_two.astype(jnp.bfloat16)
    gelu_value, gelu_back = jax.vjp(gelu_exact, up_pre)
    grad_down_rows = lax.all_gather(grad_down_low, "mp", axis=0, tiled=True)
    grad_act = contract_cols(grad_down_rows, w_down)
    grad_up = gelu_back(grad_act)[0].astype(jnp.bfloat16)
    grad_w_up = contract_rows(rows_two, grad_up)
    grad_w_down = contract_rows(activated, grad_down_rows)
    grad_b_up = jnp.sum(grad_up.astype(jnp.float32), axis=0)
    grad_rows_two = lax.psum_scatter(
        contract_cols(grad_up, w_up).astype(jnp.bfloat16), "mp", scatter_dimension=0, tiled=True
    ).astype(jnp.float32)
    norm2_value, norm2_back = jax.vjp(layer_norm, hidden_state, norm2_gain, norm2_bias)
    grad_hidden_norm, grad_norm2_gain, grad_norm2_bias = norm2_back(grad_rows_two)
    grad_hidden = grad_out + grad_hidden_norm
    grad_scale_attn = jnp.sum(grad_hidden * branch_one, axis=0)
    grad_branch_one = scale_attn * grad_hidden
    grad_b_out = jnp.sum(grad_branch_one, axis=0)
    grad_attn_low = grad_branch_one.astype(jnp.bfloat16)
    grad_attn_rows = lax.all_gather(grad_attn_low, "mp", axis=0, tiled=True)
    grad_w_out = contract_rows(attended, grad_attn_rows)
    grad_mixed = contract_cols(grad_attn_rows, w_out).astype(jnp.bfloat16)
    grad_mixed_heads = to_heads(grad_mixed, heads_here)
    scores_again = attn_scores(query_heads, key_heads)
    probs = jnp.exp(scores_again - log_total)
    probs_low = probs.astype(jnp.bfloat16)
    grad_value_heads = jnp.einsum(
        "chqk,cqhd->ckhd", probs_low, grad_mixed_heads, preferred_element_type=jnp.float32
    )
    grad_values = grad_value_heads.reshape(queries.shape).astype(jnp.bfloat16)
    grad_probs = jnp.einsum(
        "cqhd,ckhd->chqk", grad_mixed_heads, value_heads, preferred_element_type=jnp.float32
    )
    row_inner = jnp.sum(probs * grad_probs, axis=-1, keepdims=True)
    grad_scores = (probs * (grad_probs - row_inner)).astype(jnp.bfloat16)
    inverse_root = 1.0 / math.sqrt(DH)
    grad_query_heads = jnp.einsum(
        "chqk,ckhd->cqhd", grad_scores, key_heads, preferred_element_type=jnp.float32
    )
    grad_queries = (inverse_root * grad_query_heads).reshape(queries.shape).astype(jnp.bfloat16)
    grad_key_heads = jnp.einsum(
        "chqk,cqhd->ckhd", grad_scores, query_heads, preferred_element_type=jnp.float32
    )
    grad_keys = (inverse_root * grad_key_heads).reshape(queries.shape).astype(jnp.bfloat16)
    grad_w_query = contract_rows(rows_one, grad_queries)
    grad_b_query = jnp.sum(grad_queries.astype(jnp.float32), axis=0)
    grad_w_key = contract_rows(rows_one, grad_keys)
    grad_w_value = contract_rows(rows_one, grad_values)
    grad_b_value = jnp.sum(grad_values.astype(jnp.float32), axis=0)
    grad_rows_one = lax.psum_scatter(
        (
            contract_cols(grad_queries, w_query)
            + contract_cols(grad_keys, w_key)
            + contract_cols(grad_values, w_value)
        ).astype(jnp.bfloat16),
        "mp",
        scatter_dimension=0,
        tiled=True,
    ).astype(jnp.float32)
    norm1_value, norm1_back = jax.vjp(layer_norm, inputs, norm1_gain, norm1_bias)
    grad_in_norm, grad_norm1_gain, grad_norm1_bias = norm1_back(grad_rows_one)
    grad_tokens = grad_hidden + grad_in_norm
    small_stack = jnp.stack(
        [
            grad_norm1_gain,
            grad_norm1_bias,
            grad_norm2_gain,
            grad_norm2_bias,
            grad_scale_attn,
            grad_scale_mlp,
            grad_b_out,
            grad_b_down,
        ],
        axis=1,
    )
    small_total = lax.psum(small_stack.astype(jnp.bfloat16), "mp")
    (
        share_wq,
        share_bq,
        share_wk,
        share_wv,
        share_bv,
        share_wo,
        share_up,
        share_bup,
        share_down,
        share_small,
    ) = (
        lax.psum_scatter(
            grad_w_query.astype(jnp.bfloat16), "dp", scatter_dimension=0, tiled=True
        ).astype(jnp.float32),
        lax.psum_scatter(
            grad_b_query.astype(jnp.bfloat16), "dp", scatter_dimension=0, tiled=True
        ).astype(jnp.float32),
        lax.psum_scatter(
            grad_w_key.astype(jnp.bfloat16), "dp", scatter_dimension=0, tiled=True
        ).astype(jnp.float32),
        lax.psum_scatter(
            grad_w_value.astype(jnp.bfloat16), "dp", scatter_dimension=0, tiled=True
        ).astype(jnp.float32),
        lax.psum_scatter(
            grad_b_value.astype(jnp.bfloat16), "dp", scatter_dimension=0, tiled=True
        ).astype(jnp.float32),
        lax.psum_scatter(
            grad_w_out.astype(jnp.bfloat16), "dp", scatter_dimension=0, tiled=True
        ).astype(jnp.float32),
        lax.psum_scatter(
            grad_w_up.astype(jnp.bfloat16), "dp", scatter_dimension=0, tiled=True
        ).astype(jnp.float32),
        lax.psum_scatter(
            grad_b_up.astype(jnp.bfloat16), "dp", scatter_dimension=0, tiled=True
        ).astype(jnp.float32),
        lax.psum_scatter(
            grad_w_down.astype(jnp.bfloat16), "dp", scatter_dimension=0, tiled=True
        ).astype(jnp.float32),
        lax.psum_scatter(small_total, "dp", scatter_dimension=0, tiled=True).astype(jnp.float32),
    )
    (
        full_wq,
        full_bq,
        full_wk,
        full_wv,
        full_bv,
        full_wo,
        full_up,
        full_bup,
        full_down,
        full_small,
    ) = (
        lax.all_gather(share_wq.astype(jnp.bfloat16), "dp", axis=0, tiled=True).astype(
            share_wq.dtype
        ),
        lax.all_gather(share_bq.astype(jnp.bfloat16), "dp", axis=0, tiled=True).astype(
            share_bq.dtype
        ),
        lax.all_gather(share_wk.astype(jnp.bfloat16), "dp", axis=0, tiled=True).astype(
            share_wk.dtype
        ),
        lax.all_gather(share_wv.astype(jnp.bfloat16), "dp", axis=0, tiled=True).astype(
            share_wv.dtype
        ),
        lax.all_gather(share_bv.astype(jnp.bfloat16), "dp", axis=0, tiled=True).astype(
            share_bv.dtype
        ),
        lax.all_gather(share_wo.astype(jnp.bfloat16), "dp", axis=0, tiled=True).astype(
            share_wo.dtype
        ),
        lax.all_gather(share_up.astype(jnp.bfloat16), "dp", axis=0, tiled=True).astype(
            share_up.dtype
        ),
        lax.all_gather(share_bup.astype(jnp.bfloat16), "dp", axis=0, tiled=True).astype(
            share_bup.dtype
        ),
        lax.all_gather(share_down.astype(jnp.bfloat16), "dp", axis=0, tiled=True).astype(
            share_down.dtype
        ),
        lax.all_gather(share_small.astype(jnp.bfloat16), "dp", axis=0, tiled=True).astype(
            share_small.dtype
        ),
    )
    return (
        layer_out,
        grad_tokens,
        full_small[:, 0],
        full_small[:, 1],
        full_wq,
        full_bq,
        full_wk,
        full_wv,
        full_bv,
        full_wo,
        full_small[:, 6],
        full_small[:, 4],
        full_small[:, 2],
        full_small[:, 3],
        full_up,
        full_bup,
        full_down,
        full_small[:, 7],
        full_small[:, 5],
    )


def solution(mesh):
    in_specs = (
        P(("dp", "mp"), None),
        P("dp"),
        P(),
        P(),
        P(None, "mp"),
        P("mp"),
        P(None, "mp"),
        P(None, "mp"),
        P("mp"),
        P("mp", None),
        P(),
        P(),
        P(),
        P(),
        P(None, "mp"),
        P("mp"),
        P("mp", None),
        P(),
        P(),
        P(("dp", "mp"), None),
    )
    out_specs = (
        P(("dp", "mp"), None),
        P(("dp", "mp"), None),
        P(),
        P(),
        P(None, "mp"),
        P("mp"),
        P(None, "mp"),
        P(None, "mp"),
        P("mp"),
        P("mp", None),
        P(),
        P(),
        P(),
        P(),
        P(None, "mp"),
        P("mp"),
        P("mp", None),
        P(),
        P(),
    )
    paired = mesh.shape["dp"] == 8 and mesh.shape["mp"] == 4
    local = local_paired if paired else local_general
    return jax.shard_map(local, mesh=mesh, in_specs=in_specs, out_specs=out_specs, check_vma=False)
```

```python
import functools
import math

import jax
import jax.numpy as jnp
from jax import lax
from jax.experimental import pallas as pl
from jax.experimental.pallas import tpu as pltpu
from jax.sharding import PartitionSpec as P

DH = 64
L = 197
SLIDES_DEV = 2
CROPS_DEV = 8


def layer_norm(values, gain, shift):
    average = jnp.mean(values, axis=-1, keepdims=True)
    centered = values - average
    spread = jnp.mean(centered * centered, axis=-1, keepdims=True)
    return centered * lax.rsqrt(spread + 1e-06) * gain + shift


def gelu_exact(values):
    return jax.nn.gelu(values, approximate=False)


def contract_rows(left, right):
    return lax.dot_general(
        left, right, (((0,), (0,)), ((), ())), preferred_element_type=jnp.float32
    )


def contract_cols(left, right):
    return lax.dot_general(
        left, right, (((1,), (1,)), ((), ())), preferred_element_type=jnp.float32
    )


def to_heads(matrix, heads_here):
    return matrix.reshape(matrix.shape[0] // L, L, heads_here, DH)


def attn_scores(query_heads, key_heads):
    product = jnp.einsum(
        "cqhd,ckhd->chqk", query_heads, key_heads, preferred_element_type=jnp.float32
    )
    return product * (1.0 / math.sqrt(DH))


BLOCK = 128
QUARTER = 256
X_SIDE, Y_SIDE, CORE_SIDE = 2, 4, 1
PLANE = 8
CHIPS = 4
DEPTH = 4
OWN_CORE = CHIPS
OWN_LEVEL = CHIPS + 1
FLAGS = CHIPS + 2
GAIN_ONE, SHIFT_ONE, GAIN_TWO, SHIFT_TWO, SCALE_ATTN, SCALE_MLP, BIAS_OUT, BIAS_DOWN = range(8)
VMEM_BYTES = 24 * 2**20
NEAR_BYTES = 28 * 2**20
PARTS_BYTES = 24 * 2**20
NORM_BYTES = 24 * 2**20
BACK_BYTES = 24 * 2**20
PIECES_BYTES = 24 * 2**20


def swap_plane(values, mask):
    return lax.ppermute(values, "dp", [(i, i ^ mask) for i in range(PLANE)])


def swap_depth(values, mask):
    return lax.ppermute(values, "mp", [(i, i ^ mask) for i in range(DEPTH)])


def plane_swaps(values):
    return [swap_plane(values, side) for side in (X_SIDE, Y_SIDE, X_SIDE | Y_SIDE)]


class Order:
    def __init__(self, meta):
        self.meta = meta

    def hold(self, values):
        leaves, tree = jax.tree.flatten(values)
        *leaves, self.meta = lax.optimization_barrier(tuple(leaves) + (self.meta,))
        return jax.tree.unflatten(tree, leaves)

    def land(self, *arrays):
        return self.hold(list(arrays))

    def __call__(self, step, *args):
        return self.hold(step(self.meta, *args))

    def plain(self, step, *args):
        return self.hold(step(*self.hold(args)))


def dot_nt(left, right):
    return lax.dot_general(left, right, (((1,), (1,)), ((), ())), preferred_element_type=jnp.float32)


def dot_tn(left, right):
    return lax.dot_general(left, right, (((0,), (0,)), ((), ())), preferred_element_type=jnp.float32)


def dot_nn(left, right):
    return lax.dot_general(left, right, (((1,), (0,)), ((), ())), preferred_element_type=jnp.float32)


def add_low(*values):
    return sum(value.astype(jnp.float32) for value in values).astype(jnp.bfloat16)


def crop_ranges(rows):
    ranges = []
    for crop in range(rows // L):
        low = crop * L // 16 * 16
        high = min((crop + 1) * L + 15, rows + 15) // 16 * 16
        ranges.append((low, min(high, rows), crop * L - low))
    return ranges


def add_parts(meta, *sums):
    rows = [len(parts) for parts in sums]
    flat = [part for parts in sums for part in parts]
    heights = [min(array.shape[0] - start for array, start in parts) for parts in sums]

    def body(meta_ref, *refs):
        at = 0
        for count, out_ref in zip(rows, refs[len(flat) :]):
            out_ref[...] = add_low(*[ref[...] for ref in refs[at : at + count]])
            at += count

    in_specs, out = [], []
    for parts, height in zip(sums, heights):
        for array, start in parts:
            in_specs.append(pl.BlockSpec((height, array.shape[1]), lambda i, m, b=start // height: (b, 0)))
        out.append(shape_of(height, parts[0][0].shape[1]))
    return kernel_call(
        body, "add_parts", meta, [array for array, _ in flat], in_specs, out, [whole(o) for o in out], vmem=PARTS_BYTES
    )


def level_pieces(meta, kept, got, last):
    half = kept[0].shape[1] // 2

    def body(meta_ref, *refs):
        own_ref, pair_ref, send_ref = refs[6:]
        for lane, near_ref in enumerate((own_ref, pair_ref)):
            total = add_low(*[ref[...] for ref in refs[3 * lane : 3 * lane + 3]])
            heads = 3 * half // 4
            near_ref[:, :heads] = total[:, :heads]
            near_ref[:, heads:] = total[:, 2 * heads : heads + half]
            send_ref[lane, :, :heads] = total[:, heads : 2 * heads]
            send_ref[lane, :, heads:] = total[:, heads + half :]

    first = pl.BlockSpec((QUARTER, 2 * half), lambda i, m: (0, 0))
    args = [array for triple in zip(kept, got, last) for array in triple]
    out = [shape_of(QUARTER, half)] * 2 + [shape_of(2, QUARTER, half)]
    return kernel_call(
        body, "level_pieces", meta, args, [first] * 6, out, [whole(o) for o in out], vmem=PIECES_BYTES
    )


def whole(array):
    zeros = (0,) * array.ndim
    return pl.BlockSpec(array.shape, lambda *_: zeros)


def kernel_call(body, name, meta, args, in_specs, out_shape, out_specs, grid=(1,), scratch=(), flops=1000, vmem=VMEM_BYTES):
    return pl.pallas_call(
        body,
        grid_spec=pltpu.PrefetchScalarGridSpec(
            num_scalar_prefetch=1,
            grid=grid,
            in_specs=in_specs,
            out_specs=out_specs,
            scratch_shapes=list(scratch),
        ),
        out_shape=out_shape,
        compiler_params=pltpu.CompilerParams(vmem_limit_bytes=vmem),
        cost_estimate=pl.CostEstimate(flops=flops, bytes_accessed=1000, transcendentals=0),
        name=name,
    )(meta, *args)


def shape_of(*dims, dtype=jnp.bfloat16):
    return jax.ShapeDtypeStruct(dims, dtype)


def normalized(values):
    centered = values - jnp.mean(values, axis=-1, keepdims=True)
    inverse = lax.rsqrt(jnp.mean(centered * centered, axis=-1, keepdims=True) + 1e-06)
    return centered * inverse, inverse


def norm_gradient(unit, inverse, gain, grad):
    wide = grad * gain
    return inverse * (
        wide - jnp.mean(wide, axis=-1, keepdims=True) - unit * jnp.mean(wide * unit, axis=-1, keepdims=True)
    )


def valid_column(meta_ref, rows):
    row = lax.broadcasted_iota(jnp.int32, (rows, 1), 0)
    valid = jnp.zeros((rows, 1), jnp.float32)
    for crop in range(rows // L):
        inside = (row >= crop * L) & (row < (crop + 1) * L)
        valid = jnp.where(inside, meta_ref[FLAGS + crop].astype(jnp.float32), valid)
    return valid


def quarter_of(meta_ref, side):
    return pl.ds(pl.multiple_of(meta_ref[side] * QUARTER, QUARTER), QUARTER)


def slice_weights(meta, w_query, w_key, w_value, w_out, w_up, w_down, b_query, b_value, b_up):
    half_h, half_u = w_query.shape[1] // 2, w_up.shape[1] // 2
    n_h, n_u = half_h // BLOCK, half_u // BLOCK

    def body(meta_ref, q_ref, k_ref, v_ref, o_ref, up_ref, down_ref, bq_ref, bv_ref, bu_ref, attn_ref, rest_ref):
        core = meta_ref[OWN_CORE]
        for which, ref in enumerate((q_ref, k_ref, v_ref)):
            attn_ref[which * QUARTER : (which + 1) * QUARTER, :] = ref[...]
        for b in range(2):
            row = 3 * QUARTER + b * half_h
            attn_ref[row : row + half_h, :] = o_ref[:, b * BLOCK : (b + 1) * BLOCK]
        picked = jnp.concatenate(
            [
                bq_ref[pl.ds(core * n_h, n_h), :],
                bv_ref[pl.ds(core * n_h, n_h), :],
                bu_ref[pl.ds(core * n_u, n_u), :],
            ],
            axis=0,
        )
        high = picked.astype(jnp.bfloat16)
        low = (picked - high.astype(jnp.float32)).astype(jnp.bfloat16)
        spare = jnp.zeros((16 - 2 * picked.shape[0], BLOCK), jnp.bfloat16)
        attn_ref[4 * QUARTER :, :] = jnp.concatenate([high, low, spare], axis=0)
        for b in range(n_u):
            rest_ref[b * QUARTER : (b + 1) * QUARTER, :] = up_ref[:, b * BLOCK : (b + 1) * BLOCK]
        for b in range(2):
            row = n_u * QUARTER + b * half_u
            rest_ref[row : row + half_u, :] = down_ref[:, b * BLOCK : (b + 1) * BLOCK]

    args = (w_query, w_key, w_value, w_out, w_up, w_down, b_query, b_value, b_up)
    out = [shape_of(4 * QUARTER + 16, BLOCK), shape_of(2 * n_u * QUARTER, BLOCK)]
    return kernel_call(
        body,
        "slice_weights",
        meta,
        args,
        [pl.BlockSpec((QUARTER, half_h), lambda i, m: (m[0], m[OWN_CORE]))] * 3
        + [
            pl.BlockSpec((half_h, QUARTER), lambda i, m: (m[OWN_CORE], m[0])),
            pl.BlockSpec((QUARTER, half_u), lambda i, m: (m[0], m[OWN_CORE])),
            pl.BlockSpec((half_u, QUARTER), lambda i, m: (m[OWN_CORE], m[0])),
            whole(b_query),
            whole(b_value),
            whole(b_up),
        ],
        out,
        [whole(o) for o in out],
        vmem=60 * 2**20,
    )


def turn_into(meta_ref, values, turned_ref, index=None):
    for side in range(CHIPS):
        rows = slice(side * QUARTER, (side + 1) * QUARTER)
        if index is None:
            turned_ref[rows, :] = values[:, quarter_of(meta_ref, side)].T
        else:
            turned_ref[rows, :] = values[index, :, quarter_of(meta_ref, side)].T


def turn(meta, *arrays):
    def body(meta_ref, *refs):
        for source, target in zip(refs[: len(arrays)], refs[len(arrays) :]):
            turn_into(meta_ref, source, target)

    out = [shape_of(*a.shape[::-1]) for a in arrays]
    return kernel_call(body, "turn", meta, arrays, [whole(a) for a in arrays], out, [whole(o) for o in out])


def prepare(meta, tokens, tokens_other, cotangent, vectors):
    rows, width = tokens.shape

    def body(meta_ref, tokens_ref, other_ref, cot_ref, vec_ref, one_ref, two_ref, grad_ref, sum_ref, *turned):
        for source, target in ((tokens_ref, one_ref), (other_ref, two_ref)):
            unit, _ = normalized(source[...].astype(jnp.float32))
            target[...] = (unit * vec_ref[GAIN_ONE : GAIN_ONE + 1] + vec_ref[SHIFT_ONE : SHIFT_ONE + 1]).astype(
                jnp.bfloat16
            )
        grad = vec_ref[SCALE_MLP : SCALE_MLP + 1] * (valid_column(meta_ref, rows) * cot_ref[...].astype(jnp.float32))
        sum_ref[...] = jnp.sum(grad, axis=0, keepdims=True)
        grad_ref[...] = grad.astype(jnp.bfloat16)
        for source, target in zip((one_ref, two_ref, grad_ref), turned):
            turn_into(meta_ref, source, target)

    args = (tokens, tokens_other, cotangent, vectors)
    out = [shape_of(rows, width)] * 3 + [shape_of(1, width, dtype=jnp.float32)] + [shape_of(width, rows)] * 3
    return kernel_call(body, "prepare", meta, args, [whole(a) for a in args], out, [whole(o) for o in out])


def fill_heads(meta_ref, chip_refs, weight_ref):
    for side, ref in enumerate(chip_refs):
        at = quarter_of(meta_ref, side)
        for which in range(3):
            weight_ref[at, which * BLOCK : (which + 1) * BLOCK] = ref[which * QUARTER : (which + 1) * QUARTER, :]


def head_specs(width, chips):
    own = [pl.BlockSpec((width, BLOCK), lambda g, m: (0, m[OWN_CORE]))] * 3
    far = [pl.BlockSpec((4 * QUARTER, BLOCK), lambda g, m: (jnp.maximum(g - 1, 0), 0))] * len(chips)
    return own, far


def attention_forward(meta, normed, other, w_query, w_key, w_value, b_query, b_value, level_attn, chips, w_count):
    rows, width = normed.shape
    group = 3 * BLOCK
    ranges = crop_ranges(rows)
    span = max(high - low for low, high, _ in ranges)
    scale = 1.0 / math.sqrt(DH)
    count = 2 + w_count

    def body(meta_ref, normed_ref, other_ref, q_ref, k_ref, v_ref, bq_ref, bv_ref, one_ref, two_ref, three_ref, *refs):
        chip_refs, (qkv_ref, out_ref, prob_ref, weight_ref, sum_ref) = refs[:CHIPS], refs[CHIPS:]
        group_here = pl.program_id(0)
        core = meta_ref[OWN_CORE]

        @pl.when(group_here == 0)
        def _():
            for which, ref in enumerate((q_ref, k_ref, v_ref)):
                weight_ref[:, which * BLOCK : (which + 1) * BLOCK] = ref[...]
            sum_ref[0:1, :] = bq_ref[pl.ds(core, 1), :]
            sum_ref[1:2, :] = bv_ref[pl.ds(core, 1), :]

        for index, ref in enumerate((one_ref, two_ref, three_ref)):
            @pl.when(group_here == index + 1)
            def _():
                both = ref[...].astype(jnp.float32)
                sum_ref[0:2, :] = both[0:2] + both[count : count + 2]

        @pl.when(group_here > 0)
        def _():
            fill_heads(meta_ref, chip_refs, weight_ref)

        bias = jnp.concatenate([sum_ref[0:1, :], jnp.zeros((1, BLOCK), jnp.float32), sum_ref[1:2, :]], axis=1)
        for part, rows_ref in enumerate((normed_ref, other_ref)):
            qkv_ref[part] = (dot_nn(rows_ref[...], weight_ref[...]) + bias).astype(jnp.bfloat16)
        for part in range(2):
            for index, (low, high, skip) in enumerate(ranges):
                size = high - low
                query = qkv_ref[part, low:high, 0:BLOCK]
                key = qkv_ref[part, low:high, BLOCK : 2 * BLOCK]
                value = qkv_ref[part, low:high, 2 * BLOCK : 3 * BLOCK]
                lane = lax.broadcasted_iota(jnp.int32, (size, BLOCK), 1)
                row = lax.broadcasted_iota(jnp.int32, (size, size), 0)
                column = lax.broadcasted_iota(jnp.int32, (size, size), 1)
                seen = (column >= skip) & (column < skip + L)
                inside = seen & (row >= skip) & (row < skip + L)
                parts = []
                for head in range(2):
                    own = (lane < DH) if head == 0 else (lane >= DH)
                    scores = dot_nt(jnp.where(own, query, jnp.zeros_like(query)), key) * scale
                    scores = jnp.where(seen, scores, -1e30)
                    top = jnp.max(scores, axis=1, keepdims=True)
                    raised = jnp.exp(scores - top)
                    total = jnp.sum(raised, axis=1, keepdims=True)
                    probs = jnp.where(inside, raised * (1.0 / total), 0.0).astype(jnp.bfloat16)
                    prob_ref[0, part, index, head, 0:size, 0:size] = probs
                    parts.append(dot_nn(probs, value))
                mixed = jnp.where(lane < DH, parts[0], parts[1]).astype(jnp.bfloat16)
                if skip:
                    edge = lax.broadcasted_iota(jnp.int32, (size, BLOCK), 0) >= skip
                    mixed = jnp.where(edge, mixed, out_ref[part, low:high, :])
                out_ref[part, low:high, :] = mixed

    prob_shape = (DEPTH, 2, len(ranges), 2, span, span)
    own_specs, far_specs = head_specs(width, chips)
    tail = 4 * QUARTER // 16
    args = (normed, other, w_query, w_key, w_value, b_query, b_value) + tuple(level_attn) + tuple(chips)
    return kernel_call(
        body,
        "attention_forward",
        meta,
        args,
        [whole(normed), whole(other)] + own_specs + [whole(b_query), whole(b_value)] + [pl.BlockSpec((16, BLOCK), lambda g, m: (tail, 0))] * 3 + far_specs,
        [shape_of(2, rows, DEPTH * group), shape_of(2, rows, DEPTH * BLOCK), shape_of(*prob_shape)],
        [
            pl.BlockSpec((2, rows, group), lambda g, m: (0, 0, g)),
            pl.BlockSpec((2, rows, BLOCK), lambda g, m: (0, 0, g)),
            pl.BlockSpec((1,) + prob_shape[1:], lambda g, m: (g, 0, 0, 0, 0, 0)),
        ],
        grid=(DEPTH,),
        scratch=[pltpu.VMEM((width, group), jnp.bfloat16), pltpu.VMEM((8, BLOCK), jnp.float32)],
    )


def attention_out(meta, attended, w_out, chips):
    rows, width = attended.shape[1], w_out.shape[1]

    def body(meta_ref, attended_ref, own_ref, *refs):
        chip_refs, (near_ref, low_ref, high_ref, weight_ref) = refs[:CHIPS], refs[CHIPS:]
        weight_ref[0:BLOCK, :] = own_ref[...]
        for side, ref in enumerate(chip_refs):
            start = pl.multiple_of(meta_ref[side] * QUARTER, QUARTER)
            for index in range(DEPTH - 1):
                for b in range(2):
                    weight_ref[(index + 1) * BLOCK : (index + 2) * BLOCK, pl.ds(start + b * BLOCK, BLOCK)] = ref[
                        index, b * BLOCK : (b + 1) * BLOCK, :
                    ]
        near_ref[...] = dot_nn(attended_ref[0], weight_ref[...])
        across = dot_nn(attended_ref[1], weight_ref[...]).astype(jnp.bfloat16)
        low_ref[...] = across[:, : width // 2]
        high_ref[...] = across[:, width // 2 :]

    views = tuple(chip.reshape(DEPTH - 1, 4 * QUARTER, BLOCK) for chip in chips)
    view_spec = pl.BlockSpec((DEPTH - 1, QUARTER, BLOCK), lambda i, m: (0, 3, 0))
    out = [shape_of(rows, width, dtype=jnp.float32)] + [shape_of(rows, width // 2)] * 2
    return kernel_call(
        body, "attention_out", meta, (attended, w_out) + views,
        [whole(attended), pl.BlockSpec((BLOCK, width), lambda i, m: (m[OWN_CORE], 0))] + [view_spec] * CHIPS,
        out, [whole(o) for o in out], scratch=[pltpu.VMEM((DEPTH * BLOCK, width), jnp.bfloat16)],
    )


def attention_norm(meta, near, low, high, tokens, vectors):
    rows, width = tokens.shape

    def body(meta_ref, near_ref, low_ref, high_ref, tokens_ref, vec_ref, hidden_ref, branch_ref, normed_ref):
        got = jnp.concatenate([low_ref[...], high_ref[...]], axis=1).astype(jnp.float32)
        branch = near_ref[...] + got + vec_ref[BIAS_OUT : BIAS_OUT + 1]
        branch_ref[...] = branch
        hidden = tokens_ref[...].astype(jnp.float32) + vec_ref[SCALE_ATTN : SCALE_ATTN + 1] * branch
        hidden_ref[...] = hidden
        unit, _ = normalized(hidden)
        normed = (unit * vec_ref[GAIN_TWO : GAIN_TWO + 1] + vec_ref[SHIFT_TWO : SHIFT_TWO + 1]).astype(jnp.bfloat16)
        normed_ref[...] = normed

    args = (near, low, high, tokens, vectors)
    out = [shape_of(rows, width, dtype=jnp.float32)] * 2 + [shape_of(rows, width)]
    return kernel_call(body, "attention_norm", meta, args, [whole(a) for a in args], out, [whole(o) for o in out], vmem=NORM_BYTES)


def feed_rows(normed_pieces, grad, up_weight, down_weight, bias, act_ref, gup_ref, low, high):
    width = up_weight.shape[0]
    deep = width // len(normed_pieces)
    pre = bias[:, low:high] + sum(
        dot_nn(piece[...], up_weight[k * deep : (k + 1) * deep, low:high]) for k, piece in enumerate(normed_pieces)
    )
    spread = 0.5 * (1.0 + lax.erf(pre * (1.0 / math.sqrt(2.0))))
    act_ref[:, low:high] = (pre * spread).astype(jnp.bfloat16)
    slope = spread + pre * jnp.exp(-0.5 * pre * pre) * (1.0 / math.sqrt(2.0 * math.pi))
    grad_up = (dot_nt(grad[...], down_weight[low:high, :]) * slope).astype(jnp.bfloat16)
    gup_ref[:, low:high] = grad_up
    return jnp.sum(grad_up.astype(jnp.float32), axis=0, keepdims=True)


def feed_near(meta, normed, grads, w_up, w_down, bias_up, chips):
    rows, width = grads[0].shape
    normed = [part if isinstance(part, (list, tuple)) else [part] for part in normed]
    flat = [piece for part in normed for piece in part]
    half_u = w_up.shape[1] // 2
    n_u = half_u // BLOCK
    count = len(normed)
    copies = len(flat) + count + 2 + CHIPS * (n_u + 2)

    def body(meta_ref, *refs):
        bias_ref, flat_hbm, refs = refs[0], refs[1 : 1 + len(flat)], refs[1 + len(flat) :]
        grad_hbm, refs = refs[:count], refs[count:]
        up_hbm, down_hbm, chip_refs, refs = refs[0], refs[1], refs[2 : 2 + CHIPS], refs[2 + CHIPS :]
        act_refs, gup_refs, back_refs, refs = refs[:count], refs[count : 2 * count], refs[2 * count : 3 * count], refs[3 * count :]
        sum_ref, up_weight, down_weight, normed_ref, grad_ref, sems = refs
        half = pl.ds(pl.multiple_of(meta_ref[OWN_CORE] * half_u, half_u), half_u)
        pieces = []
        for part, cut in enumerate(normed):
            deep = width // len(cut)
            for k in range(len(cut)):
                pieces.append((part, (flat_hbm[len(pieces)], normed_ref.at[part, :, pl.ds(k * deep, deep)])))
        moves = [move for part, move in pieces if part == 0]
        moves += [
            (up_hbm.at[:, half], up_weight.at[:, pl.ds(0, half_u)]),
            (grad_hbm[0], grad_ref.at[0]),
            (down_hbm.at[half, :], down_weight.at[pl.ds(0, half_u), :]),
        ]
        for part in range(1, count):
            moves += [move for owner, move in pieces if owner == part] + [(grad_hbm[part], grad_ref.at[part])]
        near_moves = len(moves)
        for side, ref in enumerate(chip_refs):
            start = pl.multiple_of(meta_ref[side] * QUARTER, QUARTER)
            for b in range(n_u):
                moves.append(
                    (
                        ref.at[pl.ds(b * QUARTER, QUARTER), :],
                        up_weight.at[pl.ds(start, QUARTER), pl.ds(half_u + b * BLOCK, BLOCK)],
                    )
                )
            for b in range(2):
                moves.append(
                    (
                        ref.at[pl.ds(n_u * QUARTER + b * half_u, half_u), :],
                        down_weight.at[pl.ds(half_u, half_u), pl.ds(start + b * BLOCK, BLOCK)],
                    )
                )
        handles = [pltpu.make_async_copy(source, target, sems.at[k]) for k, (source, target) in enumerate(moves)]
        for handle in handles:
            handle.start()
        for tile, waits in enumerate((handles[:near_moves], handles[near_moves:])):
            for handle in waits:
                handle.wait()
            low, high = tile * half_u, (tile + 1) * half_u
            sums = [
                feed_rows([normed_ref.at[p]], grad_ref.at[p], up_weight, down_weight, bias_ref, act_refs[p], gup_refs[p], low, high)
                for p in range(count)
            ]
            sum_ref[:, low:high] = sum(sums)
        for part in range(count):
            back_refs[part][...] = dot_nt(gup_refs[part][...], up_weight[...]).astype(jnp.bfloat16)

    anywhere = pl.BlockSpec(memory_space=pl.ANY)
    out = [shape_of(rows, 2 * half_u)] * (2 * count) + [shape_of(rows, width)] * count
    out += [shape_of(1, 2 * half_u, dtype=jnp.float32), shape_of(width, 2 * half_u), shape_of(2 * half_u, width)]
    args = tuple(flat) + tuple(grads) + (w_up, w_down) + tuple(chips)
    outs = kernel_call(
        body, "feed_near", meta, (bias_up,) + args, [whole(bias_up)] + [anywhere] * len(args), out, [whole(o) for o in out],
        scratch=[pltpu.VMEM((count, rows, width), jnp.bfloat16)] * 2 + [pltpu.SemaphoreType.DMA((copies,))],
        vmem=NEAR_BYTES,
    )
    return outs[:count], outs[count : 2 * count], outs[2 * count : 3 * count], outs[3 * count], outs[3 * count + 1], outs[3 * count + 2]


def feed_far(meta, normed, grad, bias_up, full_up, full_down):
    rows, width = grad.shape
    units = full_up.shape[1]
    pieces = len(normed)

    def body(meta_ref, *refs):
        normed_refs = refs[:pieces]
        grad_ref, bias_ref, up_ref, down_ref, act_ref, gup_ref, back_ref, sum_ref = refs[pieces:]
        for tile in range(2):
            low, high = tile * units // 2, (tile + 1) * units // 2
            sum_ref[:, low:high] = feed_rows(
                normed_refs, grad_ref, up_ref, down_ref, bias_ref, act_ref, gup_ref, low, high
            )
        back_ref[...] = dot_nt(gup_ref[...], up_ref[...]).astype(jnp.bfloat16)

    args = tuple(normed) + (grad, bias_up, full_up, full_down)
    out = [shape_of(rows, units)] * 2 + [shape_of(rows, width), shape_of(1, units, dtype=jnp.float32)]
    return kernel_call(body, "feed_far", meta, args, [whole(a) for a in args], out, [whole(o) for o in out])


def feed_down(meta, acts, full_down):
    rows, width = acts[0].shape[0], full_down.shape[1]
    count = len(acts)

    def body(meta_ref, *refs):
        weight_ref = refs[count]
        for act_ref, out_ref in zip(refs[:count], refs[count + 1 :]):
            out_ref[...] = dot_nn(act_ref[...], weight_ref[...]).astype(jnp.bfloat16)

    args = tuple(acts) + (full_down,)
    out = [shape_of(rows, width)] * count
    return kernel_call(body, "feed_down", meta, args, [whole(a) for a in args], out, [whole(o) for o in out])


def put_sides(lane, values, keep_ref, send_ref, at):
    keep, send = ((0, 2), (1, 3)) if lane == 0 else ((0, 1), (2, 3))
    for ref, sides in ((keep_ref, keep), (send_ref, send)):
        for index, side in enumerate(sides):
            ref[index * QUARTER : (index + 1) * QUARTER, at] = values[side * QUARTER : (side + 1) * QUARTER].astype(
                jnp.bfloat16
            )


def feed_gradients(meta, normed, turned_grads, gups, acts):
    normed = [part if isinstance(part, (list, tuple)) else [part] for part in normed]
    flat = [piece for part in normed for piece in part]
    rows = flat[0].shape[0]
    width = turned_grads[0].shape[0]
    half_u = gups[0].shape[1] // 2
    n = len(gups)

    def body(meta_ref, *refs):
        normed_refs, refs = refs[: len(flat)], refs[len(flat) :]
        turned_refs, gup_refs, act_refs, refs = refs[:n], refs[n : 2 * n], refs[2 * n : 3 * n], refs[3 * n :]
        outs, own_turned, whole_ref = refs[:4], refs[4:-1], refs[-1]
        step = pl.program_id(0)

        @pl.when(step == 0)
        def _():
            at = 0
            for part, target in zip(normed, own_turned):
                if len(part) == 1:
                    turn_into(meta_ref, normed_refs[at], target)
                else:
                    deep = width // len(part)
                    for k in range(len(part)):
                        whole_ref[:, k * deep : (k + 1) * deep] = normed_refs[at + k][...]
                    turn_into(meta_ref, whole_ref, target)
                at += len(part)

        def product(lefts, rights):
            return sum(dot_nn(left[...], right[...]) for left, right in zip(lefts, rights))

        for lane in range(2):
            kept, sent = outs[2 * lane : 2 * lane + 2]

            @pl.when(step == 2 * lane)
            def _():
                put_sides(lane, product(own_turned, gup_refs), kept, sent, slice(None))

            @pl.when(step == 2 * lane + 1)
            def _():
                put_sides(lane, product(turned_refs, act_refs), kept, sent, slice(None))

    args = tuple(flat) + tuple(turned_grads)
    by_lane = [pl.BlockSpec((rows, half_u), lambda g, m: (0, g >> 1))] * (2 * n)
    out_specs = [pl.BlockSpec((2 * QUARTER, half_u), lambda g, m: (0, jnp.minimum(g, 1)))] * 2
    out_specs += [pl.BlockSpec((2 * QUARTER, half_u), lambda g, m: (0, jnp.maximum(g - 2, 0)))] * 2
    outs = kernel_call(
        body, "feed_gradients", meta, args + tuple(gups) + tuple(acts),
        [whole(a) for a in args] + by_lane, [shape_of(2 * QUARTER, 2 * half_u)] * 4, out_specs, grid=(4,),
        scratch=[pltpu.VMEM((width, rows), jnp.bfloat16)] * 4 + [pltpu.VMEM((rows, width), jnp.bfloat16)],
    )
    return outs[:2], outs[2:]


def hidden_gradient(meta, backs, hidden, branch, cotangent, vectors):
    rows, width = hidden.shape

    def body(meta_ref, *refs):
        back_refs, (hidden_ref, branch_ref, cot_ref, vec_ref, dh_ref, e1_ref, sum_ref) = refs[: len(backs)], refs[len(backs) :]
        grad = sum(ref[...].astype(jnp.float32) for ref in back_refs)
        unit, inverse = normalized(hidden_ref[...])
        sum_ref[0:1, :] = jnp.sum(grad * unit, axis=0, keepdims=True)
        sum_ref[1:2, :] = jnp.sum(grad, axis=0, keepdims=True)
        total = valid_column(meta_ref, rows) * cot_ref[...].astype(jnp.float32) + norm_gradient(
            unit, inverse, vec_ref[GAIN_TWO : GAIN_TWO + 1], grad
        )
        dh_ref[...] = total
        sum_ref[2:3, :] = jnp.sum(total * branch_ref[...], axis=0, keepdims=True)
        scaled = vec_ref[SCALE_ATTN : SCALE_ATTN + 1] * total
        sum_ref[3:4, :] = jnp.sum(scaled, axis=0, keepdims=True)
        e1_ref[...] = scaled.astype(jnp.bfloat16)

    args = tuple(backs) + (hidden, branch, cotangent, vectors)
    out = [shape_of(rows, width, dtype=jnp.float32), shape_of(rows, width), shape_of(4, width, dtype=jnp.float32)]
    return kernel_call(body, "hidden_gradient", meta, args, [whole(a) for a in args], out, [whole(o) for o in out])


def attention_backward(meta, qkv, probs, attended, grads, turned_normed, w_out, chips):
    rows, width = grads[0].shape
    group = 3 * BLOCK
    ranges = crop_ranges(rows)
    scale = 1.0 / math.sqrt(DH)

    def body(meta_ref, qkv_ref, prob_ref, mixed_ref, e1_ref, e1_other_ref, n_ref, n_other_ref, own_ref, *refs):
        chip_refs, out_ref, sides, refs = refs[:CHIPS], refs[CHIPS], refs[CHIPS + 1 : CHIPS + 5], refs[CHIPS + 5 :]
        weight_ref, grad_ref, mixed_all, turned_e, turned_other = refs
        step = pl.program_id(0)
        parity = step & 1

        @pl.when(step == 0)
        def _():
            turn_into(meta_ref, e1_ref, turned_e)
            turn_into(meta_ref, e1_other_ref, turned_other)

        def far_weights():
            for side, ref in enumerate(chip_refs):
                start = pl.multiple_of(meta_ref[side] * QUARTER, QUARTER)
                for b in range(2):
                    weight_ref[:, pl.ds(start + b * BLOCK, BLOCK)] = ref[0, b * BLOCK : (b + 1) * BLOCK, :]

        @pl.when(step == 0)
        def _():
            weight_ref[...] = own_ref[...]

        pl.when(step > 0)(far_weights)
        mixed_all[:, :, pl.ds(pl.multiple_of(parity * BLOCK, BLOCK), BLOCK)] = mixed_ref[...]
        for part, ref in enumerate((e1_ref, e1_other_ref)):
            grad_ref[part] = dot_nt(ref[...], weight_ref[...]).astype(jnp.bfloat16)
        for part in range(2):
            for index, (low, high, skip) in enumerate(ranges):
                size = high - low
                query = qkv_ref[part, low:high, 0:BLOCK]
                key = qkv_ref[part, low:high, BLOCK : 2 * BLOCK]
                value = qkv_ref[part, low:high, 2 * BLOCK : 3 * BLOCK]
                grad = grad_ref[part, low:high, :]
                lane_of = lax.broadcasted_iota(jnp.int32, (size, BLOCK), 1)
                row = lax.broadcasted_iota(jnp.int32, (size, BLOCK), 0)
                parts = []
                for head in range(2):
                    own = (lane_of < DH) if head == 0 else (lane_of >= DH)
                    low_probs = prob_ref[0, part, index, head, 0:size, 0:size]
                    grad_value = dot_tn(low_probs, grad)
                    grad_probs = dot_nt(jnp.where(own, grad, jnp.zeros_like(grad)), value)
                    wide = low_probs.astype(jnp.float32)
                    weighted = wide * grad_probs
                    inner = jnp.sum(weighted, axis=1, keepdims=True)
                    grad_scores = (weighted - wide * inner).astype(jnp.bfloat16)
                    parts.append(
                        (dot_nn(grad_scores, key) * scale, dot_tn(grad_scores, query) * scale, grad_value)
                    )
                for which in range(3):
                    at = pl.ds(pl.multiple_of(parity * group + which * BLOCK, BLOCK), BLOCK)
                    joined = jnp.where(lane_of < DH, parts[0][which], parts[1][which]).astype(jnp.bfloat16)
                    if skip:
                        joined = jnp.where(row >= skip, joined, out_ref[part, low:high, at])
                    out_ref[part, low:high, at] = joined
        for lane in range(2):
            @pl.when(step == 2 * lane + 1)
            def _():
                kept, sent = sides[2 * lane : 2 * lane + 2]
                both = dot_nn(n_ref[...], out_ref[0]) + dot_nn(n_other_ref[...], out_ref[1])
                put_sides(lane, both, kept, sent, slice(0, 2 * group))
                both = dot_nn(turned_e[...], mixed_all[0]) + dot_nn(turned_other[...], mixed_all[1])
                put_sides(lane, both, kept, sent, slice(2 * group, 2 * group + 2 * BLOCK))

    views = tuple(chip.reshape(DEPTH - 1, 4 * QUARTER, BLOCK) for chip in chips)
    args = (qkv, probs, attended) + tuple(grads) + tuple(turned_normed) + (w_out,) + views
    return kernel_call(
        body,
        "attention_backward",
        meta,
        args,
        [
            pl.BlockSpec((2, rows, group), lambda g, m: (0, 0, g)),
            pl.BlockSpec((1,) + probs.shape[1:], lambda g, m: (g, 0, 0, 0, 0, 0)),
            pl.BlockSpec((2, rows, BLOCK), lambda g, m: (0, 0, g)),
            whole(grads[0]),
            whole(grads[1]),
            whole(turned_normed[0]),
            whole(turned_normed[1]),
            pl.BlockSpec((BLOCK, width), lambda g, m: (m[OWN_CORE], 0)),
        ]
        + [pl.BlockSpec((1, QUARTER, BLOCK), lambda g, m: (jnp.maximum(g - 1, 0), 3, 0))] * CHIPS,
        [shape_of(2, rows, DEPTH * group)] + [shape_of(width // 2, 8 * BLOCK)] * 4,
        [pl.BlockSpec((2, rows, 2 * group), lambda g, m: (0, 0, g >> 1))]
        + [pl.BlockSpec((width // 2, 8 * BLOCK), lambda g, m: (0, 0))] * 4,
        grid=(DEPTH,),
        scratch=[
            pltpu.VMEM((BLOCK, width), jnp.bfloat16),
            pltpu.VMEM((2, rows, BLOCK), jnp.bfloat16),
            pltpu.VMEM((2, rows, 2 * BLOCK), jnp.bfloat16),
            pltpu.VMEM((width, rows), jnp.bfloat16),
            pltpu.VMEM((width, rows), jnp.bfloat16),
        ],
        vmem=BACK_BYTES,
    )


def token_shares(meta, grads, w_query, w_key, w_value, chips):
    rows = grads.shape[1]
    width = w_query.shape[0]
    group = 3 * BLOCK

    def body(meta_ref, grad_ref, q_ref, k_ref, v_ref, *refs):
        chip_refs, (near_ref, left_ref, right_ref, bias_ref, weight_ref, total_ref) = refs[:CHIPS], refs[CHIPS:]
        step = pl.program_id(0)

        @pl.when(step == 0)
        def _():
            for which, ref in enumerate((q_ref, k_ref, v_ref)):
                weight_ref[:, which * BLOCK : (which + 1) * BLOCK] = ref[...]

        @pl.when(step > 0)
        def _():
            fill_heads(meta_ref, chip_refs, weight_ref)

        sums = jnp.sum(grad_ref[0].astype(jnp.float32), axis=0, keepdims=True)
        bias_ref[0] = sums + jnp.sum(grad_ref[1].astype(jnp.float32), axis=0, keepdims=True)
        for part in range(2):
            share = dot_nt(grad_ref[part], weight_ref[...])

            @pl.when(step == 0)
            def _():
                total_ref[part] = share

            @pl.when(step > 0)
            def _():
                total_ref[part] += share

        @pl.when(step == DEPTH - 1)
        def _():
            near_ref[...] = total_ref[0]
            left_ref[...] = total_ref[1, :, : width // 2].astype(jnp.bfloat16)
            right_ref[...] = total_ref[1, :, width // 2 :].astype(jnp.bfloat16)

    own_specs, far_specs = head_specs(width, chips)
    out = [shape_of(rows, width, dtype=jnp.float32)] + [shape_of(rows, width // 2)] * 2
    return kernel_call(
        body,
        "token_shares",
        meta,
        (grads, w_query, w_key, w_value) + tuple(chips),
        [pl.BlockSpec((2, rows, group), lambda g, m: (0, 0, g))]
        + own_specs
        + far_specs,
        out + [shape_of(DEPTH, 1, group, dtype=jnp.float32)],
        [whole(o) for o in out] + [pl.BlockSpec((1, 1, group), lambda g, m: (g, 0, 0))],
        grid=(DEPTH,),
        scratch=[pltpu.VMEM((width, group), jnp.bfloat16), pltpu.VMEM((2, rows, width), jnp.float32)],
    )


def token_gradient(meta, near, left, right, tokens, dh, vectors):
    rows, width = tokens.shape

    def body(meta_ref, near_ref, left_ref, right_ref, tokens_ref, dh_ref, vec_ref, out_ref, sum_ref):
        got = jnp.concatenate([left_ref[...], right_ref[...]], axis=1).astype(jnp.float32)
        grad = near_ref[...] + got
        unit, inverse = normalized(tokens_ref[...].astype(jnp.float32))
        sum_ref[0:1, :] = jnp.sum(grad * unit, axis=0, keepdims=True)
        sum_ref[1:2, :] = jnp.sum(grad, axis=0, keepdims=True)
        out_ref[...] = dh_ref[...] + norm_gradient(unit, inverse, vec_ref[GAIN_ONE : GAIN_ONE + 1], grad)

    args = (near, left, right, tokens, dh, vectors)
    out = [shape_of(rows, width, dtype=jnp.float32), shape_of(2, width, dtype=jnp.float32)]
    return kernel_call(body, "token_gradient", meta, args, [whole(a) for a in args], out, [whole(o) for o in out])


def layer_result(meta, downs, hidden, cotangent, vectors):
    rows, width = hidden.shape

    def body(meta_ref, *refs):
        down_refs, (hidden_ref, cot_ref, vec_ref, out_ref, sum_ref) = refs[: len(downs)], refs[len(downs) :]
        branch = sum(ref[...].astype(jnp.float32) for ref in down_refs) + vec_ref[BIAS_DOWN : BIAS_DOWN + 1]
        valid = valid_column(meta_ref, rows)
        out_ref[...] = valid * (hidden_ref[...] + vec_ref[SCALE_MLP : SCALE_MLP + 1] * branch)
        sum_ref[...] = jnp.sum(valid * cot_ref[...].astype(jnp.float32) * branch, axis=0, keepdims=True)

    args = tuple(downs) + (hidden, cotangent, vectors)
    out = [shape_of(rows, width, dtype=jnp.float32), shape_of(1, width, dtype=jnp.float32)]
    return kernel_call(body, "layer_result", meta, args, [whole(a) for a in args], out, [whole(o) for o in out])


def pack_small(meta, wide, sums_qkv, sums_up):
    lines = wide[0].shape[1] // BLOCK
    n_u = sums_up[0].shape[1] // 2 // BLOCK
    share = 2 + n_u
    rows = sum(value.shape[0] for value in wide) * lines
    total = rows + 2 * DEPTH * share

    def body(meta_ref, *refs):
        wide_refs, qkv_ref, up_refs, out_ref = refs[: len(wide)], refs[len(wide)], refs[len(wide) + 1 : -1], refs[-1]
        at = 0
        for ref in wide_refs:
            for index in range(ref.shape[0]):
                for k in range(lines):
                    out_ref[at : at + 1, :] = ref[index : index + 1, k * BLOCK : (k + 1) * BLOCK]
                    at += 1
        out_ref[rows:, :] = jnp.zeros((total - rows, BLOCK), jnp.float32)
        core, level = meta_ref[OWN_CORE], meta_ref[OWN_LEVEL]
        for index in range(DEPTH):
            start = rows + core * (DEPTH * share) + (level ^ index) * share
            out_ref[pl.ds(start, 1), :] = qkv_ref[index, :, 0:BLOCK]
            out_ref[pl.ds(start + 1, 1), :] = qkv_ref[index, :, 2 * BLOCK : 3 * BLOCK]
            if index in (0, 2):
                for k in range(n_u):
                    column = (index // 2 * n_u + k) * BLOCK
                    out_ref[pl.ds(start + 2 + k, 1), :] = sum(ref[:, column : column + BLOCK] for ref in up_refs)

    args = tuple(wide) + (sums_qkv,) + tuple(sums_up)
    out = shape_of(total, BLOCK, dtype=jnp.float32)
    return kernel_call(body, "pack_small", meta, args, [whole(a) for a in args], out, whole(out))


def finish(meta, mine, other, kinds, name):
    width = CHIPS * QUARTER

    def body(meta_ref, mine_ref, other_ref, *outs):
        core = meta_ref[OWN_CORE]
        for ref, half in ((mine_ref, core), (other_ref, 1 - core)):
            at = 0
            for out_ref, (units, turned) in zip(outs, kinds):
                values = ref[0, :, at : at + units].astype(jnp.float32)
                place = pl.ds(pl.multiple_of(half * units, units), units)
                if turned:
                    out_ref[place, :] = values.T
                else:
                    out_ref[:, place] = values
                at += units

    side = pl.BlockSpec((1,) + mine.shape[1:], lambda j, m: (j, 0, 0))
    out, specs = [], []
    for units, turned in kinds:
        shape = (2 * units, width) if turned else (width, 2 * units)
        block = (2 * units, QUARTER) if turned else (QUARTER, 2 * units)
        out.append(shape_of(*shape, dtype=jnp.float32))
        specs.append(pl.BlockSpec(block, (lambda j, m: (0, m[j])) if turned else (lambda j, m: (m[j], 0))))
    return kernel_call(body, name, meta, (mine, other), [side, side], out, specs, grid=(CHIPS,))


def local_paired(
    tokens,
    slide_tiles,
    norm1_gain,
    norm1_bias,
    w_query,
    b_query,
    w_key,
    w_value,
    b_value,
    w_out,
    b_out,
    scale_attn,
    norm2_gain,
    norm2_bias,
    w_up,
    b_up,
    w_down,
    b_down,
    scale_mlp,
    cotangent,
):
    row_count, width = tokens.shape
    half_u = w_up.shape[1] // 2
    here = lax.axis_index("dp")
    level = lax.axis_index("mp")
    crops_here = row_count // L
    per_slide = CROPS_DEV // SLIDES_DEV
    crop = level * crops_here + jnp.arange(crops_here, dtype=jnp.int32)
    owner = (crop // per_slide)[:, None] == jnp.arange(SLIDES_DEV, dtype=jnp.int32)[None, :]
    limit = jnp.sum(jnp.where(owner, slide_tiles[None, :], 0), axis=1)
    valid = (crop % per_slide < limit).astype(jnp.int32)
    core = here & 1
    sides = jnp.stack([(here >> 1) ^ side for side in range(CHIPS)] + [core, level]).astype(jnp.int32)
    meta = jnp.concatenate([sides, valid])
    bias_q, bias_v, bias_u = [values.reshape(-1, BLOCK) for values in (b_query, b_value, b_up)]
    vectors = jnp.stack([norm1_gain, norm1_bias, norm2_gain, norm2_bias, scale_attn, scale_mlp, b_out, b_down])
    first, second = (X_SIDE, Y_SIDE), (Y_SIDE, X_SIDE)

    order = Order(meta)

    tokens_other = swap_plane(tokens, CORE_SIDE)
    slice_attn, slice_rest = order(slice_weights, w_query, w_key, w_value, w_out, w_up, w_down, bias_q, bias_v, bias_u)
    level_attn = [swap_depth(slice_attn, mask) for mask in (1, 2, 3)]
    one, one_other, grad, grad_b_down, one_turned, one_other_turned, grad_turned = order(
        prepare, tokens, tokens_other, cotangent, vectors
    )
    level_attn = order.land(*level_attn)
    far_attn = order.plain(lambda *parts: jnp.concatenate([part[: 4 * QUARTER] for part in parts], axis=0), *level_attn)
    attn_x, attn_y = swap_plane(far_attn, X_SIDE), swap_plane(far_attn, Y_SIDE)
    level_rest = swap_depth(order.hold(slice_rest), 2)
    n_u = half_u // BLOCK

    def unit_bias(rows, own):
        rows = rows[4 * QUARTER :].astype(jnp.float32)
        pair = (rows[2 : 2 + n_u] + rows[4 + n_u : 4 + 2 * n_u]).reshape(-1)
        return jnp.concatenate([lax.dynamic_slice_in_dim(own, core * half_u, half_u), pair])[None, :]

    bias_up = order.plain(unit_bias, level_attn[1], b_up)
    attn_x, attn_y = order.land(attn_x, attn_y)
    half = far_attn.shape[0] // 2
    low, high = order.hold((attn_y[:half], attn_x[half:]))
    low, high = swap_plane(low, X_SIDE), swap_plane(high, Y_SIDE)
    level_rest, low, high = order.land(level_rest, low, high)
    corner = order.plain(lambda *parts: jnp.concatenate(parts), low, high)
    chips_attn = [far_attn, attn_x, attn_y, corner]
    level_rest, grad, grad_far = order.hold((level_rest, grad, grad))
    plane_rest = plane_swaps(level_rest)
    grad_other = swap_plane(grad, CORE_SIDE)
    grad_far = swap_depth(grad_far, 1)
    qkv, attended, probs = order(
        attention_forward, one, one_other, w_query, w_key, w_value, bias_q, bias_v, level_attn, chips_attn, n_u
    )
    grad_other, grad_far = order.land(grad_other, grad_far)
    out_near, *out_across = order(attention_out, attended, w_out, chips_attn)
    out_got = [swap_plane(part, CORE_SIDE) for part in out_across]
    hidden, branch, normed = order(attention_norm, out_near, *out_got, tokens, vectors)
    normed_far = swap_depth(normed, 1)
    plane_rest = order.land(*plane_rest)
    chips_rest = [level_rest] + plane_rest
    normed_other, grad_far_other = order.hold((normed, grad_far))
    normed_other = swap_plane(normed_other, CORE_SIDE)
    grad_far_other = swap_plane(grad_far_other, CORE_SIDE)

    *near, full_up, full_down = order(
        feed_near, (normed, normed_other), (grad, grad_other), w_up, w_down, bias_up, chips_rest
    )
    (normed_far,) = order.land(normed_far)
    normed_far, back_near = order.hold((normed_far, near[2][1]))
    normed_far_other = swap_plane(normed_far, CORE_SIDE)
    back_near = swap_plane(back_near, CORE_SIDE)
    far = order(feed_far, (normed_far,), grad_far, bias_up, full_up, full_down)
    far_other = order(feed_far, (normed_far_other,), grad_far_other, bias_up, full_up, full_down)
    acts, gups, backs = [list(a) + [b, c] for a, b, c in zip(near[:3], far[:3], far_other[:3])]
    back_got, back_near = order.land(swap_plane(backs[3], CORE_SIDE), back_near)
    back_far = swap_depth(order.plain(add_low, backs[2], back_got), 1)
    grads_turned = [grad_turned] + list(order(turn, grad_other, grad_far, grad_far_other))
    rest_sides = order(
        feed_gradients, (normed, normed_other, normed_far, normed_far_other), grads_turned, gups, acts
    )
    downs = order(feed_down, acts, full_down)
    down_near, down_far = swap_plane(downs[1], CORE_SIDE), swap_plane(downs[3], CORE_SIDE)
    (back_far,) = order.land(back_far)
    rest_sent = order.hold([sent for _, sent in rest_sides])
    rest_got = [swap_plane(sent, side) for sent, side in zip(rest_sent, first)]
    dh, e1, sums_two = order(
        hidden_gradient, (backs[0], back_near, back_far), hidden, branch, cotangent, vectors
    )
    e1_other = swap_plane(e1, CORE_SIDE)
    down_near, down_far = order.land(down_near, down_far)
    down_far = order(lambda meta, *parts: add_parts(meta, [(part, 0) for part in parts])[0], downs[2], down_far)
    (e1_other,) = order.land(e1_other)
    down_far = swap_depth(order.hold(down_far), 1)
    grad_heads, low_kept, low_sent, high_kept, high_sent = order(
        attention_backward, qkv, probs, attended, (e1, e1_other), (one_turned, one_other_turned), w_out, chips_attn
    )
    *rest_got, down_far = order.land(*rest_got, down_far)

    def onward(kept, got):
        return order(
            lambda meta, *args: add_parts(meta, *[((args[2 * k], QUARTER), (args[2 * k + 1], QUARTER)) for k in range(2)]),
            *[array for pair in zip(kept, got) for array in pair],
        )

    def arrived(kept, got, last):
        return order(
            lambda meta, *args: add_parts(meta, *[[(part, 0) for part in args[3 * k : 3 * k + 3]] for k in range(2)]),
            *[array for triple in zip(kept, got, last) for array in triple],
        )

    rest_kept = [kept for kept, _ in rest_sides]
    rest_sent = order.hold(onward(rest_kept, rest_got))
    rest_last = [swap_plane(sent, side) for sent, side in zip(rest_sent, second)]
    one_near, *one_across, sums_qkv = order(
        token_shares, grad_heads, w_query, w_key, w_value, chips_attn
    )
    one_got = [swap_plane(part, CORE_SIDE) for part in one_across]
    *rest_last, one_got[0], one_got[1] = order.land(*rest_last, *one_got)
    rest_own, rest_pair = arrived(rest_kept, rest_got, rest_last)
    low_sent, high_sent, rest_pair = order.hold((low_sent, high_sent, rest_pair))
    attn_got = [swap_plane(sent, side) for sent, side in zip((low_sent, high_sent), first)]
    rest_pair = swap_depth(rest_pair, 2)
    layer_out, grad_scale_mlp = order(
        layer_result, (downs[0], down_near, down_far), hidden, cotangent, vectors
    )
    grad_tokens, sums_one = order(token_gradient, one_near, *one_got, tokens, dh, vectors)

    totals = order(
        pack_small, (sums_one, sums_two, grad_scale_mlp, grad_b_down), sums_qkv, (near[3], far[3], far_other[3])
    )
    totals_got = swap_plane(totals, X_SIDE)
    *attn_got, rest_pair, totals_got = order.land(*attn_got, rest_pair, totals_got)
    attn_kept = (low_kept, high_kept)
    attn_sent = onward(attn_kept, attn_got)
    attn_last = [swap_plane(sent, side) for sent, side in zip(attn_sent, second)]

    totals = order.plain(jnp.add, totals, totals_got)
    totals_got = swap_plane(totals, Y_SIDE)
    grad_rest = order(lambda meta, *parts: add_parts(meta, [(part, 0) for part in parts])[0], rest_own, rest_pair)
    *attn_last, totals_got = order.land(*attn_last, totals_got)
    own_piece, pair_piece, level_sent = order(level_pieces, attn_kept, attn_got, attn_last)
    level_got = swap_depth(level_sent, 1)
    totals = order.plain(jnp.add, totals, totals_got)
    totals_got, grad_rest = order.hold((totals, grad_rest))
    rest_x, rest_y = swap_plane(grad_rest, X_SIDE), swap_plane(grad_rest, Y_SIDE)
    totals_got = swap_depth(totals_got, 1)
    level_got, rest_x, rest_y, totals_got = order.land(level_got, rest_x, rest_y, totals_got)
    level_kept, level_sent = order.plain(
        lambda own, pair, got: (add_low(own, got[0]), add_low(pair, got[1])), own_piece, pair_piece, level_got
    )
    totals = order.plain(jnp.add, totals, totals_got)
    totals_got, grad_rest, level_sent = order.hold((totals, grad_rest, level_sent))
    level_got = swap_depth(level_sent, 2)
    rest_corner = swap_plane(grad_rest, X_SIDE | Y_SIDE)
    totals_got = swap_depth(totals_got, 2)
    level_got, rest_corner, totals_got = order.land(level_got, rest_corner, totals_got)
    grad_attn = order.plain(add_low, level_kept, level_got)
    totals = order.plain(jnp.add, totals, totals_got)
    plane_attn = plane_swaps(order.hold(grad_attn))
    totals_got = swap_plane(order.hold(totals), CORE_SIDE)
    rest_mine = order.plain(lambda *parts: jnp.stack(parts), grad_rest, rest_x, rest_y, rest_corner)
    rest_other = swap_plane(order.hold(rest_mine), CORE_SIDE)
    (rest_other,) = order.land(rest_other)
    full_grad_up, full_grad_down = order(
        finish, rest_mine, rest_other, ((half_u, False), (half_u, True)), "finish_rest"
    )
    *plane_attn, totals_got = order.land(*plane_attn, totals_got)
    attn_mine = order.plain(lambda *parts: jnp.stack(parts), grad_attn, *plane_attn)
    attn_other = swap_plane(order.hold(attn_mine), CORE_SIDE)
    totals = order.plain(jnp.add, totals, totals_got)
    (attn_other,) = order.land(attn_other)
    full_grad_q, full_grad_k, full_grad_v, full_grad_o = order(
        finish, attn_mine, attn_other, ((BLOCK, False),) * 3 + ((BLOCK, True),), "finish_attn"
    )
    lines = width // BLOCK
    small_total = totals[: 8 * lines].reshape(8, width)
    shared_total = totals[8 * lines :].reshape(2, DEPTH, -1)
    shared_total = lax.dynamic_index_in_dim(shared_total, level, 1, keepdims=False)
    return (
        layer_out,
        grad_tokens,
        small_total[0],
        small_total[1],
        full_grad_q,
        shared_total[:, :BLOCK].reshape(-1),
        full_grad_k,
        full_grad_v,
        shared_total[:, BLOCK : 2 * BLOCK].reshape(-1),
        full_grad_o,
        small_total[5],
        small_total[4],
        small_total[2],
        small_total[3],
        full_grad_up,
        shared_total[:, 2 * BLOCK :].reshape(-1),
        full_grad_down,
        small_total[7],
        small_total[6],
    )


def local_general(
    tokens,
    slide_tiles,
    norm1_gain,
    norm1_bias,
    w_query,
    b_query,
    w_key,
    w_value,
    b_value,
    w_out,
    b_out,
    scale_attn,
    norm2_gain,
    norm2_bias,
    w_up,
    b_up,
    w_down,
    b_down,
    scale_mlp,
    cotangent,
):
    row_count = tokens.shape[0]
    per_slide = CROPS_DEV // SLIDES_DEV
    crop_index = (lax.axis_index("mp") * row_count + jnp.arange(row_count, dtype=jnp.int32)) // L
    slide_index = crop_index // per_slide
    owner = slide_index[:, None] == jnp.arange(SLIDES_DEV, dtype=jnp.int32)[None, :]
    limit_rows = jnp.sum(jnp.where(owner, slide_tiles[None, :], 0), axis=1)
    valid_rows = (crop_index % per_slide < limit_rows).astype(jnp.float32)[:, None]
    inputs = tokens.astype(jnp.float32)
    normed_one = layer_norm(inputs, norm1_gain, norm1_bias).astype(jnp.bfloat16)
    rows_one = lax.all_gather(normed_one, "mp", axis=0, tiled=True)
    queries = (jnp.dot(rows_one, w_query, preferred_element_type=jnp.float32) + b_query).astype(
        jnp.bfloat16
    )
    keys_all = jnp.dot(rows_one, w_key, preferred_element_type=jnp.float32).astype(jnp.bfloat16)
    values_all = (jnp.dot(rows_one, w_value, preferred_element_type=jnp.float32) + b_value).astype(
        jnp.bfloat16
    )
    heads_here = w_query.shape[1] // DH
    query_heads = to_heads(queries, heads_here)
    key_heads = to_heads(keys_all, heads_here)
    value_heads = to_heads(values_all, heads_here)
    scores = attn_scores(query_heads, key_heads)
    top_score = jnp.max(scores, axis=-1, keepdims=True)
    log_total = top_score + jnp.log(jnp.sum(jnp.exp(scores - top_score), axis=-1, keepdims=True))
    weights_low = jnp.exp(scores - log_total).astype(jnp.bfloat16)
    mixed_heads = jnp.einsum(
        "chqk,ckhd->cqhd", weights_low, value_heads, preferred_element_type=jnp.float32
    )
    attended = mixed_heads.reshape(queries.shape).astype(jnp.bfloat16)
    attn_sum = lax.psum_scatter(
        jnp.dot(attended, w_out, preferred_element_type=jnp.float32).astype(jnp.bfloat16),
        "mp",
        scatter_dimension=0,
        tiled=True,
    ).astype(jnp.float32)
    branch_one = attn_sum + b_out
    hidden_state = inputs + scale_attn * branch_one
    normed_two = layer_norm(hidden_state, norm2_gain, norm2_bias).astype(jnp.bfloat16)
    rows_two = lax.all_gather(normed_two, "mp", axis=0, tiled=True)
    up_pre = jnp.dot(rows_two, w_up, preferred_element_type=jnp.float32) + b_up
    activated = gelu_exact(up_pre).astype(jnp.bfloat16)
    down_sum = lax.psum_scatter(
        jnp.dot(activated, w_down, preferred_element_type=jnp.float32).astype(jnp.bfloat16),
        "mp",
        scatter_dimension=0,
        tiled=True,
    ).astype(jnp.float32)
    branch_two = down_sum + b_down
    layer_out = valid_rows * (hidden_state + scale_mlp * branch_two)
    grad_out = valid_rows * cotangent.astype(jnp.float32)
    grad_scale_mlp = jnp.sum(grad_out * branch_two, axis=0)
    grad_branch_two = scale_mlp * grad_out
    grad_b_down = jnp.sum(grad_branch_two, axis=0)
    grad_down_low = grad_branch_two.astype(jnp.bfloat16)
    gelu_value, gelu_back = jax.vjp(gelu_exact, up_pre)
    grad_down_rows = lax.all_gather(grad_down_low, "mp", axis=0, tiled=True)
    grad_act = contract_cols(grad_down_rows, w_down)
    grad_up = gelu_back(grad_act)[0].astype(jnp.bfloat16)
    grad_w_up = contract_rows(rows_two, grad_up)
    grad_w_down = contract_rows(activated, grad_down_rows)
    grad_b_up = jnp.sum(grad_up.astype(jnp.float32), axis=0)
    grad_rows_two = lax.psum_scatter(
        contract_cols(grad_up, w_up).astype(jnp.bfloat16), "mp", scatter_dimension=0, tiled=True
    ).astype(jnp.float32)
    norm2_value, norm2_back = jax.vjp(layer_norm, hidden_state, norm2_gain, norm2_bias)
    grad_hidden_norm, grad_norm2_gain, grad_norm2_bias = norm2_back(grad_rows_two)
    grad_hidden = grad_out + grad_hidden_norm
    grad_scale_attn = jnp.sum(grad_hidden * branch_one, axis=0)
    grad_branch_one = scale_attn * grad_hidden
    grad_b_out = jnp.sum(grad_branch_one, axis=0)
    grad_attn_low = grad_branch_one.astype(jnp.bfloat16)
    grad_attn_rows = lax.all_gather(grad_attn_low, "mp", axis=0, tiled=True)
    grad_w_out = contract_rows(attended, grad_attn_rows)
    grad_mixed = contract_cols(grad_attn_rows, w_out).astype(jnp.bfloat16)
    grad_mixed_heads = to_heads(grad_mixed, heads_here)
    scores_again = attn_scores(query_heads, key_heads)
    probs = jnp.exp(scores_again - log_total)
    probs_low = probs.astype(jnp.bfloat16)
    grad_value_heads = jnp.einsum(
        "chqk,cqhd->ckhd", probs_low, grad_mixed_heads, preferred_element_type=jnp.float32
    )
    grad_values = grad_value_heads.reshape(queries.shape).astype(jnp.bfloat16)
    grad_probs = jnp.einsum(
        "cqhd,ckhd->chqk", grad_mixed_heads, value_heads, preferred_element_type=jnp.float32
    )
    row_inner = jnp.sum(probs * grad_probs, axis=-1, keepdims=True)
    grad_scores = (probs * (grad_probs - row_inner)).astype(jnp.bfloat16)
    inverse_root = 1.0 / math.sqrt(DH)
    grad_query_heads = jnp.einsum(
        "chqk,ckhd->cqhd", grad_scores, key_heads, preferred_element_type=jnp.float32
    )
    grad_queries = (inverse_root * grad_query_heads).reshape(queries.shape).astype(jnp.bfloat16)
    grad_key_heads = jnp.einsum(
        "chqk,cqhd->ckhd", grad_scores, query_heads, preferred_element_type=jnp.float32
    )
    grad_keys = (inverse_root * grad_key_heads).reshape(queries.shape).astype(jnp.bfloat16)
    grad_w_query = contract_rows(rows_one, grad_queries)
    grad_b_query = jnp.sum(grad_queries.astype(jnp.float32), axis=0)
    grad_w_key = contract_rows(rows_one, grad_keys)
    grad_w_value = contract_rows(rows_one, grad_values)
    grad_b_value = jnp.sum(grad_values.astype(jnp.float32), axis=0)
    grad_rows_one = lax.psum_scatter(
        (
            contract_cols(grad_queries, w_query)
            + contract_cols(grad_keys, w_key)
            + contract_cols(grad_values, w_value)
        ).astype(jnp.bfloat16),
        "mp",
        scatter_dimension=0,
        tiled=True,
    ).astype(jnp.float32)
    norm1_value, norm1_back = jax.vjp(layer_norm, inputs, norm1_gain, norm1_bias)
    grad_in_norm, grad_norm1_gain, grad_norm1_bias = norm1_back(grad_rows_one)
    grad_tokens = grad_hidden + grad_in_norm
    small_stack = jnp.stack(
        [
            grad_norm1_gain,
            grad_norm1_bias,
            grad_norm2_gain,
            grad_norm2_bias,
            grad_scale_attn,
            grad_scale_mlp,
            grad_b_out,
            grad_b_down,
        ],
        axis=1,
    )
    small_total = lax.psum(small_stack.astype(jnp.bfloat16), "mp")
    (
        share_wq,
        share_bq,
        share_wk,
        share_wv,
        share_bv,
        share_wo,
        share_up,
        share_bup,
        share_down,
        share_small,
    ) = (
        lax.psum_scatter(
            grad_w_query.astype(jnp.bfloat16), "dp", scatter_dimension=0, tiled=True
        ).astype(jnp.float32),
        lax.psum_scatter(
            grad_b_query.astype(jnp.bfloat16), "dp", scatter_dimension=0, tiled=True
        ).astype(jnp.float32),
        lax.psum_scatter(
            grad_w_key.astype(jnp.bfloat16), "dp", scatter_dimension=0, tiled=True
        ).astype(jnp.float32),
        lax.psum_scatter(
            grad_w_value.astype(jnp.bfloat16), "dp", scatter_dimension=0, tiled=True
        ).astype(jnp.float32),
        lax.psum_scatter(
            grad_b_value.astype(jnp.bfloat16), "dp", scatter_dimension=0, tiled=True
        ).astype(jnp.float32),
        lax.psum_scatter(
            grad_w_out.astype(jnp.bfloat16), "dp", scatter_dimension=0, tiled=True
        ).astype(jnp.float32),
        lax.psum_scatter(
            grad_w_up.astype(jnp.bfloat16), "dp", scatter_dimension=0, tiled=True
        ).astype(jnp.float32),
        lax.psum_scatter(
            grad_b_up.astype(jnp.bfloat16), "dp", scatter_dimension=0, tiled=True
        ).astype(jnp.float32),
        lax.psum_scatter(
            grad_w_down.astype(jnp.bfloat16), "dp", scatter_dimension=0, tiled=True
        ).astype(jnp.float32),
        lax.psum_scatter(small_total, "dp", scatter_dimension=0, tiled=True).astype(jnp.float32),
    )
    (
        full_wq,
        full_bq,
        full_wk,
        full_wv,
        full_bv,
        full_wo,
        full_up,
        full_bup,
        full_down,
        full_small,
    ) = (
        lax.all_gather(share_wq.astype(jnp.bfloat16), "dp", axis=0, tiled=True).astype(
            share_wq.dtype
        ),
        lax.all_gather(share_bq.astype(jnp.bfloat16), "dp", axis=0, tiled=True).astype(
            share_bq.dtype
        ),
        lax.all_gather(share_wk.astype(jnp.bfloat16), "dp", axis=0, tiled=True).astype(
            share_wk.dtype
        ),
        lax.all_gather(share_wv.astype(jnp.bfloat16), "dp", axis=0, tiled=True).astype(
            share_wv.dtype
        ),
        lax.all_gather(share_bv.astype(jnp.bfloat16), "dp", axis=0, tiled=True).astype(
            share_bv.dtype
        ),
        lax.all_gather(share_wo.astype(jnp.bfloat16), "dp", axis=0, tiled=True).astype(
            share_wo.dtype
        ),
        lax.all_gather(share_up.astype(jnp.bfloat16), "dp", axis=0, tiled=True).astype(
            share_up.dtype
        ),
        lax.all_gather(share_bup.astype(jnp.bfloat16), "dp", axis=0, tiled=True).astype(
            share_bup.dtype
        ),
        lax.all_gather(share_down.astype(jnp.bfloat16), "dp", axis=0, tiled=True).astype(
            share_down.dtype
        ),
        lax.all_gather(share_small.astype(jnp.bfloat16), "dp", axis=0, tiled=True).astype(
            share_small.dtype
        ),
    )
    return (
        layer_out,
        grad_tokens,
        full_small[:, 0],
        full_small[:, 1],
        full_wq,
        full_bq,
        full_wk,
        full_wv,
        full_bv,
        full_wo,
        full_small[:, 6],
        full_small[:, 4],
        full_small[:, 2],
        full_small[:, 3],
        full_up,
        full_bup,
        full_down,
        full_small[:, 7],
        full_small[:, 5],
    )


def solution(mesh):
    in_specs = (
        P(("dp", "mp"), None),
        P("dp"),
        P(),
        P(),
        P(None, "mp"),
        P("mp"),
        P(None, "mp"),
        P(None, "mp"),
        P("mp"),
        P("mp", None),
        P(),
        P(),
        P(),
        P(),
        P(None, "mp"),
        P("mp"),
        P("mp", None),
        P(),
        P(),
        P(("dp", "mp"), None),
    )
    out_specs = (
        P(("dp", "mp"), None),
        P(("dp", "mp"), None),
        P(),
        P(),
        P(None, "mp"),
        P("mp"),
        P(None, "mp"),
        P(None, "mp"),
        P("mp"),
        P("mp", None),
        P(),
        P(),
        P(),
        P(),
        P(None, "mp"),
        P("mp"),
        P("mp", None),
        P(),
        P(),
    )
    paired = mesh.shape["dp"] == 8 and mesh.shape["mp"] == 4
    local = local_paired if paired else local_general
    return jax.shard_map(local, mesh=mesh, in_specs=in_specs, out_specs=out_specs, check_vma=False)
```
